32 devices in a mesh: group: 2 (over x), wide: 4 (over y, core), narrow: 4 (over z).
Axes of the slice: x: 2, y: 2, z: 4, core: 2. Of those that a mesh axis runs over, the one named last changes fastest.
Arguments:
- right_side: float32 [128, 256, 256], P(('group', 'wide'), 'narrow'), parts along dimension 0, may hold values from -4 to 4
- conduct_half: bfloat16 [128, 256, 256], P(('group', 'wide'), 'narrow'), parts along dimension 0, may hold values from 0.59765625 to 1.59375
- reaction_half: bfloat16 [128, 256, 256], P(('group', 'wide'), 'narrow'), parts along dimension 0, may hold values from 1 to 4
Outputs:
- solution: float32 [128, 256, 256], P(('group', 'wide'), 'narrow'), parts along dimension 0
- residual: float32 [128, 256, 256], P(('group', 'wide'), 'narrow'), parts along dimension 0
The draws below stay inside these ranges and needn't reach their ends.
There are 2 independent parts, one for each index of `group`. The reference program is written for one: setup_inputs(seed, part) draws one part's arguments, and reference() takes and returns one part's arrays. A program takes and returns all parts, laid end to end along the dimension named above; each array names one. Nothing has to cross between parts.
All inputs are finite; a program needn't handle non-finite values.
Results may differ from the reference program's by a relative error of at most 0.02.
Values may be sent and summed in bfloat16 or wider, within the bound.
No kernel may reach another device: no remote copies, remote signals or barrier semaphores. Data moves between devices by JAX's collectives and lax.ppermute only.
A program may use at most 128 MiB of HBM per device.

```python
import math
import jax
import jax.numpy as jnp
import numpy as np
from jax import lax

CZ = 256
S = 4
OUTER = 2
NX = 64
NY = 256


def draw_right_side(key, part):
    key = jax.random.fold_in(key, 11)
    first = jnp.arange(NX, dtype=jnp.float32) / max(NX - 1, 1)
    second = jnp.arange(NY, dtype=jnp.float32) / max(NY - 1, 1)
    ramp = jnp.power(3.0, 0.5 * (first[:, None, None] + second[None, :, None]))
    rough = jnp.clip(0.5 * jax.random.normal(key, (NX, NY, CZ), jnp.float32), -1.25, 1.25)
    return ramp * rough


def level_of(key, shape, shards, smallest, high):
    level, own = 1.0, jax.random.fold_in(key, 6)
    for dim, blocks in shards:
        steps = jnp.exp(jax.random.uniform(jax.random.fold_in(own, dim), (blocks,), jnp.float32, smallest / len(shards), high / len(shards)))
        level = level * jnp.repeat(steps, shape[dim] // blocks).reshape([-1 if axis == dim else 1 for axis in range(len(shape))])
    return level


def setup_inputs(seed: int = 0, part: int = 0) -> dict:
    streams_of = jax.random.split(jax.random.key(seed), 4)
    part_splits = jax.random.split(jax.random.fold_in(streams_of[3], part), 4)
    return {
        "right_side": draw_right_side(jax.random.fold_in(jax.random.fold_in(streams_of[3], part), 71), part),
        "conduct_half": jnp.clip(jnp.exp(math.log(1.59375) - 0.98082925 * jax.random.uniform(part_splits[1], (NX, NY, CZ), jnp.float32) ** level_of(part_splits[1], (NX, NY, CZ), ((0, 4), (1, 4)), -0.2, 0.2)), 0.59765625, 1.59375).astype(jnp.bfloat16),
        "reaction_half": jnp.clip(jnp.exp(math.log(4.0) - 1.3862944 * jax.random.uniform(part_splits[2], (NX, NY, CZ), jnp.float32) ** level_of(part_splits[2], (NX, NY, CZ), ((0, 4), (1, 4)), -0.2, 0.2)), 1.0, 4.0).astype(jnp.bfloat16),
    }


center_shift = 16.0
basis_scale = 16.0


def shift_matrix():
    dimension = 2 * S + 1
    entries = np.zeros((dimension, dimension))
    for column in range(S):
        entries[column, column] = center_shift
        entries[column + 1, column] = basis_scale
    for column in range(S - 1):
        entries[S + 1 + column, S + 1 + column] = center_shift
        entries[S + 2 + column, S + 1 + column] = basis_scale
    return jnp.asarray(entries, dtype=jnp.float32)


def laplace_zero(scaled):
    padded = jnp.pad(scaled, 1)
    center = padded[1:-1, 1:-1, 1:-1]
    neighbours = padded[2:, 1:-1, 1:-1] + padded[:-2, 1:-1, 1:-1]
    neighbours = neighbours + padded[1:-1, 2:, 1:-1] + padded[1:-1, :-2, 1:-1]
    neighbours = neighbours + padded[1:-1, 1:-1, 2:] + padded[1:-1, 1:-1, :-2]
    return 6.0 * center - neighbours


def next_basis(vector, conduct, reaction):
    mapped = reaction * vector + conduct * laplace_zero(conduct * vector)
    return (mapped - center_shift * vector) / basis_scale


def coordinates(gram_matrix, shift_table):
    highest = lax.Precision.HIGHEST
    identity = jnp.eye(2 * S + 1, dtype=jnp.float32)
    search_coord = identity[0]
    resid_coord = identity[S + 1]
    sol_coord = jnp.zeros((2 * S + 1,), jnp.float32)
    norm_now = jnp.dot(resid_coord, jnp.dot(gram_matrix, resid_coord, precision=highest), precision=highest)
    for inner_step in range(S):
        mapped = jnp.dot(shift_table, search_coord, precision=highest)
        curvature = jnp.dot(search_coord, jnp.dot(gram_matrix, mapped, precision=highest), precision=highest)
        step_length = norm_now / curvature
        sol_coord = sol_coord + step_length * search_coord
        resid_coord = resid_coord - step_length * mapped
        norm_next = jnp.dot(resid_coord, jnp.dot(gram_matrix, resid_coord, precision=highest), precision=highest)
        search_coord = resid_coord + (norm_next / norm_now) * search_coord
        norm_now = norm_next
    return sol_coord, resid_coord, search_coord


def reference(right_side, conduct_half, reaction_half):
    highest = lax.Precision.HIGHEST
    conduct = conduct_half.astype(jnp.float32)
    reaction = reaction_half.astype(jnp.float32)
    shift_table = shift_matrix()
    solution = jnp.zeros_like(right_side)
    residual = right_side
    search = right_side
    for outer_step in range(OUTER):
        fields = [search]
        for inner_step in range(S):
            fields.append(next_basis(fields[-1], conduct, reaction))
        fields.append(residual)
        for inner_step in range(S - 1):
            fields.append(next_basis(fields[-1], conduct, reaction))
        stacked = jnp.stack(fields)
        fields = None
        flattened = stacked.reshape(2 * S + 1, -1)
        gram_matrix = jnp.dot(flattened, flattened.T, precision=highest)
        sol_coord, resid_coord, search_coord = coordinates(gram_matrix, shift_table)
        solution = solution + jnp.tensordot(sol_coord, stacked, axes=1, precision=highest)
        residual = jnp.tensordot(resid_coord, stacked, axes=1, precision=highest)
        search = jnp.tensordot(search_coord, stacked, axes=1, precision=highest)
    return solution, residual
```

```python
import jax
import jax.numpy as jnp
from jax import lax
from jax.experimental import pallas as pl
from jax.experimental.pallas import tpu as pltpu
from jax.sharding import PartitionSpec as P

S = 4
OUTER = 2
STEPS = S * OUTER

SCALE = 16.0
CENTER = 13.0
RATIO = CENTER / SCALE

LANES = 128
AXES = ("wide", "narrow")
VMEM = pl.BlockSpec(memory_space=pltpu.VMEM)
LIMIT = 56 * 1024 * 1024


def two_sum(a, b):
    total = a + b
    part = total - a
    return total, (a - (total - part)) + (b - part)


def fast_two_sum(a, b):
    total = a + b
    return total, b - (total - a)


def split(a):
    big = a * 4097.0
    high = big - (big - a)
    return high, a - high


def two_product(a, b):
    product = a * b
    a_high, a_low = split(a)
    b_high, b_low = split(b)
    error = ((a_high * b_high - product) + a_high * b_low + a_low * b_high) + a_low * b_low
    return product, error


def pair_add(a, b):
    total, error = two_sum(a[0], b[0])
    return fast_two_sum(total, error + (a[1] + b[1]))


def pair_scale(a, factor):
    product, error = two_product(a[0], factor)
    return fast_two_sum(product, error + a[1] * factor)


def send_kernel(b_ref, c_ref, r_ref, wm, wp, nm, np_, cmm, cmp, cpm, cpp):
    rows, columns = b_ref.shape[:2]
    h = STEPS

    def plane(i):
        field = b_ref[i]
        packed = r_ref[i].astype(jnp.float32) + c_ref[i].astype(jnp.float32) * (1.0 / 256.0)
        return (field, packed)

    def low(i, _):
        for k, value in enumerate(plane(i)):
            wm[k, i] = value
            nm[k, i] = value[:h]
            np_[k, i] = value[columns - h :]
            cmm[k, i] = value[:h]
            cmp[k, i] = value[columns - h :]
        return 0

    def middle(i, _):
        for k, value in enumerate(plane(i)):
            nm[k, i] = value[:h]
            np_[k, i] = value[columns - h :]
        return 0

    def high(i, _):
        at = i - (rows - h)
        for k, value in enumerate(plane(i)):
            wp[k, at] = value
            nm[k, i] = value[:h]
            np_[k, i] = value[columns - h :]
            cpm[k, at] = value[:h]
            cpp[k, at] = value[columns - h :]
        return 0

    lax.fori_loop(0, h, low, 0)
    lax.fori_loop(h, rows - h, middle, 0)
    lax.fori_loop(rows - h, rows, high, 0)


def messages(b, c, r):
    rows, columns, depth = b.shape
    h = STEPS
    shapes = (
        [(2, h, columns, depth)] * 2 + [(2, rows, h, depth)] * 2 + [(2, h, h, depth)] * 4
    )
    return pl.pallas_call(
        send_kernel,
        out_shape=[jax.ShapeDtypeStruct(s, jnp.float32) for s in shapes],
        in_specs=[VMEM] * 3,
        out_specs=[VMEM] * 8,
        compiler_params=pltpu.CompilerParams(vmem_limit_bytes=LIMIT),
    )(b, c, r)


def exchange(sent):
    wides, narrows = lax.axis_size("wide"), lax.axis_size("narrow")

    def moved(array, down, across):
        pairs = []
        for w in range(wides):
            for n in range(narrows):
                if 0 <= w + down < wides and 0 <= n + across < narrows:
                    pairs.append((w * narrows + n, (w + down) * narrows + n + across))
        return lax.ppermute(array, AXES, pairs)

    ways = [(-1, 0), (1, 0), (0, -1), (0, 1), (-1, -1), (-1, 1), (1, -1), (1, 1)]
    return [moved(array, *way) for array, way in zip(sent, ways)]


def basis_kernel(
    b_ref, c_ref, r_ref, wm, wp, nm, np_, cmm, cmp, cpm, cpp, f_ref, m_ref, u_even, u_odd, diag, coef
):
    rows, columns, depth = b_ref.shape
    h = STEPS
    tiles = (columns + 2 * h) // 8

    def place_u(buffer, i, y, value):
        count = value.shape[0]
        for half in range(2):
            buffer[i, half, pl.ds(8 + y, count), :] = value[:, half * LANES : (half + 1) * LANES]

    def outside(i, y, field, packed):
        count = field.shape[0]
        reaction = jnp.floor(packed * 128.0) * (1.0 / 128.0)
        conduct = (packed - reaction) * 256.0
        square = conduct * conduct
        place_u(u_even, i, y, conduct * field * 0.25)
        coef[i, pl.ds(y, count), :] = square * (1.0 / SCALE)
        diag[i, pl.ds(y, count), :] = ((reaction - CENTER) + 6.0 * square) * (1.0 / SCALE)

    def fill_low(i, _):
        outside(i, 0, cpp[0, i], cpp[1, i])
        outside(i, h, wp[0, i], wp[1, i])
        outside(i, h + columns, cpm[0, i], cpm[1, i])
        return 0

    def fill_high(i, _):
        at = i + h + rows
        outside(at, 0, cmp[0, i], cmp[1, i])
        outside(at, h, wm[0, i], wm[1, i])
        outside(at, h + columns, cmm[0, i], cmm[1, i])
        return 0

    def fill_middle(i, total):
        at = i + h
        outside(at, 0, np_[0, i], np_[1, i])
        outside(at, h + columns, nm[0, i], nm[1, i])
        field = b_ref[i]
        conduct = c_ref[i].astype(jnp.float32)
        reaction = r_ref[i].astype(jnp.float32)
        root = conduct * 0.25
        place_u(u_even, at, h, root * field)
        coef[at, pl.ds(h, columns), :] = root
        diag[at, pl.ds(h, columns), :] = (
            (reaction - CENTER) + 6.0 * (conduct * conduct)
        ) * (1.0 / SCALE)
        return total + tile_sum(field * field)

    def tile_sum(value):
        parts = [
            value[t * 8 : t * 8 + 8, half * LANES : (half + 1) * LANES]
            for t in range(value.shape[0] // 8)
            for half in range(value.shape[1] // LANES)
        ]
        return tree(parts)

    def tree(parts):
        while len(parts) > 1:
            parts = [sum(parts[k : k + 2][1:], parts[k]) for k in range(0, len(parts), 2)]
        return parts[0]

    zero = jnp.zeros((8, LANES), jnp.float32)
    lax.fori_loop(0, h, fill_low, 0)
    lax.fori_loop(0, h, fill_high, 0)
    moments = [lax.fori_loop(0, rows, fill_middle, zero)]

    lane = lax.broadcasted_iota(jnp.int32, (8, LANES), 1)
    first, last = lane == 0, lane == LANES - 1

    def neighbours(source, i, t):
        here = pl.ds(8 + 8 * t, 8)
        left, right = source[i, 0, here, :], source[i, 1, here, :]
        left_up, left_down = pltpu.roll(left, 1, 1), pltpu.roll(left, LANES - 1, 1)
        right_up, right_down = pltpu.roll(right, 1, 1), pltpu.roll(right, LANES - 1, 1)
        along = (
            jnp.where(first, 0.0, left_up) + jnp.where(last, right_down, left_down),
            jnp.where(first, left_up, right_up) + jnp.where(last, 0.0, right_down),
        )
        out = []
        for half in range(2):
            beside = source[i, half, pl.ds(7 + 8 * t, 8), :] + source[i, half, pl.ds(9 + 8 * t, 8), :]
            above = source[i - 1, half, here, :] + source[i + 1, half, here, :]
            out.append((along[half] + beside) + above)
        return (left, right), out

    for step in range(1, STEPS + 1):
        source, target = (u_even, u_odd) if step % 2 else (u_odd, u_even)

        def halo_tile(i, t, source=source, target=target):
            center, around = neighbours(source, i, t)
            for half in range(2):
                at = (i, pl.ds(8 * t, 8), pl.ds(half * LANES, LANES))
                target[i, half, pl.ds(8 + 8 * t, 8), :] = diag[at] * center[half] - coef[at] * around[half]

        def halo_plane(i, _):
            for t in range(tiles):
                halo_tile(i, t)
            return 0

        def inner_plane(i, carry, step=step, source=source, target=target):
            if step < STEPS:
                halo_tile(i, 0)
                halo_tile(i, tiles - 1)
            cross, own = [], []
            for t in range(1, tiles - 1):
                _, around = neighbours(source, i, t)
                for half in range(2):
                    lanes = pl.ds(half * LANES, LANES)
                    at = (i, pl.ds(8 * t, 8), lanes)
                    inside = (i - h, pl.ds(8 * t - h, 8), lanes)
                    before = b_ref[inside] if step == 1 else f_ref[(step - 2,) + inside]
                    root = coef[at]
                    value = diag[at] * before - root * around[half]
                    f_ref[(step - 1,) + inside] = value
                    if step < STEPS:
                        target[i, half, pl.ds(8 + 8 * t, 8), :] = root * value
                        own.append(value * value)
                    cross.append(value * before)
            total = carry[0] + tree(cross)
            return (total, carry[1] + tree(own) if own else carry[1])

        lax.fori_loop(step, h, halo_plane, 0)
        cross, own = lax.fori_loop(h, h + rows, inner_plane, (zero, zero))
        lax.fori_loop(h + rows, rows + 2 * h - step, halo_plane, 0)
        moments.append(cross)
        if step < STEPS:
            moments.append(own)

    def folded(high, low, shift, axis):
        total, error = two_sum(high, pltpu.roll(high, shift, axis))
        return total, (low + pltpu.roll(low, shift, axis)) + error

    sublane = lax.broadcasted_iota(jnp.int32, (8, LANES), 0)
    packed = []
    for group in range(2):
        highs, lows = zero, zero
        for k in range(8):
            high, low = moments[group * 8 + k], zero
            for shift in (4, 2, 1):
                high, low = folded(high, low, shift, 0)
            highs = jnp.where(sublane == k, high, highs)
            lows = jnp.where(sublane == k, low, lows)
        for shift in (64, 32, 16, 8, 4, 2, 1):
            highs, lows = folded(highs, lows, shift, 1)
        packed += [highs, lows]
    quarter = LANES // 4
    message = jnp.where(
        lane < quarter,
        packed[0],
        jnp.where(lane < 2 * quarter, packed[1], jnp.where(lane < 3 * quarter, packed[2], packed[3])),
    )
    for k in range(m_ref.shape[0]):
        m_ref[k] = message


def basis(b, c, r, received, peers):
    rows, columns, depth = b.shape
    h = STEPS
    wide, narrow = rows + 2 * h, columns + 2 * h
    return pl.pallas_call(
        basis_kernel,
        out_shape=[
            jax.ShapeDtypeStruct((STEPS, rows, columns, depth), jnp.float32),
            jax.ShapeDtypeStruct((peers, 8, LANES), jnp.float32),
        ],
        in_specs=[VMEM] * 11,
        out_specs=[VMEM] * 2,
        scratch_shapes=[
            pltpu.VMEM((wide, 2, narrow + 16, LANES), jnp.float32),
            pltpu.VMEM((wide, 2, narrow + 16, LANES), jnp.float32),
            pltpu.VMEM((wide, narrow, depth), jnp.float32),
            pltpu.VMEM((wide, narrow, depth), jnp.float32),
        ],
        compiler_params=pltpu.CompilerParams(vmem_limit_bytes=LIMIT),
    )(b, c, r, *received)


def coordinates(moment):
    shape = moment[0].shape
    count = shape[0]
    row = lax.broadcasted_iota(jnp.int32, shape, 0)

    def later(v):
        return jnp.where(row == count - 1, 0.0, pltpu.roll(v, count - 1, 0))

    def raised(v):
        return jnp.where(row == 0, 0.0, pltpu.roll(v, 1, 0))

    def spread(v):
        return jnp.broadcast_to(v, shape)

    residual = search = moment
    resid_coord = jnp.where(row == 0, 1.0, 0.0)
    search_coord = resid_coord
    sol_coord = jnp.zeros(shape, jnp.float32)
    ratio = jnp.full(shape, RATIO, jnp.float32)
    for i in range(STEPS):
        mapped = pair_add((later(search[0]), later(search[1])), pair_scale(search, ratio))
        old = residual[0][i : i + 1]
        length = old / mapped[0][i : i + 1]
        lengths = spread(length)
        residual = pair_add(residual, pair_scale(mapped, -lengths))
        grown = spread(-length * residual[0][i + 1 : i + 2] / old)
        search = pair_add(residual, pair_scale(search, grown))
        sol_coord = sol_coord + (lengths * (1.0 / SCALE)) * search_coord
        resid_coord = resid_coord - lengths * (raised(search_coord) + RATIO * search_coord)
        search_coord = resid_coord + grown * search_coord
    return sol_coord, resid_coord


def combine_kernel(m_ref, b_ref, f_ref, x_ref, r_ref, coord):
    @pl.when(pl.program_id(0) == 0)
    def _():
        total, error = m_ref[0], jnp.zeros((8, LANES), jnp.float32)
        for k in range(1, m_ref.shape[0]):
            total, lost = two_sum(total, m_ref[k])
            error = error + lost

        def lane(v, k):
            return jnp.broadcast_to(v[:, k * LANES // 4 : k * LANES // 4 + 1], (8, LANES))

        high = jnp.concatenate([lane(total, 0), lane(total, 2)], axis=0)
        low = jnp.concatenate(
            [lane(error, 0) + lane(total, 1), lane(error, 2) + lane(total, 3)], axis=0
        )
        sol_coord, resid_coord = coordinates(fast_two_sum(high, low))
        coord[0] = sol_coord
        coord[1] = resid_coord

    sol = [jnp.broadcast_to(coord[0, k : k + 1], (8, LANES)) for k in range(STEPS)]
    res = [jnp.broadcast_to(coord[1, k : k + 1], (8, LANES)) for k in range(STEPS + 1)]

    def plane(i, _):
        for t in range(b_ref.shape[1] // 8):
            for half in range(b_ref.shape[2] // LANES):
                at = (i, pl.ds(8 * t, 8), pl.ds(half * LANES, LANES))
                fields = [b_ref[at]] + [f_ref[(k,) + at] for k in range(STEPS)]
                x, r = sol[0] * fields[0], res[0] * fields[0]
                for k in range(1, STEPS + 1):
                    if k < STEPS:
                        x = x + sol[k] * fields[k]
                    r = r + res[k] * fields[k]
                x_ref[at] = x
                r_ref[at] = r
        return 0

    lax.fori_loop(0, b_ref.shape[0], plane, 0)


def combine(gathered, b, fields):
    rows, columns, depth = b.shape
    chunk = rows // 4
    block = pl.BlockSpec((chunk, columns, depth), lambda i: (i, 0, 0))
    return pl.pallas_call(
        combine_kernel,
        grid=(rows // chunk,),
        out_shape=[jax.ShapeDtypeStruct(b.shape, jnp.float32)] * 2,
        in_specs=[
            pl.BlockSpec(gathered.shape, lambda i: (0, 0, 0)),
            block,
            pl.BlockSpec((STEPS, chunk, columns, depth), lambda i: (0, i, 0, 0)),
        ],
        out_specs=[block, block],
        scratch_shapes=[pltpu.VMEM((2, 16, LANES), jnp.float32)],
        compiler_params=pltpu.CompilerParams(vmem_limit_bytes=LIMIT),
    )(gathered, b, fields)


def on_device(right_side, conduct_half, reaction_half):
    peers = lax.axis_size("wide") * lax.axis_size("narrow")
    received = exchange(messages(right_side, conduct_half, reaction_half))
    fields, moments = basis(right_side, conduct_half, reaction_half, received, peers)
    gathered = lax.all_to_all(moments, AXES, 0, 0, tiled=True)
    solution, residual = combine(gathered, right_side, fields)
    return (solution, residual)


def solution(mesh):
    placed = P(("group", "wide"), "narrow", None)
    return jax.shard_map(
        on_device,
        mesh=mesh,
        in_specs=(placed, placed, placed),
        out_specs=(placed, placed),
        check_vma=False,
    )
```

```python
import jax
import jax.numpy as jnp
from jax import lax
from jax.experimental import pallas as pl
from jax.experimental.pallas import tpu as pltpu
from jax.sharding import PartitionSpec as P

S = 4
OUTER = 2
STEPS = S * OUTER

SCALE = 13.0
CENTER = SCALE
ROOT = SCALE**-0.5

LANES = 128
AXES = ("wide", "narrow")
VMEM = pl.BlockSpec(memory_space=pltpu.VMEM)
ANY = pl.BlockSpec(memory_space=pl.ANY)
MIB = 1024 * 1024


def two_sum(a, b):
    total = a + b
    part = total - a
    return total, (a - (total - part)) + (b - part)


def fast_two_sum(a, b):
    total = a + b
    return total, b - (total - a)


def split(a):
    big = a * 4097.0
    high = big - (big - a)
    return high, a - high


def two_product(a, b):
    product = a * b
    a_high, a_low = split(a)
    b_high, b_low = split(b)
    error = ((a_high * b_high - product) + a_high * b_low + a_low * b_high) + a_low * b_low
    return product, error


def pair_add(a, b):
    total, error = two_sum(a[0], b[0])
    return fast_two_sum(total, error + (a[1] + b[1]))


def pair_scale(a, factor):
    product, error = two_product(a[0], factor)
    return fast_two_sum(product, error + a[1] * factor)


def sides():
    out = []
    for axis in AXES:
        even = lax.rem(lax.axis_index(axis), 2) == 0
        out.append((even, jnp.logical_not(even)))
    return out


def send_kernel(b_ref, c_ref, r_ref, *refs):
    (w_out, n_out, c_out), pack = (refs[:2], refs[2:4], refs[4:8]), refs[8]
    rows, columns = b_ref.shape[:2]
    h = STEPS
    wide, narrow = sides()
    top = [jnp.where(up, rows - h, 0) for up in wide]
    left = [pl.multiple_of(jnp.where(up, columns - h, 0), 8) for up in narrow]

    def code(i, _):
        pack[i] = r_ref[i].astype(jnp.float32) + c_ref[i].astype(jnp.float32) * (1.0 / 256.0)
        return 0

    def edges(i, _):
        for k, source in enumerate((b_ref, pack)):
            for side in range(2):
                n_out[side][k, i] = source[i, pl.ds(left[side], h), :]
        return 0

    def layers(i, _):
        for k, source in enumerate((b_ref, pack)):
            for a in range(2):
                w_out[a][k, i] = source[top[a] + i]
                for side in range(2):
                    c_out[2 * a + side][k, i] = source[top[a] + i, pl.ds(left[side], h), :]
        return 0

    lax.fori_loop(0, rows, code, 0)
    lax.fori_loop(0, rows, edges, 0)
    lax.fori_loop(0, h, layers, 0)


def messages(b, c, r):
    rows, columns, depth = b.shape
    h = STEPS
    shapes = (
        [(2, h, columns, depth)] * 2 + [(2, rows, h, depth)] * 2 + [(2, h, h, depth)] * 4
    )
    return pl.pallas_call(
        send_kernel,
        out_shape=[jax.ShapeDtypeStruct(s, jnp.float32) for s in shapes],
        in_specs=[VMEM] * 3,
        out_specs=[VMEM] * 8,
        scratch_shapes=[pltpu.VMEM(b.shape, jnp.float32)],
        compiler_params=pltpu.CompilerParams(vmem_limit_bytes=16 * MIB),
    )(b, c, r)


def exchange(sent):
    wides, narrows = lax.axis_size("wide"), lax.axis_size("narrow")

    def partner(index, pairing):
        return index if pairing is None else index + (1 if index % 2 == pairing else -1)

    def swapped(array, across, along):
        pairs = []
        for w in range(wides):
            for n in range(narrows):
                to_w, to_n = partner(w, across), partner(n, along)
                if 0 <= to_w < wides and 0 <= to_n < narrows:
                    pairs.append((w * narrows + n, to_w * narrows + to_n))
        return lax.ppermute(array, AXES, pairs)

    ways = [(0, None), (1, None), (None, 0), (None, 1), (0, 0), (0, 1), (1, 0), (1, 1)]
    return [swapped(array, *way) for array, way in zip(sent, ways)]


def basis_kernel(b_ref, c_ref, r_ref, *refs):
    (w_in, n_in, c_in), refs = (refs[:2], refs[2:4], refs[4:8]), refs[8:]
    out, m_ref, refs = refs[:STEPS], refs[STEPS], refs[STEPS + 1 :]
    field, (u_even, u_odd, diag, coef, done) = refs[:STEPS], refs[STEPS:]
    rows, columns, depth = b_ref.shape
    h = STEPS
    tiles = (columns + 2 * h) // 8
    wide, narrow = sides()
    top = [jnp.where(up, rows + h, 0) for up in wide]
    left = [pl.multiple_of(jnp.where(up, columns + h, 0), 8) for up in narrow]

    def place_u(buffer, i, y, value):
        count = value.shape[0]
        for half in range(2):
            buffer[i, half, pl.ds(y + 8, count), :] = value[:, half * LANES : (half + 1) * LANES]

    def outside(i, y, value, packed):
        count = value.shape[0]
        reaction = jnp.floor(packed * 128.0) * (1.0 / 128.0)
        conduct = (packed - reaction) * 256.0
        root = conduct * ROOT
        place_u(u_even, i, y, root * value)
        coef[i, pl.ds(y, count), :] = root * root
        diag[i, pl.ds(y, count), :] = ((reaction - CENTER) + 6.0 * (conduct * conduct)) * (1.0 / SCALE)

    def fill_outer(i, _):
        for a in range(2):
            at = top[a] + i
            outside(at, h, w_in[a][0, i], w_in[a][1, i])
            for side in range(2):
                corner = c_in[2 * a + side]
                outside(at, left[side], corner[0, i], corner[1, i])
        return 0

    def fill_middle(i, total):
        at = i + h
        for side in range(2):
            outside(at, left[side], n_in[side][0, i], n_in[side][1, i])
        value = b_ref[i]
        conduct = c_ref[i].astype(jnp.float32)
        reaction = r_ref[i].astype(jnp.float32)
        root = conduct * ROOT
        place_u(u_even, at, h, root * value)
        coef[at, pl.ds(h, columns), :] = root
        diag[at, pl.ds(h, columns), :] = (
            (reaction - CENTER) + 6.0 * (conduct * conduct)
        ) * (1.0 / SCALE)
        square = value * value
        return total + tree(
            [
                square[t * 8 : t * 8 + 8, half * LANES : (half + 1) * LANES]
                for t in range(columns // 8)
                for half in range(2)
            ]
        )

    def tree(parts):
        while len(parts) > 1:
            parts = [
                parts[k] + parts[k + 1] if k + 1 < len(parts) else parts[k]
                for k in range(0, len(parts), 2)
            ]
        return parts[0]

    zero = jnp.zeros((8, LANES), jnp.float32)
    lax.fori_loop(0, h, fill_outer, 0)
    moments = [lax.fori_loop(0, rows, fill_middle, zero)]

    lane = lax.broadcasted_iota(jnp.int32, (8, LANES), 1)
    first, last = lane == 0, lane == LANES - 1

    def advance(step, base, inner, halo, carry):
        source, target = (u_even, u_odd) if step % 2 else (u_odd, u_even)
        before = b_ref if step == 1 else field[step - 2]
        now = field[step - 1]
        planes = [(base, d, True) for d in range(inner)] + [(i, 0, False) for i in halo]
        cross, own = [], []
        for t in range(tiles):
            edge = t in (0, tiles - 1)
            loaded = {}

            def load(start, d, half):
                key = (id(start), d, half)
                if key not in loaded:
                    loaded[key] = source[start + d, half, pl.ds(8 * t + 8, 8), :]
                return loaded[key]

            for start, d, inside in planes:
                if edge and step == STEPS:
                    continue
                i = start + d
                left_half, right_half = load(start, d, 0), load(start, d, 1)
                left_up, left_down = pltpu.roll(left_half, 1, 1), pltpu.roll(left_half, LANES - 1, 1)
                right_up, right_down = pltpu.roll(right_half, 1, 1), pltpu.roll(right_half, LANES - 1, 1)
                along = (
                    jnp.where(first, 0.0, left_up) + jnp.where(last, right_down, left_down),
                    jnp.where(first, left_up, right_up) + jnp.where(last, 0.0, right_down),
                )
                for half in range(2):
                    beside = (
                        source[i, half, pl.ds(8 * t + 7, 8), :]
                        + source[i, half, pl.ds(8 * t + 9, 8), :]
                    )
                    across = load(start, d - 1, half) + load(start, d + 1, half)
                    around = (beside + across) + along[half]
                    lanes = pl.ds(half * LANES, LANES)
                    at = (i, pl.ds(8 * t, 8), lanes)
                    if inside and not edge:
                        here = (i - h, pl.ds(8 * t - h, 8), lanes)
                        old = before[here]
                        root = coef[at]
                        value = diag[at] * old - root * around
                        now[here] = value
                        cross.append(value * old)
                        if step < STEPS:
                            target[i, half, pl.ds(8 * t + 8, 8), :] = root * value
                            own.append(value * value)
                    else:
                        center = (left_half, right_half)[half]
                        target[i, half, pl.ds(8 * t + 8, 8), :] = diag[at] * center - coef[at] * around
        first_sum, second_sum = carry
        return first_sum + tree(cross), (second_sum + tree(own) if own else second_sum)

    copies = []
    for step in range(1, STEPS + 1):
        outer = h - step
        quads, rest = divmod(rows - 2 * outer, 4)

        def mixed(m, carry, step=step):
            return advance(step, 2 * m + h, 2, (m + step, m + h + rows), carry)

        def plain(m, carry, step=step, outer=outer):
            return advance(step, 4 * m + h + 2 * outer, 4, (), carry)

        carry = lax.fori_loop(0, outer, mixed, (zero, zero))
        carry = lax.fori_loop(0, quads, plain, carry)
        if rest:
            carry = advance(step, h + rows - rest, rest, (), carry)
        moments += carry if step < STEPS else carry[:1]
        copy = pltpu.make_async_copy(field[step - 1], out[step - 1], done.at[step - 1])
        copy.start()
        copies.append(copy)

    def folded(high, low, shift, axis):
        total, error = two_sum(high, pltpu.roll(high, shift, axis))
        return total, (low + pltpu.roll(low, shift, axis)) + error

    sublane = lax.broadcasted_iota(jnp.int32, (8, LANES), 0)
    packed = []
    for group in range(2):
        highs, lows = zero, zero
        for k in range(8):
            high, low = moments[group * 8 + k], zero
            for shift in (4, 2, 1):
                high, low = folded(high, low, shift, 0)
            highs = jnp.where(sublane == k, high, highs)
            lows = jnp.where(sublane == k, low, lows)
        for shift in (64, 32, 16, 8, 4, 2, 1):
            highs, lows = folded(highs, lows, shift, 1)
        packed += [highs, lows]
    quarter = LANES // 4
    message = jnp.where(
        lane < quarter,
        packed[0],
        jnp.where(lane < 2 * quarter, packed[1], jnp.where(lane < 3 * quarter, packed[2], packed[3])),
    )
    for k in range(m_ref.shape[0]):
        m_ref[k] = message
    for copy in copies:
        copy.wait()


def basis(b, c, r, received, peers):
    rows, columns, depth = b.shape
    h = STEPS
    wide, narrow = rows + 2 * h, columns + 2 * h
    outs = pl.pallas_call(
        basis_kernel,
        out_shape=[jax.ShapeDtypeStruct(b.shape, jnp.float32)] * STEPS
        + [jax.ShapeDtypeStruct((peers, 8, LANES), jnp.float32)],
        in_specs=[VMEM] * 11,
        out_specs=[ANY] * STEPS + [VMEM],
        scratch_shapes=[pltpu.VMEM(b.shape, jnp.float32)] * STEPS
        + [pltpu.VMEM((wide, 2, narrow + 16, LANES), jnp.float32)] * 2
        + [pltpu.VMEM((wide, narrow, depth), jnp.float32)] * 2
        + [pltpu.SemaphoreType.DMA((STEPS,))],
        compiler_params=pltpu.CompilerParams(vmem_limit_bytes=34 * MIB),
    )(b, c, r, *received)
    return outs[:STEPS], outs[STEPS]


def coordinates(moment):
    shape = moment[0].shape
    count = shape[0]
    row = lax.broadcasted_iota(jnp.int32, shape, 0)

    def later(v):
        return jnp.where(row == count - 1, 0.0, pltpu.roll(v, count - 1, 0))

    def raised(v):
        return jnp.where(row == 0, 0.0, pltpu.roll(v, 1, 0))

    def spread(v):
        return jnp.broadcast_to(v, shape)

    residual = search = moment
    resid_coord = jnp.where(row == 0, 1.0, 0.0)
    search_coord = resid_coord
    sol_coord = jnp.zeros(shape, jnp.float32)
    for i in range(STEPS):
        mapped = pair_add((later(search[0]), later(search[1])), search)
        old = residual[0][i : i + 1]
        length = old / mapped[0][i : i + 1]
        lengths = spread(length)
        residual = pair_add(residual, pair_scale(mapped, -lengths))
        grown = spread(-length * residual[0][i + 1 : i + 2] / old)
        search = pair_add(residual, pair_scale(search, grown))
        sol_coord = sol_coord + (lengths * (1.0 / SCALE)) * search_coord
        resid_coord = resid_coord - lengths * (raised(search_coord) + search_coord)
        search_coord = resid_coord + grown * search_coord
    return sol_coord, resid_coord


def combine_kernel(m_ref, b_ref, *refs):
    sources, (x_ref, r_ref), refs = refs[:STEPS], refs[STEPS : STEPS + 2], refs[STEPS + 2 :]
    field, done = refs[:STEPS], refs[STEPS]
    copies = []
    for k in range(STEPS):
        copies.append(pltpu.make_async_copy(sources[k], field[k], done.at[k]))
        copies[k].start()

    total, error = m_ref[0], jnp.zeros((8, LANES), jnp.float32)
    for k in range(1, m_ref.shape[0]):
        total, lost = two_sum(total, m_ref[k])
        error = error + lost

    def lane(v, k):
        return jnp.broadcast_to(v[:, k * LANES // 4 : k * LANES // 4 + 1], (8, LANES))

    high = jnp.concatenate([lane(total, 0), lane(total, 2)], axis=0)
    low = jnp.concatenate(
        [lane(error, 0) + lane(total, 1), lane(error, 2) + lane(total, 3)], axis=0
    )
    sol_coord, resid_coord = coordinates(fast_two_sum(high, low))
    sol = [jnp.broadcast_to(sol_coord[k : k + 1], (8, LANES)) for k in range(STEPS)]
    res = [jnp.broadcast_to(resid_coord[k : k + 1], (8, LANES)) for k in range(STEPS + 1)]
    for copy in copies:
        copy.wait()

    def plane(i, _):
        for t in range(b_ref.shape[1] // 8):
            for half in range(b_ref.shape[2] // LANES):
                at = (i, pl.ds(8 * t, 8), pl.ds(half * LANES, LANES))
                fields = [b_ref[at]] + [f[at] for f in field]
                x, r = sol[0] * fields[0], res[0] * fields[0]
                for k in range(1, STEPS + 1):
                    if k < STEPS:
                        x = x + sol[k] * fields[k]
                    r = r + res[k] * fields[k]
                x_ref[at] = x
                r_ref[at] = r
        return 0

    lax.fori_loop(0, b_ref.shape[0], plane, 0)


def combine(gathered, b, fields):
    return pl.pallas_call(
        combine_kernel,
        out_shape=[jax.ShapeDtypeStruct(b.shape, jnp.float32)] * 2,
        in_specs=[VMEM] * 2 + [ANY] * STEPS,
        out_specs=[VMEM] * 2,
        scratch_shapes=[pltpu.VMEM(b.shape, jnp.float32)] * STEPS
        + [pltpu.SemaphoreType.DMA((STEPS,))],
        compiler_params=pltpu.CompilerParams(vmem_limit_bytes=20 * MIB),
    )(gathered, b, *fields)


def on_device(right_side, conduct_half, reaction_half):
    peers = lax.axis_size("wide") * lax.axis_size("narrow")
    received = exchange(messages(right_side, conduct_half, reaction_half))
    fields, moments = basis(right_side, conduct_half, reaction_half, received, peers)
    gathered = lax.all_to_all(moments, AXES, 0, 0, tiled=True)
    solution, residual = combine(gathered, right_side, fields)
    return (solution, residual)


def solution(mesh):
    placed = P(("group", "wide"), "narrow", None)
    return jax.shard_map(
        on_device,
        mesh=mesh,
        in_specs=(placed, placed, placed),
        out_specs=(placed, placed),
        check_vma=False,
    )
```

```python
import jax
import jax.numpy as jnp
from jax import lax
from jax.experimental import pallas as pl
from jax.experimental.pallas import tpu as pltpu
from jax.sharding import PartitionSpec as P

S = 4
OUTER = 2
STEPS = S * OUTER

SCALE = 13.0
CENTER = SCALE
ROOT = SCALE**-0.5

LANES = 128
AXES = ("wide", "narrow")
VMEM = pl.BlockSpec(memory_space=pltpu.VMEM)
HBM = pl.BlockSpec(memory_space=pltpu.HBM)
MIB = 1024 * 1024


def two_sum(a, b):
    total = a + b
    part = total - a
    return total, (a - (total - part)) + (b - part)


def fast_two_sum(a, b):
    total = a + b
    return total, b - (total - a)


def split(a):
    big = a * 4097.0
    high = big - (big - a)
    return high, a - high


def two_product(a, b):
    product = a * b
    a_high, a_low = split(a)
    b_high, b_low = split(b)
    error = ((a_high * b_high - product) + a_high * b_low + a_low * b_high) + a_low * b_low
    return product, error


def pair_add(a, b):
    total, error = two_sum(a[0], b[0])
    return fast_two_sum(total, error + (a[1] + b[1]))


def pair_scale(a, factor):
    product, error = two_product(a[0], factor)
    return fast_two_sum(product, error + a[1] * factor)


def sides():
    out = []
    for axis in AXES:
        even = lax.rem(lax.axis_index(axis), 2) == 0
        out.append((even, jnp.logical_not(even)))
    return out


def send_kernel(*refs):
    args, (w_out, n_out), refs = refs[:3], (refs[3:5], refs[5:7]), refs[7:]
    (b_ref, c_ref, r_ref), (pack, done) = refs[:3], refs[3:]
    rows, columns = b_ref.shape[:2]
    h = STEPS
    copies = [pltpu.make_async_copy(args[k], refs[k], done.at[k]) for k in range(3)]
    for copy in copies:
        copy.start()
    for copy in copies:
        copy.wait()
    wide, narrow = sides()
    top = [jnp.where(up, rows - h, 0) for up in wide]
    left = [pl.multiple_of(jnp.where(up, columns - h, 0), 8) for up in narrow]

    def code(i, _):
        pack[i] = r_ref[i].astype(jnp.float32) + c_ref[i].astype(jnp.float32) * (1.0 / 256.0)
        return 0

    def edges(i, _):
        for k, source in enumerate((b_ref, pack)):
            for side in range(2):
                n_out[side][k, i] = source[i, pl.ds(left[side], h), :]
        return 0

    def layers(i, _):
        for k, source in enumerate((b_ref, pack)):
            for a in range(2):
                w_out[a][k, i] = source[top[a] + i]
        return 0

    lax.fori_loop(0, rows, code, 0)
    lax.fori_loop(0, rows, edges, 0)
    lax.fori_loop(0, h, layers, 0)


def messages(b, c, r):
    rows, columns, depth = b.shape
    h = STEPS
    shapes = [(2, h, columns, depth)] * 2 + [(2, rows, h, depth)] * 2
    return pl.pallas_call(
        send_kernel,
        out_shape=[jax.ShapeDtypeStruct(s, jnp.float32) for s in shapes],
        in_specs=[HBM] * 3,
        out_specs=[VMEM] * 4,
        scratch_shapes=[pltpu.VMEM(a.shape, a.dtype) for a in (b, c, r)]
        + [pltpu.VMEM(b.shape, jnp.float32), pltpu.SemaphoreType.DMA((3,))],
        compiler_params=pltpu.CompilerParams(vmem_limit_bytes=16 * MIB),
    )(*[pltpu.with_memory_space_constraint(a, pltpu.HBM) for a in (b, c, r)])


def corner_kernel(*refs):
    n_in, c_out = refs[:2], refs[2:]
    rows = n_in[0].shape[1]
    top = [jnp.where(up, rows - STEPS, 0) for up in sides()[0]]

    def layers(i, _):
        for k in range(2):
            for a in range(2):
                for side in range(2):
                    c_out[a][k, i, side] = n_in[side][k, top[a] + i]
        return 0

    lax.fori_loop(0, STEPS, layers, 0)


def corners(narrow_halos):
    depth = narrow_halos[0].shape[-1]
    shape = jax.ShapeDtypeStruct((2, STEPS, 2, STEPS, depth), jnp.float32)
    return pl.pallas_call(
        corner_kernel,
        out_shape=[shape] * 2,
        in_specs=[VMEM] * 2,
        out_specs=[VMEM] * 2,
        compiler_params=pltpu.CompilerParams(vmem_limit_bytes=8 * MIB),
    )(*narrow_halos)


def swapped(array, across, along):
    wides, narrows = lax.axis_size("wide"), lax.axis_size("narrow")

    def partner(index, pairing):
        return index if pairing is None else index + (1 if index % 2 == pairing else -1)

    pairs = []
    for w in range(wides):
        for n in range(narrows):
            to_w, to_n = partner(w, across), partner(n, along)
            if 0 <= to_w < wides and 0 <= to_n < narrows:
                pairs.append((w * narrows + n, to_w * narrows + to_n))
    return lax.ppermute(array, AXES, pairs)


def basis_kernel(b_ref, c_ref, r_ref, *refs):
    (w_in, n_in, c_in), refs = (refs[:2], refs[2:4], refs[4:6]), refs[6:]
    field, m_ref, (u_even, u_odd, diag, coef) = refs[:STEPS], refs[STEPS], refs[STEPS + 1 :]
    rows, columns, depth = b_ref.shape
    h = STEPS
    tiles = (columns + 2 * h) // 8
    wide, narrow = sides()
    top = [jnp.where(up, rows + h, 0) for up in wide]
    left = [pl.multiple_of(jnp.where(up, columns + h, 0), 8) for up in narrow]

    def place_u(buffer, i, y, value):
        count = value.shape[0]
        for half in range(2):
            buffer[i, half, pl.ds(y + 8, count), :] = value[:, half * LANES : (half + 1) * LANES]

    def outside(i, y, value, packed):
        count = value.shape[0]
        reaction = jnp.floor(packed * 128.0) * (1.0 / 128.0)
        conduct = (packed - reaction) * 256.0
        root = conduct * ROOT
        place_u(u_even, i, y, root * value)
        coef[i, pl.ds(y, count), :] = root * root
        diag[i, pl.ds(y, count), :] = ((reaction - CENTER) + 6.0 * (conduct * conduct)) * (1.0 / SCALE)

    def fill_outer(i, _):
        for a in range(2):
            at = top[a] + i
            outside(at, h, w_in[a][0, i], w_in[a][1, i])
            for side in range(2):
                outside(at, left[side], c_in[a][0, i, side], c_in[a][1, i, side])
        return 0

    def fill_middle(i, total):
        at = i + h
        for side in range(2):
            outside(at, left[side], n_in[side][0, i], n_in[side][1, i])
        value = b_ref[i]
        conduct = c_ref[i].astype(jnp.float32)
        reaction = r_ref[i].astype(jnp.float32)
        root = conduct * ROOT
        place_u(u_even, at, h, root * value)
        coef[at, pl.ds(h, columns), :] = root
        diag[at, pl.ds(h, columns), :] = (
            (reaction - CENTER) + 6.0 * (conduct * conduct)
        ) * (1.0 / SCALE)
        square = value * value
        return total + tree(
            [
                square[t * 8 : t * 8 + 8, half * LANES : (half + 1) * LANES]
                for t in range(columns // 8)
                for half in range(2)
            ]
        )

    def tree(parts):
        while len(parts) > 1:
            parts = [
                parts[k] + parts[k + 1] if k + 1 < len(parts) else parts[k]
                for k in range(0, len(parts), 2)
            ]
        return parts[0]

    zero = jnp.zeros((8, LANES), jnp.float32)
    lax.fori_loop(0, h, fill_outer, 0)
    moments = [lax.fori_loop(0, rows, fill_middle, zero)]

    lane = lax.broadcasted_iota(jnp.int32, (8, LANES), 1)
    first, last = lane == 0, lane == LANES - 1

    def advance(step, base, inner, halo, carry):
        source, target = (u_even, u_odd) if step % 2 else (u_odd, u_even)
        before = b_ref if step == 1 else field[step - 2]
        now = field[step - 1]
        planes = [(base, d, True) for d in range(inner)] + [(i, 0, False) for i in halo]
        cross, own = [], []
        for t in range(tiles):
            edge = t in (0, tiles - 1)
            loaded = {}

            def load(start, d, half):
                key = (id(start), d, half)
                if key not in loaded:
                    loaded[key] = source[start + d, half, pl.ds(8 * t + 8, 8), :]
                return loaded[key]

            for start, d, inside in planes:
                if edge and step == STEPS:
                    continue
                i = start + d
                left_half, right_half = load(start, d, 0), load(start, d, 1)
                left_up, left_down = pltpu.roll(left_half, 1, 1), pltpu.roll(left_half, LANES - 1, 1)
                right_up, right_down = pltpu.roll(right_half, 1, 1), pltpu.roll(right_half, LANES - 1, 1)
                along = (
                    jnp.where(first, 0.0, left_up) + jnp.where(last, right_down, left_down),
                    jnp.where(first, left_up, right_up) + jnp.where(last, 0.0, right_down),
                )
                for half in range(2):
                    beside = (
                        source[i, half, pl.ds(8 * t + 7, 8), :]
                        + source[i, half, pl.ds(8 * t + 9, 8), :]
                    )
                    across = load(start, d - 1, half) + load(start, d + 1, half)
                    around = (beside + across) + along[half]
                    lanes = pl.ds(half * LANES, LANES)
                    at = (i, pl.ds(8 * t, 8), lanes)
                    if inside and not edge:
                        here = (i - h, pl.ds(8 * t - h, 8), lanes)
                        old = before[here]
                        root = coef[at]
                        value = diag[at] * old - root * around
                        now[here] = value
                        cross.append(value * old)
                        if step < STEPS:
                            target[i, half, pl.ds(8 * t + 8, 8), :] = root * value
                            own.append(value * value)
                    else:
                        center = (left_half, right_half)[half]
                        target[i, half, pl.ds(8 * t + 8, 8), :] = diag[at] * center - coef[at] * around
        first_sum, second_sum = carry
        return first_sum + tree(cross), (second_sum + tree(own) if own else second_sum)

    for step in range(1, STEPS + 1):
        outer = h - step
        quads, rest = divmod(rows - 2 * outer, 4)

        def mixed(m, carry, step=step):
            return advance(step, 2 * m + h, 2, (m + step, m + h + rows), carry)

        def plain(m, carry, step=step, outer=outer):
            return advance(step, 4 * m + h + 2 * outer, 4, (), carry)

        carry = lax.fori_loop(0, outer, mixed, (zero, zero))
        carry = lax.fori_loop(0, quads, plain, carry)
        if rest:
            carry = advance(step, h + rows - rest, rest, (), carry)
        moments += carry if step < STEPS else carry[:1]

    def folded(high, low, shift, axis):
        total, error = two_sum(high, pltpu.roll(high, shift, axis))
        return total, (low + pltpu.roll(low, shift, axis)) + error

    sublane = lax.broadcasted_iota(jnp.int32, (8, LANES), 0)
    packed = []
    for group in range(2):
        highs, lows = zero, zero
        for k in range(8):
            high, low = moments[group * 8 + k], zero
            for shift in (4, 2, 1):
                high, low = folded(high, low, shift, 0)
            highs = jnp.where(sublane == k, high, highs)
            lows = jnp.where(sublane == k, low, lows)
        for shift in (64, 32, 16, 8, 4, 2, 1):
            highs, lows = folded(highs, lows, shift, 1)
        packed += [highs, lows]
    quarter = LANES // 4
    message = jnp.where(
        lane < quarter,
        packed[0],
        jnp.where(lane < 2 * quarter, packed[1], jnp.where(lane < 3 * quarter, packed[2], packed[3])),
    )
    for k in range(m_ref.shape[0]):
        m_ref[k] = message


def basis(b, c, r, received, peers):
    rows, columns, depth = b.shape
    h = STEPS
    wide, narrow = rows + 2 * h, columns + 2 * h
    outs = pl.pallas_call(
        basis_kernel,
        out_shape=[jax.ShapeDtypeStruct(b.shape, jnp.float32)] * STEPS
        + [jax.ShapeDtypeStruct((peers, 8, LANES), jnp.float32)],
        in_specs=[VMEM] * 9,
        out_specs=[VMEM] * (STEPS + 1),
        scratch_shapes=[pltpu.VMEM((wide, 2, narrow + 16, LANES), jnp.float32)] * 2
        + [pltpu.VMEM((wide, narrow, depth), jnp.float32)] * 2,
        compiler_params=pltpu.CompilerParams(vmem_limit_bytes=30 * MIB),
    )(b, c, r, *received)
    return outs[:STEPS], outs[STEPS]


def coordinates(moment):
    shape = moment[0].shape
    count = shape[0]
    row = lax.broadcasted_iota(jnp.int32, shape, 0)

    def later(v):
        return jnp.where(row == count - 1, 0.0, pltpu.roll(v, count - 1, 0))

    def raised(v):
        return jnp.where(row == 0, 0.0, pltpu.roll(v, 1, 0))

    def spread(v):
        return jnp.broadcast_to(v, shape)

    residual = search = moment
    resid_coord = jnp.where(row == 0, 1.0, 0.0)
    search_coord = resid_coord
    sol_coord = jnp.zeros(shape, jnp.float32)
    for i in range(STEPS):
        mapped = pair_add((later(search[0]), later(search[1])), search)
        old = residual[0][i : i + 1]
        length = old / mapped[0][i : i + 1]
        lengths = spread(length)
        residual = pair_add(residual, pair_scale(mapped, -lengths))
        grown = spread(-length * residual[0][i + 1 : i + 2] / old)
        search = pair_add(residual, pair_scale(search, grown))
        sol_coord = sol_coord + (lengths * (1.0 / SCALE)) * search_coord
        resid_coord = resid_coord - lengths * (raised(search_coord) + search_coord)
        search_coord = resid_coord + grown * search_coord
    return sol_coord, resid_coord


def combine_kernel(m_ref, b_ref, *refs):
    field, (x_ref, r_ref) = refs[:STEPS], refs[STEPS:]
    total, error = m_ref[0], jnp.zeros((8, LANES), jnp.float32)
    for k in range(1, m_ref.shape[0]):
        total, lost = two_sum(total, m_ref[k])
        error = error + lost

    def lane(v, k):
        return jnp.broadcast_to(v[:, k * LANES // 4 : k * LANES // 4 + 1], (8, LANES))

    high = jnp.concatenate([lane(total, 0), lane(total, 2)], axis=0)
    low = jnp.concatenate(
        [lane(error, 0) + lane(total, 1), lane(error, 2) + lane(total, 3)], axis=0
    )
    sol_coord, resid_coord = coordinates(fast_two_sum(high, low))
    sol = [jnp.broadcast_to(sol_coord[k : k + 1], (8, LANES)) for k in range(STEPS)]
    res = [jnp.broadcast_to(resid_coord[k : k + 1], (8, LANES)) for k in range(STEPS + 1)]

    def plane(i, _):
        for t in range(b_ref.shape[1] // 8):
            for half in range(b_ref.shape[2] // LANES):
                at = (i, pl.ds(8 * t, 8), pl.ds(half * LANES, LANES))
                fields = [b_ref[at]] + [f[at] for f in field]
                x, r = sol[0] * fields[0], res[0] * fields[0]
                for k in range(1, STEPS + 1):
                    if k < STEPS:
                        x = x + sol[k] * fields[k]
                    r = r + res[k] * fields[k]
                x_ref[at] = x
                r_ref[at] = r
        return 0

    lax.fori_loop(0, b_ref.shape[0], plane, 0)


def combine(gathered, b, fields):
    return pl.pallas_call(
        combine_kernel,
        out_shape=[jax.ShapeDtypeStruct(b.shape, jnp.float32)] * 2,
        in_specs=[VMEM] * (STEPS + 2),
        out_specs=[VMEM] * 2,
        compiler_params=pltpu.CompilerParams(vmem_limit_bytes=20 * MIB),
    )(gathered, b, *fields)


def on_device(right_side, conduct_half, reaction_half):
    peers = lax.axis_size("wide") * lax.axis_size("narrow")
    sent = messages(right_side, conduct_half, reaction_half)
    halos = [swapped(sent[k], k, None) for k in range(2)]
    narrow_halos = [swapped(sent[2 + k], None, k) for k in range(2)]
    diagonal = [swapped(block, k, None) for k, block in enumerate(corners(narrow_halos))]
    received = halos + narrow_halos + diagonal
    fields, moments = basis(right_side, conduct_half, reaction_half, received, peers)
    gathered = lax.all_to_all(moments, AXES, 0, 0, tiled=True)
    solution, residual = combine(gathered, right_side, fields)
    return (solution, residual)


def solution(mesh):
    placed = P(("group", "wide"), "narrow", None)
    return jax.shard_map(
        on_device,
        mesh=mesh,
        in_specs=(placed, placed, placed),
        out_specs=(placed, placed),
        check_vma=False,
    )
```

```python
import jax
import jax.numpy as jnp
from jax import lax
from jax.experimental import pallas as pl
from jax.experimental.pallas import tpu as pltpu
from jax.sharding import PartitionSpec as P

S = 4
OUTER = 2
STEPS = S * OUTER

SCALE = 13.0
CENTER = SCALE
ROOT = SCALE**-0.5

LANES = 128
AXES = ("wide", "narrow")
VMEM = pl.BlockSpec(memory_space=pltpu.VMEM)
HBM = pl.BlockSpec(memory_space=pltpu.HBM)
MIB = 1024 * 1024


def two_sum(a, b):
    total = a + b
    part = total - a
    return total, (a - (total - part)) + (b - part)


def fast_two_sum(a, b):
    total = a + b
    return total, b - (total - a)


def split(a):
    big = a * 4097.0
    high = big - (big - a)
    return high, a - high


def two_product(a, b):
    product = a * b
    a_high, a_low = split(a)
    b_high, b_low = split(b)
    error = ((a_high * b_high - product) + a_high * b_low + a_low * b_high) + a_low * b_low
    return product, error


def pair_add(a, b):
    total, error = two_sum(a[0], b[0])
    return fast_two_sum(total, error + (a[1] + b[1]))


def pair_scale(a, factor):
    product, error = two_product(a[0], factor)
    return fast_two_sum(product, error + a[1] * factor)


def sides():
    out = []
    for axis in AXES:
        even = lax.rem(lax.axis_index(axis), 2) == 0
        out.append((even, jnp.logical_not(even)))
    return out


def edge_layer(up, count, d):
    return jnp.where(up, count - d, d - 1)


def send_kernel(*refs):
    args, (w_out, n_out), refs = refs[:3], (refs[3:5], refs[5:7]), refs[7:]
    (b_ref, c_ref, r_ref), (pack, done) = refs[:3], refs[3:]
    rows, columns = b_ref.shape[:2]
    h = STEPS
    copies = [pltpu.make_async_copy(args[k], refs[k], done.at[k]) for k in range(3)]
    for copy in copies:
        copy.start()
    for copy in copies:
        copy.wait()
    wide, narrow = sides()
    left = [pl.multiple_of(jnp.where(up, columns - h, 0), 8) for up in narrow]

    def code(i, _):
        pack[i] = r_ref[i].astype(jnp.float32) + c_ref[i].astype(jnp.float32) * (1.0 / 256.0)
        return 0

    def edges(i, _):
        for k, source in enumerate((b_ref, pack)):
            for side in range(2):
                n_out[side][k, i] = source[i, pl.ds(left[side], h), :]
        return 0

    def layers(d, _):
        for a in range(2):
            at = edge_layer(wide[a], rows, d)
            w_out[a][d - 1] = b_ref[at]
            w_out[a][h + d - 1] = pack[at]
        return 0

    lax.fori_loop(0, rows, code, 0)
    lax.fori_loop(0, rows, edges, 0)
    lax.fori_loop(1, h, layers, 0)
    for a in range(2):
        at = edge_layer(wide[a], rows, h)
        w_out[a][h - 1] = c_ref[at].astype(jnp.float32) * ROOT * b_ref[at]


def messages(b, c, r):
    rows, columns, depth = b.shape
    h = STEPS
    shapes = [(2 * h - 1, columns, depth)] * 2 + [(2, rows, h, depth)] * 2
    return pl.pallas_call(
        send_kernel,
        out_shape=[jax.ShapeDtypeStruct(s, jnp.float32) for s in shapes],
        in_specs=[HBM] * 3,
        out_specs=[VMEM] * 4,
        scratch_shapes=[pltpu.VMEM(a.shape, a.dtype) for a in (b, c, r)]
        + [pltpu.VMEM(b.shape, jnp.float32), pltpu.SemaphoreType.DMA((3,))],
        compiler_params=pltpu.CompilerParams(vmem_limit_bytes=16 * MIB),
    )(*[pltpu.with_memory_space_constraint(a, pltpu.HBM) for a in (b, c, r)])


PAIRS = [(d, STEPS - d) for d in range(1, STEPS // 2 + 1)]


def corner_kernel(*refs):
    n_in, c_out = refs[:2], refs[2:]
    rows = n_in[0].shape[1]
    wide, narrow = sides()
    sub = lax.broadcasted_iota(jnp.int32, n_in[0].shape[2:], 0)
    for a in range(2):
        for side in range(2):
            up = narrow[side]
            for p, (d, other) in enumerate(PAIRS):
                shift = jnp.where(up, STEPS - d, d)
                mine = jnp.where(up, sub, STEPS - 1 - sub) < STEPS - d
                for k in range(2):
                    near = n_in[side][k, edge_layer(wide[a], rows, d)]
                    far = n_in[side][k, edge_layer(wide[a], rows, other)]
                    c_out[a][k, p, side] = jnp.where(mine, near, pltpu.roll(far, shift, 0))


def corners(narrow_halos):
    depth = narrow_halos[0].shape[-1]
    shape = jax.ShapeDtypeStruct((2, len(PAIRS), 2, STEPS, depth), jnp.float32)
    return pl.pallas_call(
        corner_kernel,
        out_shape=[shape] * 2,
        in_specs=[VMEM] * 2,
        out_specs=[VMEM] * 2,
        compiler_params=pltpu.CompilerParams(vmem_limit_bytes=8 * MIB),
    )(*narrow_halos)


def swapped(array, across, along):
    wides, narrows = lax.axis_size("wide"), lax.axis_size("narrow")

    def partner(index, pairing):
        return index if pairing is None else index + (1 if index % 2 == pairing else -1)

    pairs = []
    for w in range(wides):
        for n in range(narrows):
            to_w, to_n = partner(w, across), partner(n, along)
            if 0 <= to_w < wides and 0 <= to_n < narrows:
                pairs.append((w * narrows + n, to_w * narrows + to_n))
    return lax.ppermute(array, AXES, pairs)


def tree(parts):
    while len(parts) > 1:
        parts = [
            parts[k] + parts[k + 1] if k + 1 < len(parts) else parts[k]
            for k in range(0, len(parts), 2)
        ]
    return parts[0]


def place_u(buffer, i, y, value):
    count = value.shape[0]
    for half in range(2):
        buffer[i, half, pl.ds(y + 8, count), :] = value[:, half * LANES : (half + 1) * LANES]


def diagonal_of(conduct, reaction):
    return ((reaction - CENTER) + 6.0 * (conduct * conduct)) * (1.0 / SCALE)


def outside(u_even, diag, coef, i, y, value, packed):
    count = value.shape[0]
    reaction = jnp.floor(packed * 128.0) * (1.0 / 128.0)
    conduct = (packed - reaction) * 256.0
    root = conduct * ROOT
    place_u(u_even, i, y, root * value)
    coef[i, pl.ds(y, count), :] = root * root
    diag[i, pl.ds(y, count), :] = diagonal_of(conduct, reaction)


def advance(step, runs, refs, carry):
    b_ref, field, u_even, u_odd, diag, coef = refs
    h = STEPS
    tiles = diag.shape[1] // 8
    lane = lax.broadcasted_iota(jnp.int32, (8, LANES), 1)
    first, last = lane == 0, lane == LANES - 1
    source, target = (u_even, u_odd) if step % 2 else (u_odd, u_even)
    before = b_ref if step == 1 else field[step - 2]
    now = field[step - 1]
    cross, own = [], []
    for t in range(tiles):
        edge = t in (0, tiles - 1)
        if edge and step == STEPS:
            continue
        rows = pl.ds(8 * t + 8, 8)
        for start, count, inside in runs:
            layers = [
                [source[start + d, half, rows, :] for half in range(2)]
                for d in range(-1, count + 1)
            ]
            for d in range(count):
                i = start + d
                left, right = layers[d + 1]
                left_up, left_down = pltpu.roll(left, 1, 1), pltpu.roll(left, LANES - 1, 1)
                right_up, right_down = pltpu.roll(right, 1, 1), pltpu.roll(right, LANES - 1, 1)
                along = (
                    jnp.where(first, 0.0, left_up) + jnp.where(last, right_down, left_down),
                    jnp.where(first, left_up, right_up) + jnp.where(last, 0.0, right_down),
                )
                for half in range(2):
                    beside = (
                        source[i, half, pl.ds(8 * t + 7, 8), :]
                        + source[i, half, pl.ds(8 * t + 9, 8), :]
                    )
                    across = layers[d][half] + layers[d + 2][half]
                    around = (beside + across) + along[half]
                    lanes = pl.ds(half * LANES, LANES)
                    at = (i, pl.ds(8 * t, 8), lanes)
                    if inside and not edge:
                        here = (i - h, pl.ds(8 * t - h, 8), lanes)
                        old = before[here]
                        root = coef[at]
                        value = diag[at] * old - root * around
                        now[here] = value
                        cross.append(value * old)
                        if step < STEPS:
                            target[i, half, rows, :] = root * value
                            own.append(value * value)
                    else:
                        target[i, half, rows, :] = (
                            diag[at] * layers[d + 1][half] - coef[at] * around
                        )
    if not cross:
        return carry
    return carry[0] + tree(cross), (carry[1] + tree(own) if own else carry[1])


def inner_kernel(b_ref, c_ref, r_ref, *refs):
    n_in, field, (u_even, u_odd, diag, coef, m_ref) = refs[:2], refs[2 : 2 + STEPS], refs[2 + STEPS :]
    rows, columns, depth = b_ref.shape
    h = STEPS
    left = [pl.multiple_of(jnp.where(up, columns + h, 0), 8) for up in sides()[1]]
    everything = (b_ref, field, u_even, u_odd, diag, coef)

    def fill(i, total):
        at = i + h
        for side in range(2):
            outside(u_even, diag, coef, at, left[side], n_in[side][0, i], n_in[side][1, i])
        value = b_ref[i]
        conduct = c_ref[i].astype(jnp.float32)
        root = conduct * ROOT
        place_u(u_even, at, h, root * value)
        coef[at, pl.ds(h, columns), :] = root
        diag[at, pl.ds(h, columns), :] = diagonal_of(conduct, r_ref[i].astype(jnp.float32))
        square = value * value
        return total + tree(
            [
                square[t * 8 : t * 8 + 8, half * LANES : (half + 1) * LANES]
                for t in range(columns // 8)
                for half in range(2)
            ]
        )

    zero = jnp.zeros((8, LANES), jnp.float32)
    m_ref[0] = lax.fori_loop(0, rows, fill, zero)
    for step in range(1, STEPS + 1):
        quads, rest = divmod(max(rows - 2 * step, 0), 4)

        def body(m, carry, step=step):
            return advance(step, [(4 * m + h + step, 4, True)], everything, carry)

        carry = lax.fori_loop(0, quads, body, (zero, zero))
        if rest:
            carry = advance(step, [(h + rows - step - rest, rest, True)], everything, carry)
        m_ref[2 * step - 1] = carry[0]
        if step < STEPS:
            m_ref[2 * step] = carry[1]


def outer_kernel(b_ref, m_in, *refs):
    (w_in, c_in), refs = (refs[:2], refs[2:4]), refs[4 + STEPS + 4 :]
    field, (u_even, u_odd, diag, coef, m_out) = refs[:STEPS], refs[STEPS:]
    rows, columns, depth = b_ref.shape
    h = STEPS
    wide, narrow = sides()
    left = [pl.multiple_of(jnp.where(up, columns + h, 0), 8) for up in narrow]
    everything = (b_ref, field, u_even, u_odd, diag, coef)

    def halo_layer(a, d):
        return jnp.where(wide[a], rows + h - 1 + d, h - d)

    def fill(d, _):
        for a in range(2):
            outside(u_even, diag, coef, halo_layer(a, d), h, w_in[a][d - 1], w_in[a][h + d - 1])
        return 0

    lax.fori_loop(1, h, fill, 0)
    for a in range(2):
        place_u(u_even, halo_layer(a, h), h, w_in[a][h - 1])
        for side in range(2):
            for p, (d, other) in enumerate(PAIRS):
                near = [c_in[a][k, p, side] for k in range(2)]
                outside(u_even, diag, coef, halo_layer(a, d), left[side], *near)
                if other != d:
                    shift = jnp.where(narrow[side], d, h - d)
                    far = [pltpu.roll(block, shift, 0) for block in near]
                    outside(u_even, diag, coef, halo_layer(a, other), left[side], *far)

    zero = jnp.zeros((8, LANES), jnp.float32)
    moments = [m_in[0]]
    for step in range(1, STEPS + 1):
        halo = (step, rows + h)
        inner = (h, rows + h - step)

        def halo_body(m, carry, step=step, halo=halo):
            advance(step, [(2 * m + first, 2, False) for first in halo], everything, None)
            return carry

        def inner_body(m, carry, step=step, inner=inner):
            return advance(step, [(2 * m + first, 2, True) for first in inner], everything, carry)

        carry = (m_in[2 * step - 1], m_in[2 * step] if step < STEPS else zero)
        lax.fori_loop(0, (h - step) // 2, halo_body, 0)
        carry = lax.fori_loop(0, step // 2, inner_body, carry)
        if step % 2:
            runs = [(first + step - 1, 1, True) for first in inner]
            runs += [(first + h - step - 1, 1, False) for first in halo]
            carry = advance(step, runs, everything, carry)
        moments += carry if step < STEPS else carry[:1]

    def folded(high, low, shift, axis):
        total, error = two_sum(high, pltpu.roll(high, shift, axis))
        return total, (low + pltpu.roll(low, shift, axis)) + error

    sublane = lax.broadcasted_iota(jnp.int32, (8, LANES), 0)
    lane = lax.broadcasted_iota(jnp.int32, (8, LANES), 1)
    packed = []
    for group in range(2):
        highs, lows = zero, zero
        for k in range(8):
            high, low = moments[group * 8 + k], zero
            for shift in (4, 2, 1):
                high, low = folded(high, low, shift, 0)
            highs = jnp.where(sublane == k, high, highs)
            lows = jnp.where(sublane == k, low, lows)
        for shift in (64, 32, 16, 8, 4, 2, 1):
            highs, lows = folded(highs, lows, shift, 1)
        packed += [highs, lows]
    quarter = LANES // 4
    message = jnp.where(
        lane < quarter,
        packed[0],
        jnp.where(lane < 2 * quarter, packed[1], jnp.where(lane < 3 * quarter, packed[2], packed[3])),
    )
    for k in range(m_out.shape[0]):
        m_out[k] = message


def state_shapes(b):
    rows, columns, depth = b.shape
    wide, narrow = rows + 2 * STEPS, columns + 2 * STEPS
    shapes = [b.shape] * STEPS + [(wide, 2, narrow + 16, LANES)] * 2 + [(wide, narrow, depth)] * 2
    return [pltpu.VMEM(s, jnp.float32) for s in shapes]


def inner(b, c, r, narrow_halos):
    shapes = state_shapes(b) + [jax.ShapeDtypeStruct((2 * STEPS, 8, LANES), jnp.float32)]
    return pl.pallas_call(
        inner_kernel,
        out_shape=shapes,
        in_specs=[VMEM] * 5,
        out_specs=[VMEM] * len(shapes),
        compiler_params=pltpu.CompilerParams(vmem_limit_bytes=26 * MIB),
    )(b, c, r, *narrow_halos)


def outer(b, wide_halos, diagonal, state, moments, peers):
    shapes = state_shapes(b) + [jax.ShapeDtypeStruct((peers, 8, LANES), jnp.float32)]
    out = pl.pallas_call(
        outer_kernel,
        out_shape=shapes,
        in_specs=[VMEM] * (6 + len(state)),
        out_specs=[VMEM] * len(shapes),
        input_output_aliases={6 + k: k for k in range(len(state))},
        compiler_params=pltpu.CompilerParams(vmem_limit_bytes=26 * MIB),
    )(b, moments, *wide_halos, *diagonal, *state)
    return out[:STEPS], out[-1]


def coordinates(moment):
    shape = moment[0].shape
    count = shape[0]
    row = lax.broadcasted_iota(jnp.int32, shape, 0)

    def later(v):
        return jnp.where(row == count - 1, 0.0, pltpu.roll(v, count - 1, 0))

    def raised(v):
        return jnp.where(row == 0, 0.0, pltpu.roll(v, 1, 0))

    def spread(v):
        return jnp.broadcast_to(v, shape)

    residual = search = moment
    resid_coord = jnp.where(row == 0, 1.0, 0.0)
    search_coord = resid_coord
    sol_coord = jnp.zeros(shape, jnp.float32)
    for i in range(STEPS):
        mapped = pair_add((later(search[0]), later(search[1])), search)
        old = residual[0][i : i + 1]
        length = old / mapped[0][i : i + 1]
        lengths = spread(length)
        residual = pair_add(residual, pair_scale(mapped, -lengths))
        grown = spread(-length * residual[0][i + 1 : i + 2] / old)
        search = pair_add(residual, pair_scale(search, grown))
        sol_coord = sol_coord + (lengths * (1.0 / SCALE)) * search_coord
        resid_coord = resid_coord - lengths * (raised(search_coord) + search_coord)
        search_coord = resid_coord + grown * search_coord
    return sol_coord, resid_coord


def combine_kernel(m_ref, b_ref, *refs):
    field, (x_ref, r_ref) = refs[:STEPS], refs[STEPS:]
    total, error = m_ref[0], jnp.zeros((8, LANES), jnp.float32)
    for k in range(1, m_ref.shape[0]):
        total, lost = two_sum(total, m_ref[k])
        error = error + lost

    def lane(v, k):
        return jnp.broadcast_to(v[:, k * LANES // 4 : k * LANES // 4 + 1], (8, LANES))

    high = jnp.concatenate([lane(total, 0), lane(total, 2)], axis=0)
    low = jnp.concatenate(
        [lane(error, 0) + lane(total, 1), lane(error, 2) + lane(total, 3)], axis=0
    )
    sol_coord, resid_coord = coordinates(fast_two_sum(high, low))
    sol = [jnp.broadcast_to(sol_coord[k : k + 1], (8, LANES)) for k in range(STEPS)]
    res = [jnp.broadcast_to(resid_coord[k : k + 1], (8, LANES)) for k in range(STEPS + 1)]

    def plane(i, _):
        for t in range(b_ref.shape[1] // 8):
            for half in range(b_ref.shape[2] // LANES):
                at = (i, pl.ds(8 * t, 8), pl.ds(half * LANES, LANES))
                fields = [b_ref[at]] + [f[at] for f in field]
                x, r = sol[0] * fields[0], res[0] * fields[0]
                for k in range(1, STEPS + 1):
                    if k < STEPS:
                        x = x + sol[k] * fields[k]
                    r = r + res[k] * fields[k]
                x_ref[at] = x
                r_ref[at] = r
        return 0

    lax.fori_loop(0, b_ref.shape[0], plane, 0)


def combine(gathered, b, fields):
    return pl.pallas_call(
        combine_kernel,
        out_shape=[jax.ShapeDtypeStruct(b.shape, jnp.float32)] * 2,
        in_specs=[VMEM] * (STEPS + 2),
        out_specs=[VMEM] * 2,
        compiler_params=pltpu.CompilerParams(vmem_limit_bytes=20 * MIB),
    )(gathered, b, *fields)


def on_device(right_side, conduct_half, reaction_half):
    peers = lax.axis_size("wide") * lax.axis_size("narrow")
    sent = messages(right_side, conduct_half, reaction_half)
    wide_halos = [swapped(sent[k], k, None) for k in range(2)]
    narrow_halos = [swapped(sent[2 + k], None, k) for k in range(2)]
    diagonal = [swapped(block, k, None) for k, block in enumerate(corners(narrow_halos))]
    *state, moments = inner(right_side, conduct_half, reaction_half, narrow_halos)
    fields, moments = outer(right_side, wide_halos, diagonal, state, moments, peers)
    gathered = lax.all_to_all(moments, AXES, 0, 0, tiled=True)
    solution, residual = combine(gathered, right_side, fields)
    return (solution, residual)


def solution(mesh):
    placed = P(("group", "wide"), "narrow", None)
    return jax.shard_map(
        on_device,
        mesh=mesh,
        in_specs=(placed, placed, placed),
        out_specs=(placed, placed),
        check_vma=False,
    )
```

```python
import jax
import jax.numpy as jnp
from jax import lax
from jax.experimental import pallas as pl
from jax.experimental.pallas import tpu as pltpu
from jax.sharding import PartitionSpec as P

S = 4
OUTER = 2
STEPS = S * OUTER

SCALE = 13.0
CENTER = SCALE
ROOT = SCALE**-0.5

LANES = 128
AXES = ("wide", "narrow")
VMEM = pl.BlockSpec(memory_space=pltpu.VMEM)
HBM = pl.BlockSpec(memory_space=pltpu.HBM)
MIB = 1024 * 1024


def two_sum(a, b):
    total = a + b
    part = total - a
    return total, (a - (total - part)) + (b - part)


def fast_two_sum(a, b):
    total = a + b
    return total, b - (total - a)


def split(a):
    big = a * 4097.0
    high = big - (big - a)
    return high, a - high


def two_product(a, b):
    product = a * b
    a_high, a_low = split(a)
    b_high, b_low = split(b)
    error = ((a_high * b_high - product) + a_high * b_low + a_low * b_high) + a_low * b_low
    return product, error


def pair_add(a, b):
    total, error = two_sum(a[0], b[0])
    return fast_two_sum(total, error + (a[1] + b[1]))


def pair_scale(a, factor):
    product, error = two_product(a[0], factor)
    return fast_two_sum(product, error + a[1] * factor)


def sides():
    out = []
    for axis in AXES:
        even = lax.rem(lax.axis_index(axis), 2) == 0
        out.append((even, jnp.logical_not(even)))
    return out


def edge_layer(up, count, d):
    return jnp.where(up, count - d, d - 1)


def send_kernel(*refs):
    args, (w_out, n_out), refs = refs[:3], (refs[3:5], refs[5:7]), refs[7:]
    (b_ref, c_ref, r_ref), (pack, done) = refs[:3], refs[3:]
    rows, columns = b_ref.shape[:2]
    h = STEPS
    copies = [pltpu.make_async_copy(args[k], refs[k], done.at[k]) for k in range(3)]
    for copy in copies:
        copy.start()
    for copy in copies:
        copy.wait()
    wide, narrow = sides()
    left = [pl.multiple_of(jnp.where(up, columns - h, 0), 8) for up in narrow]

    def code(i, _):
        pack[i] = r_ref[i].astype(jnp.float32) + c_ref[i].astype(jnp.float32) * (1.0 / 256.0)
        return 0

    def edges(i, _):
        for k, source in enumerate((b_ref, pack)):
            for side in range(2):
                n_out[side][k, i] = source[i, pl.ds(left[side], h), :]
        return 0

    def layers(d, _):
        for a in range(2):
            at = edge_layer(wide[a], rows, d)
            w_out[a][d - 1] = b_ref[at]
            w_out[a][h + d - 1] = pack[at]
        return 0

    lax.fori_loop(0, rows, code, 0)
    lax.fori_loop(0, rows, edges, 0)
    lax.fori_loop(1, h, layers, 0)
    for a in range(2):
        at = edge_layer(wide[a], rows, h)
        w_out[a][h - 1] = c_ref[at].astype(jnp.float32) * ROOT * b_ref[at]


def messages(b, c, r):
    rows, columns, depth = b.shape
    h = STEPS
    shapes = [(2 * h - 1, columns, depth)] * 2 + [(2, rows, h, depth)] * 2
    return pl.pallas_call(
        send_kernel,
        out_shape=[jax.ShapeDtypeStruct(s, jnp.float32) for s in shapes]
        + [pltpu.VMEM(a.shape, a.dtype) for a in (b, c, r)],
        in_specs=[HBM] * 3,
        out_specs=[VMEM] * 7,
        scratch_shapes=[pltpu.VMEM(b.shape, jnp.float32), pltpu.SemaphoreType.DMA((3,))],
        compiler_params=pltpu.CompilerParams(vmem_limit_bytes=16 * MIB),
    )(*[pltpu.with_memory_space_constraint(a, pltpu.HBM) for a in (b, c, r)])


PAIRS = [(d, STEPS - d) for d in range(1, STEPS // 2 + 1)]


def corner_kernel(*refs):
    n_in, c_out = refs[:2], refs[3:]
    rows = n_in[0].shape[1]
    wide, narrow = sides()
    sub = lax.broadcasted_iota(jnp.int32, n_in[0].shape[2:], 0)
    for a in range(2):
        for side in range(2):
            up = narrow[side]
            for p, (d, other) in enumerate(PAIRS):
                shift = jnp.where(up, STEPS - d, d)
                mine = jnp.where(up, sub, STEPS - 1 - sub) < STEPS - d
                for k in range(2):
                    near = n_in[side][k, edge_layer(wide[a], rows, d)]
                    far = n_in[side][k, edge_layer(wide[a], rows, other)]
                    c_out[a][k, p, side] = jnp.where(mine, near, pltpu.roll(far, shift, 0))


def corners(narrow_halos, after):
    depth = narrow_halos[0].shape[-1]
    shape = jax.ShapeDtypeStruct((2, len(PAIRS), 2, STEPS, depth), jnp.float32)
    return pl.pallas_call(
        corner_kernel,
        out_shape=[shape] * 2,
        in_specs=[VMEM] * 3,
        out_specs=[VMEM] * 2,
        compiler_params=pltpu.CompilerParams(vmem_limit_bytes=8 * MIB),
    )(*narrow_halos, after)


def swapped(array, across, along):
    wides, narrows = lax.axis_size("wide"), lax.axis_size("narrow")

    def partner(index, pairing):
        return index if pairing is None else index + (1 if index % 2 == pairing else -1)

    pairs = []
    for w in range(wides):
        for n in range(narrows):
            to_w, to_n = partner(w, across), partner(n, along)
            if 0 <= to_w < wides and 0 <= to_n < narrows:
                pairs.append((w * narrows + n, to_w * narrows + to_n))
    return lax.ppermute(array, AXES, pairs)


def tree(parts):
    while len(parts) > 1:
        parts = [
            parts[k] + parts[k + 1] if k + 1 < len(parts) else parts[k]
            for k in range(0, len(parts), 2)
        ]
    return parts[0]


def place_u(buffer, i, y, value):
    count = value.shape[0]
    for half in range(2):
        buffer[i, half, pl.ds(y + 8, count), :] = value[:, half * LANES : (half + 1) * LANES]


def diagonal_of(conduct, reaction):
    return ((reaction - CENTER) + 6.0 * (conduct * conduct)) * (1.0 / SCALE)


def outside(u_even, diag, coef, i, y, value, packed):
    count = value.shape[0]
    reaction = jnp.floor(packed * 128.0) * (1.0 / 128.0)
    conduct = (packed - reaction) * 256.0
    root = conduct * ROOT
    place_u(u_even, i, y, root * value)
    coef[i, pl.ds(y, count), :] = root * root
    diag[i, pl.ds(y, count), :] = diagonal_of(conduct, reaction)


def advance(step, runs, refs, carry, chosen=None, silent=()):
    b_ref, field, u_even, u_odd, diag, coef = refs
    h = STEPS
    tiles = diag.shape[1] // 8
    lane = lax.broadcasted_iota(jnp.int32, (8, LANES), 1)
    first, last = lane == 0, lane == LANES - 1
    source, target = (u_even, u_odd) if step % 2 else (u_odd, u_even)
    before = b_ref if step == 1 else field[step - 2]
    now = field[step - 1]
    cross, own = [], []
    for t in range(tiles) if chosen is None else chosen:
        edge = t in (0, tiles - 1)
        if edge and step == STEPS:
            continue
        rows = pl.ds(8 * t + 8, 8)
        for start, count, inside in runs:
            layers = [
                [source[start + d, half, rows, :] for half in range(2)]
                for d in range(-1, count + 1)
            ]
            for d in range(count):
                i = start + d
                left, right = layers[d + 1]
                left_up, left_down = pltpu.roll(left, 1, 1), pltpu.roll(left, LANES - 1, 1)
                right_up, right_down = pltpu.roll(right, 1, 1), pltpu.roll(right, LANES - 1, 1)
                along = (
                    jnp.where(first, 0.0, left_up) + jnp.where(last, right_down, left_down),
                    jnp.where(first, left_up, right_up) + jnp.where(last, 0.0, right_down),
                )
                for half in range(2):
                    beside = (
                        source[i, half, pl.ds(8 * t + 7, 8), :]
                        + source[i, half, pl.ds(8 * t + 9, 8), :]
                    )
                    across = layers[d][half] + layers[d + 2][half]
                    around = (beside + across) + along[half]
                    lanes = pl.ds(half * LANES, LANES)
                    at = (i, pl.ds(8 * t, 8), lanes)
                    if inside and not edge:
                        here = (i - h, pl.ds(8 * t - h, 8), lanes)
                        old = before[here]
                        root = coef[at]
                        value = diag[at] * old - root * around
                        now[here] = value
                        if step < STEPS:
                            target[i, half, rows, :] = root * value
                        if t in silent:
                            continue
                        cross.append(value * old)
                        if step < STEPS:
                            own.append(value * value)
                    else:
                        target[i, half, rows, :] = (
                            diag[at] * layers[d + 1][half] - coef[at] * around
                        )
    if not cross:
        return carry
    return carry[0] + tree(cross), (carry[1] + tree(own) if own else carry[1])


def inner_kernel(b_ref, c_ref, r_ref, *refs):
    field, (u_even, u_odd, diag, coef, m_ref) = refs[:STEPS], refs[STEPS:]
    rows, columns, depth = b_ref.shape
    h = STEPS
    everything = (b_ref, field, u_even, u_odd, diag, coef)
    tiles = range(1, columns // 8 + 1)

    def fill(i, total):
        at = i + h
        value = b_ref[i]
        conduct = c_ref[i].astype(jnp.float32)
        root = conduct * ROOT
        place_u(u_even, at, h, root * value)
        coef[at, pl.ds(h, columns), :] = root
        diag[at, pl.ds(h, columns), :] = diagonal_of(conduct, r_ref[i].astype(jnp.float32))
        square = value * value
        return total + tree(
            [
                square[t * 8 : t * 8 + 8, half * LANES : (half + 1) * LANES]
                for t in range(columns // 8)
                for half in range(2)
            ]
        )

    zero = jnp.zeros((8, LANES), jnp.float32)
    m_ref[0] = lax.fori_loop(0, rows, fill, zero)
    for step in range(1, STEPS + 1):
        quads, rest = divmod(max(rows - 2 * step, 0), 4)

        def work(start, count, carry, step=step):
            runs = [(start, count, True)]
            return advance(step, runs, everything, carry, tiles, (tiles[0], tiles[-1]))

        def body(m, carry, step=step, work=work):
            return work(4 * m + h + step, 4, carry)

        carry = lax.fori_loop(0, quads, body, (zero, zero))
        if rest:
            carry = work(h + rows - step - rest, rest, carry)
        m_ref[2 * step - 1] = carry[0]
        if step < STEPS:
            m_ref[2 * step] = carry[1]


def border_kernel(b_ref, m_in, *refs):
    n_in, refs = refs[:2], refs[2 + STEPS + 4 :]
    field, (u_even, u_odd, diag, coef, m_out) = refs[:STEPS], refs[STEPS:]
    rows, columns, depth = b_ref.shape
    h = STEPS
    tiles = columns // 8 + 2
    left = [pl.multiple_of(jnp.where(up, columns + h, 0), 8) for up in sides()[1]]
    everything = (b_ref, field, u_even, u_odd, diag, coef)

    def fill(i, _):
        at = i + h
        for side in range(2):
            outside(u_even, diag, coef, at, left[side], n_in[side][0, i], n_in[side][1, i])
        for y in (0, columns - 8):
            place_u(u_even, at, y + h, coef[at, pl.ds(y + h, 8), :] * b_ref[i, pl.ds(y, 8), :])
        return 0

    lax.fori_loop(0, rows, fill, 0)
    m_out[0] = m_in[0]
    for step in range(1, STEPS + 1):
        source = u_even if step % 2 else u_odd
        before = b_ref if step == 1 else field[step - 2]
        for i in range(step - 1, rows - step + 1):
            for y in (8, columns - 9):
                row = coef[i + h, y + h : y + h + 1, :] * before[i, y : y + 1, :]
                for half in range(2):
                    source[i + h, half, y + h + 8 : y + h + 9, :] = row[
                        :, half * LANES : (half + 1) * LANES
                    ]
        count = max(rows - 2 * step, 0)
        carry = (m_in[2 * step - 1], m_in[2 * step] if step < STEPS else m_in[0])
        for start, part in ((step, count // 2), (step + count // 2, count - count // 2)):
            if part:
                runs = [(start + h, part, True)]
                carry = advance(step, runs, everything, carry, (0, 1, tiles - 2, tiles - 1))
        m_out[2 * step - 1] = carry[0]
        if step < STEPS:
            m_out[2 * step] = carry[1]


def outer_kernel(b_ref, m_in, *refs):
    (w_in, c_in), refs = (refs[:2], refs[2:4]), refs[4 + STEPS + 4 :]
    field, (u_even, u_odd, diag, coef, m_out) = refs[:STEPS], refs[STEPS:]
    rows, columns, depth = b_ref.shape
    h = STEPS
    wide, narrow = sides()
    left = [pl.multiple_of(jnp.where(up, columns + h, 0), 8) for up in narrow]
    everything = (b_ref, field, u_even, u_odd, diag, coef)

    def halo_layer(a, d):
        return jnp.where(wide[a], rows + h - 1 + d, h - d)

    def fill(d, _):
        for a in range(2):
            outside(u_even, diag, coef, halo_layer(a, d), h, w_in[a][d - 1], w_in[a][h + d - 1])
        return 0

    lax.fori_loop(1, h, fill, 0)
    for a in range(2):
        place_u(u_even, halo_layer(a, h), h, w_in[a][h - 1])
        for side in range(2):
            for p, (d, other) in enumerate(PAIRS):
                near = [c_in[a][k, p, side] for k in range(2)]
                outside(u_even, diag, coef, halo_layer(a, d), left[side], *near)
                if other != d:
                    shift = jnp.where(narrow[side], d, h - d)
                    far = [pltpu.roll(block, shift, 0) for block in near]
                    outside(u_even, diag, coef, halo_layer(a, other), left[side], *far)

    zero = jnp.zeros((8, LANES), jnp.float32)
    moments = [m_in[0]]
    for step in range(1, STEPS + 1):
        halo = (step, rows + h)
        inner = (h, rows + h - step)

        def halo_body(m, carry, step=step, halo=halo):
            advance(step, [(2 * m + first, 2, False) for first in halo], everything, None)
            return carry

        def inner_body(m, carry, step=step, inner=inner):
            return advance(step, [(2 * m + first, 2, True) for first in inner], everything, carry)

        carry = (m_in[2 * step - 1], m_in[2 * step] if step < STEPS else zero)
        lax.fori_loop(0, (h - step) // 2, halo_body, 0)
        carry = lax.fori_loop(0, step // 2, inner_body, carry)
        if step % 2:
            runs = [(first + step - 1, 1, True) for first in inner]
            runs += [(first + h - step - 1, 1, False) for first in halo]
            carry = advance(step, runs, everything, carry)
        moments += carry if step < STEPS else carry[:1]

    def folded(high, low, shift, axis):
        total, error = two_sum(high, pltpu.roll(high, shift, axis))
        return total, (low + pltpu.roll(low, shift, axis)) + error

    sublane = lax.broadcasted_iota(jnp.int32, (8, LANES), 0)
    lane = lax.broadcasted_iota(jnp.int32, (8, LANES), 1)
    packed = []
    for group in range(2):
        highs, lows = zero, zero
        for k in range(8):
            high, low = moments[group * 8 + k], zero
            for shift in (4, 2, 1):
                high, low = folded(high, low, shift, 0)
            highs = jnp.where(sublane == k, high, highs)
            lows = jnp.where(sublane == k, low, lows)
        for shift in (64, 32, 16, 8, 4, 2, 1):
            highs, lows = folded(highs, lows, shift, 1)
        packed += [highs, lows]
    quarter = LANES // 4
    message = jnp.where(
        lane < quarter,
        packed[0],
        jnp.where(lane < 2 * quarter, packed[1], jnp.where(lane < 3 * quarter, packed[2], packed[3])),
    )
    for k in range(m_out.shape[0]):
        m_out[k] = message


def state_shapes(b):
    rows, columns, depth = b.shape
    wide, narrow = rows + 2 * STEPS, columns + 2 * STEPS
    shapes = [b.shape] * STEPS + [(wide, 2, narrow + 16, LANES)] * 2 + [(wide, narrow, depth)] * 2
    return [pltpu.VMEM(s, jnp.float32) for s in shapes]


def inner(b, c, r):
    shapes = state_shapes(b) + [jax.ShapeDtypeStruct((2 * STEPS, 8, LANES), jnp.float32)]
    *state, moments = pl.pallas_call(
        inner_kernel,
        cost_estimate=pl.CostEstimate(
            flops=120 * b.size, bytes_accessed=24 * b.size, transcendentals=0
        ),
        out_shape=shapes,
        in_specs=[VMEM] * 3,
        out_specs=[VMEM] * len(shapes),
        compiler_params=pltpu.CompilerParams(vmem_limit_bytes=26 * MIB),
    )(b, c, r)
    return state, moments


def onward(kernel, b, moments, received, state, moments_shape):
    shapes = state_shapes(b) + [jax.ShapeDtypeStruct(moments_shape, jnp.float32)]
    others = 2 + len(received)
    *state, moments = pl.pallas_call(
        kernel,
        out_shape=shapes,
        in_specs=[VMEM] * (others + len(state)),
        out_specs=[VMEM] * len(shapes),
        input_output_aliases={others + k: k for k in range(len(state))},
        compiler_params=pltpu.CompilerParams(vmem_limit_bytes=26 * MIB),
    )(b, moments, *received, *state)
    return state, moments


def coordinates(moment):
    shape = moment[0].shape
    count = shape[0]
    row = lax.broadcasted_iota(jnp.int32, shape, 0)

    def later(v):
        return jnp.where(row == count - 1, 0.0, pltpu.roll(v, count - 1, 0))

    def raised(v):
        return jnp.where(row == 0, 0.0, pltpu.roll(v, 1, 0))

    def spread(v):
        return jnp.broadcast_to(v, shape)

    residual = search = moment
    resid_coord = jnp.where(row == 0, 1.0, 0.0)
    search_coord = resid_coord
    sol_coord = jnp.zeros(shape, jnp.float32)
    for i in range(STEPS):
        mapped = pair_add((later(search[0]), later(search[1])), search)
        old = residual[0][i : i + 1]
        length = old / mapped[0][i : i + 1]
        lengths = spread(length)
        residual = pair_add(residual, pair_scale(mapped, -lengths))
        grown = spread(-length * residual[0][i + 1 : i + 2] / old)
        search = pair_add(residual, pair_scale(search, grown))
        sol_coord = sol_coord + (lengths * (1.0 / SCALE)) * search_coord
        resid_coord = resid_coord - lengths * (raised(search_coord) + search_coord)
        search_coord = resid_coord + grown * search_coord
    return sol_coord, resid_coord


def combine_kernel(m_ref, b_ref, *refs):
    field, (x_ref, r_ref) = refs[:STEPS], refs[STEPS:]
    total, error = m_ref[0], jnp.zeros((8, LANES), jnp.float32)
    for k in range(1, m_ref.shape[0]):
        total, lost = two_sum(total, m_ref[k])
        error = error + lost

    def lane(v, k):
        return jnp.broadcast_to(v[:, k * LANES // 4 : k * LANES // 4 + 1], (8, LANES))

    high = jnp.concatenate([lane(total, 0), lane(total, 2)], axis=0)
    low = jnp.concatenate(
        [lane(error, 0) + lane(total, 1), lane(error, 2) + lane(total, 3)], axis=0
    )
    sol_coord, resid_coord = coordinates(fast_two_sum(high, low))
    sol = [jnp.broadcast_to(sol_coord[k : k + 1], (8, LANES)) for k in range(STEPS)]
    res = [jnp.broadcast_to(resid_coord[k : k + 1], (8, LANES)) for k in range(STEPS + 1)]

    def plane(i, _):
        for t in range(b_ref.shape[1] // 8):
            for half in range(b_ref.shape[2] // LANES):
                at = (i, pl.ds(8 * t, 8), pl.ds(half * LANES, LANES))
                fields = [b_ref[at]] + [f[at] for f in field]
                x, r = sol[0] * fields[0], res[0] * fields[0]
                for k in range(1, STEPS + 1):
                    if k < STEPS:
                        x = x + sol[k] * fields[k]
                    r = r + res[k] * fields[k]
                x_ref[at] = x
                r_ref[at] = r
        return 0

    lax.fori_loop(0, b_ref.shape[0], plane, 0)


def combine(gathered, b, fields):
    return pl.pallas_call(
        combine_kernel,
        out_shape=[jax.ShapeDtypeStruct(b.shape, jnp.float32)] * 2,
        in_specs=[VMEM] * (STEPS + 2),
        out_specs=[VMEM] * 2,
        compiler_params=pltpu.CompilerParams(vmem_limit_bytes=20 * MIB),
    )(gathered, b, *fields)


def on_device(right_side, conduct_half, reaction_half):
    peers = lax.axis_size("wide") * lax.axis_size("narrow")
    *sent, b, c, r = messages(right_side, conduct_half, reaction_half)
    far, near = swapped(sent[1], 1, None), swapped(sent[0], 0, None)
    narrow_halos = [swapped(sent[2 + k], None, k) for k in range(2)]
    state, moments = inner(b, c, r)
    diagonal = corners(narrow_halos, moments)
    diagonal = [swapped(block, k, None) for k, block in enumerate(diagonal)]
    state, moments = onward(border_kernel, b, moments, narrow_halos, state, moments.shape)
    received = [near, far, *diagonal]
    state, moments = onward(outer_kernel, b, moments, received, state, (peers, 8, LANES))
    fields = state[:STEPS]
    gathered = lax.all_to_all(moments, AXES, 0, 0, tiled=True)
    solution, residual = combine(gathered, b, fields)
    return (solution, residual)


def solution(mesh):
    placed = P(("group", "wide"), "narrow", None)
    return jax.shard_map(
        on_device,
        mesh=mesh,
        in_specs=(placed, placed, placed),
        out_specs=(placed, placed),
        check_vma=False,
    )
```

```python
import functools

import jax
import jax.numpy as jnp
from jax import lax
from jax.experimental import pallas as pl
from jax.experimental.pallas import tpu as pltpu
from jax.sharding import PartitionSpec as P

S = 4
OUTER = 2
STEPS = S * OUTER

SCALE = 13.0
CENTER = SCALE
ROOT = SCALE**-0.5

LANES = 128
QUARTER = LANES // 4
AXES = ("wide", "narrow")
VMEM = pl.BlockSpec(memory_space=pltpu.VMEM)
HBM = pl.BlockSpec(memory_space=pltpu.HBM)
MIB = 1024 * 1024


def two_sum(a, b):
    total = a + b
    part = total - a
    return total, (a - (total - part)) + (b - part)


def fast_two_sum(a, b):
    total = a + b
    return total, b - (total - a)


def split(a):
    big = a * 4097.0
    high = big - (big - a)
    return high, a - high


def two_product(a, b):
    product = a * b
    a_high, a_low = split(a)
    b_high, b_low = split(b)
    error = ((a_high * b_high - product) + a_high * b_low + a_low * b_high) + a_low * b_low
    return product, error


def pair_add(a, b):
    total, error = two_sum(a[0], b[0])
    return fast_two_sum(total, error + (a[1] + b[1]))


def pair_scale(a, factor):
    product, error = two_product(a[0], factor)
    return fast_two_sum(product, error + a[1] * factor)


def sides():
    out = []
    for axis in AXES:
        even = lax.rem(lax.axis_index(axis), 2) == 0
        out.append((even, jnp.logical_not(even)))
    return out


def edge_layer(up, count, d):
    return jnp.where(up, count - d, d - 1)


def send_kernel(*refs):
    args, (w_out, n_out), refs = refs[:3], (refs[3:5], refs[5:7]), refs[7:]
    (b_ref, c_ref, r_ref), (pack, done) = refs[:3], refs[3:]
    rows, columns = b_ref.shape[:2]
    h = STEPS
    copies = [pltpu.make_async_copy(args[k], refs[k], done.at[k]) for k in range(3)]
    for copy in copies:
        copy.start()
    for copy in copies:
        copy.wait()
    wide, narrow = sides()
    left = [pl.multiple_of(jnp.where(up, columns - h, 0), 8) for up in narrow]

    def code(i, _):
        pack[i] = r_ref[i].astype(jnp.float32) + c_ref[i].astype(jnp.float32) * (1.0 / 256.0)
        return 0

    def edges(i, _):
        for k, source in enumerate((b_ref, pack)):
            for side in range(2):
                n_out[side][k, i] = source[i, pl.ds(left[side], h), :]
        return 0

    def layers(d, _):
        for a in range(2):
            at = edge_layer(wide[a], rows, d)
            w_out[a][d - 1] = b_ref[at]
            w_out[a][h + d - 1] = pack[at]
        return 0

    lax.fori_loop(0, rows, code, 0)
    lax.fori_loop(0, rows, edges, 0)
    lax.fori_loop(1, h, layers, 0)
    for a in range(2):
        at = edge_layer(wide[a], rows, h)
        w_out[a][h - 1] = c_ref[at].astype(jnp.float32) * ROOT * b_ref[at]


def messages(b, c, r):
    rows, columns, depth = b.shape
    h = STEPS
    shapes = [(2 * h - 1, columns, depth)] * 2 + [(2, rows, h, depth)] * 2
    return pl.pallas_call(
        send_kernel,
        out_shape=[jax.ShapeDtypeStruct(s, jnp.float32) for s in shapes]
        + [pltpu.VMEM(a.shape, a.dtype) for a in (b, c, r)],
        in_specs=[HBM] * 3,
        out_specs=[VMEM] * 7,
        scratch_shapes=[pltpu.VMEM(b.shape, jnp.float32), pltpu.SemaphoreType.DMA((3,))],
        compiler_params=pltpu.CompilerParams(vmem_limit_bytes=16 * MIB),
    )(*[pltpu.with_memory_space_constraint(a, pltpu.HBM) for a in (b, c, r)])


PAIRS = [(d, STEPS - d) for d in range(1, STEPS // 2 + 1)]


def corner_kernel(*refs):
    n_in, c_out = refs[:2], refs[3:]
    rows = n_in[0].shape[1]
    wide, narrow = sides()
    sub = lax.broadcasted_iota(jnp.int32, n_in[0].shape[2:], 0)
    for a in range(2):
        for side in range(2):
            up = narrow[side]
            for p, (d, other) in enumerate(PAIRS):
                shift = jnp.where(up, STEPS - d, d)
                mine = jnp.where(up, sub, STEPS - 1 - sub) < STEPS - d
                for k in range(2):
                    near = n_in[side][k, edge_layer(wide[a], rows, d)]
                    far = n_in[side][k, edge_layer(wide[a], rows, other)]
                    c_out[a][k, p, side] = jnp.where(mine, near, pltpu.roll(far, shift, 0))


def corners(narrow_halos, after):
    depth = narrow_halos[0].shape[-1]
    shape = jax.ShapeDtypeStruct((2, len(PAIRS), 2, STEPS, depth), jnp.float32)
    return pl.pallas_call(
        corner_kernel,
        out_shape=[shape] * 2,
        in_specs=[VMEM] * 3,
        out_specs=[VMEM] * 2,
        compiler_params=pltpu.CompilerParams(vmem_limit_bytes=8 * MIB),
    )(*narrow_halos, after)


def swapped(array, across, along):
    wides, narrows = lax.axis_size("wide"), lax.axis_size("narrow")

    def partner(index, pairing):
        return index if pairing is None else index + (1 if index % 2 == pairing else -1)

    pairs = []
    for w in range(wides):
        for n in range(narrows):
            to_w, to_n = partner(w, across), partner(n, along)
            if 0 <= to_w < wides and 0 <= to_n < narrows:
                pairs.append((w * narrows + n, to_w * narrows + to_n))
    return lax.ppermute(array, AXES, pairs)


def tree(parts):
    while len(parts) > 1:
        parts = [
            parts[k] + parts[k + 1] if k + 1 < len(parts) else parts[k]
            for k in range(0, len(parts), 2)
        ]
    return parts[0]


def place_u(buffer, i, y, value):
    count = value.shape[0]
    for half in range(2):
        buffer[i, half, pl.ds(y + 8, count), :] = value[:, half * LANES : (half + 1) * LANES]


def diagonal_of(conduct, reaction):
    return ((reaction - CENTER) + 6.0 * (conduct * conduct)) * (1.0 / SCALE)


def outside(u_even, diag, coef, i, y, value, packed):
    count = value.shape[0]
    reaction = jnp.floor(packed * 128.0) * (1.0 / 128.0)
    conduct = (packed - reaction) * 256.0
    root = conduct * ROOT
    place_u(u_even, i, y, root * value)
    coef[i, pl.ds(y, count), :] = root * root
    diag[i, pl.ds(y, count), :] = diagonal_of(conduct, reaction)


def advance(step, runs, refs, carry, chosen=None, silent=()):
    b_ref, field, u_even, u_odd, diag, coef = refs
    h = STEPS
    tiles = diag.shape[1] // 8
    lane = lax.broadcasted_iota(jnp.int32, (8, LANES), 1)
    first, last = lane == 0, lane == LANES - 1
    source, target = (u_even, u_odd) if step % 2 else (u_odd, u_even)
    before = b_ref if step == 1 else field[step - 2]
    now = field[step - 1]
    cross, own = [], []
    for t in range(tiles) if chosen is None else chosen:
        edge = t in (0, tiles - 1)
        if edge and step == STEPS:
            continue
        rows = pl.ds(8 * t + 8, 8)
        for start, count, inside in runs:
            layers = [
                [source[start + d, half, rows, :] for half in range(2)]
                for d in range(-1, count + 1)
            ]
            for d in range(count):
                i = start + d
                left, right = layers[d + 1]
                left_up, left_down = pltpu.roll(left, 1, 1), pltpu.roll(left, LANES - 1, 1)
                right_up, right_down = pltpu.roll(right, 1, 1), pltpu.roll(right, LANES - 1, 1)
                along = (
                    jnp.where(first, 0.0, left_up) + jnp.where(last, right_down, left_down),
                    jnp.where(first, left_up, right_up) + jnp.where(last, 0.0, right_down),
                )
                for half in range(2):
                    beside = (
                        source[i, half, pl.ds(8 * t + 7, 8), :]
                        + source[i, half, pl.ds(8 * t + 9, 8), :]
                    )
                    across = layers[d][half] + layers[d + 2][half]
                    around = (beside + across) + along[half]
                    lanes = pl.ds(half * LANES, LANES)
                    at = (i, pl.ds(8 * t, 8), lanes)
                    if inside and not edge:
                        here = (i - h, pl.ds(8 * t - h, 8), lanes)
                        old = before[here]
                        root = coef[at]
                        value = diag[at] * old - root * around
                        now[here] = value
                        if step < STEPS:
                            target[i, half, rows, :] = root * value
                        if t in silent:
                            continue
                        cross.append(value * old)
                        if step < STEPS:
                            own.append(value * value)
                    else:
                        target[i, half, rows, :] = (
                            diag[at] * layers[d + 1][half] - coef[at] * around
                        )
    if not cross:
        return carry
    return carry[0] + tree(cross), (carry[1] + tree(own) if own else carry[1])


def inner_kernel(b_ref, c_ref, r_ref, *refs):
    field, (u_even, u_odd, diag, coef, m_ref) = refs[:STEPS], refs[STEPS:]
    rows, columns, depth = b_ref.shape
    h = STEPS
    everything = (b_ref, field, u_even, u_odd, diag, coef)
    tiles = range(1, columns // 8 + 1)

    def fill(i, total):
        at = i + h
        value = b_ref[i]
        conduct = c_ref[i].astype(jnp.float32)
        root = conduct * ROOT
        place_u(u_even, at, h, root * value)
        coef[at, pl.ds(h, columns), :] = root
        diag[at, pl.ds(h, columns), :] = diagonal_of(conduct, r_ref[i].astype(jnp.float32))
        square = value * value
        return total + tree(
            [
                square[t * 8 : t * 8 + 8, half * LANES : (half + 1) * LANES]
                for t in range(columns // 8)
                for half in range(2)
            ]
        )

    zero = jnp.zeros((8, LANES), jnp.float32)
    m_ref[0] = lax.fori_loop(0, rows, fill, zero)
    for step in range(1, STEPS + 1):
        quads, rest = divmod(max(rows - 2 * step, 0), 4)

        def work(start, count, carry, step=step):
            runs = [(start, count, True)]
            return advance(step, runs, everything, carry, tiles, (tiles[0], tiles[-1]))

        def body(m, carry, step=step, work=work):
            return work(4 * m + h + step, 4, carry)

        carry = lax.fori_loop(0, quads, body, (zero, zero))
        if rest:
            carry = work(h + rows - step - rest, rest, carry)
        m_ref[2 * step - 1] = carry[0]
        if step < STEPS:
            m_ref[2 * step] = carry[1]


def border_kernel(b_ref, m_in, *refs):
    n_in, refs = refs[:2], refs[2 + STEPS + 4 :]
    field, (u_even, u_odd, diag, coef, m_out) = refs[:STEPS], refs[STEPS:]
    rows, columns, depth = b_ref.shape
    h = STEPS
    tiles = columns // 8 + 2
    left = [pl.multiple_of(jnp.where(up, columns + h, 0), 8) for up in sides()[1]]
    everything = (b_ref, field, u_even, u_odd, diag, coef)

    def fill(i, _):
        at = i + h
        for side in range(2):
            outside(u_even, diag, coef, at, left[side], n_in[side][0, i], n_in[side][1, i])
        for y in (0, columns - 8):
            place_u(u_even, at, y + h, coef[at, pl.ds(y + h, 8), :] * b_ref[i, pl.ds(y, 8), :])
        return 0

    lax.fori_loop(0, rows, fill, 0)
    m_out[0] = m_in[0]
    for step in range(1, STEPS + 1):
        source = u_even if step % 2 else u_odd
        before = b_ref if step == 1 else field[step - 2]
        for i in range(step - 1, rows - step + 1):
            for y in (8, columns - 9):
                row = coef[i + h, y + h : y + h + 1, :] * before[i, y : y + 1, :]
                for half in range(2):
                    source[i + h, half, y + h + 8 : y + h + 9, :] = row[
                        :, half * LANES : (half + 1) * LANES
                    ]
        count = max(rows - 2 * step, 0)
        carry = (m_in[2 * step - 1], m_in[2 * step] if step < STEPS else m_in[0])
        for start, part in ((step, count // 2), (step + count // 2, count - count // 2)):
            if part:
                runs = [(start + h, part, True)]
                carry = advance(step, runs, everything, carry, (0, 1, tiles - 2, tiles - 1))
        m_out[2 * step - 1] = carry[0]
        if step < STEPS:
            m_out[2 * step] = carry[1]


def outer_kernel(pairing, b_ref, m_in, *refs):
    (w_in, c_in), refs = refs[:2], refs[2 + STEPS + 4 :]
    field, (u_even, u_odd, diag, coef, m_out) = refs[:STEPS], refs[STEPS:]
    rows, columns, depth = b_ref.shape
    h = STEPS
    wide, narrow = sides()
    up = wide[pairing]
    left = [pl.multiple_of(jnp.where(side, columns + h, 0), 8) for side in narrow]
    everything = (b_ref, field, u_even, u_odd, diag, coef)

    def halo_layer(d):
        return jnp.where(up, rows + h - 1 + d, h - d)

    def fill(d, _):
        outside(u_even, diag, coef, halo_layer(d), h, w_in[d - 1], w_in[h + d - 1])
        return 0

    lax.fori_loop(1, h, fill, 0)
    place_u(u_even, halo_layer(h), h, w_in[h - 1])
    for side in range(2):
        for p, (d, other) in enumerate(PAIRS):
            near = [c_in[k, p, side] for k in range(2)]
            outside(u_even, diag, coef, halo_layer(d), left[side], *near)
            if other != d:
                shift = jnp.where(narrow[side], d, h - d)
                far = [pltpu.roll(block, shift, 0) for block in near]
                outside(u_even, diag, coef, halo_layer(other), left[side], *far)

    zero = jnp.zeros((8, LANES), jnp.float32)
    moments = [m_in[0]]
    for step in range(1, STEPS + 1):
        carry = (m_in[2 * step - 1], m_in[2 * step] if step < STEPS else zero)
        runs = [(jnp.where(up, rows + h - step, h), step, True)]
        if step < STEPS:
            runs.append((jnp.where(up, rows + h, step), h - step, False))
        carry = advance(step, runs, everything, carry)
        moments += carry if step < STEPS else carry[:1]
    if pairing == 0:
        for k, moment in enumerate(moments):
            m_out[k] = moment
        return

    def folded(high, low, shift, axis):
        total, error = two_sum(high, pltpu.roll(high, shift, axis))
        return total, (low + pltpu.roll(low, shift, axis)) + error

    sublane = lax.broadcasted_iota(jnp.int32, (8, LANES), 0)
    lane = lax.broadcasted_iota(jnp.int32, (8, LANES), 1)
    packed = []
    for group in range(2):
        highs, lows = zero, zero
        for k in range(8):
            high, low = moments[group * 8 + k], zero
            for shift in (4, 2, 1):
                high, low = folded(high, low, shift, 0)
            highs = jnp.where(sublane == k, high, highs)
            lows = jnp.where(sublane == k, low, lows)
        for shift in (64, 32, 16, 8, 4, 2, 1):
            highs, lows = folded(highs, lows, shift, 1)
        packed += [highs, lows]
    message = jnp.where(
        lane < QUARTER,
        packed[0],
        jnp.where(lane < 2 * QUARTER, packed[1], jnp.where(lane < 3 * QUARTER, packed[2], packed[3])),
    )
    for k in range(m_out.shape[0]):
        m_out[k] = message


def summed(m_ref):
    total, error = m_ref[0], jnp.zeros((8, LANES), jnp.float32)
    for k in range(1, m_ref.shape[0]):
        total, lost = two_sum(total, m_ref[k])
        error = error + lost
    return total, error


def relay_kernel(m_ref, out_ref):
    total, error = summed(m_ref)
    lane = lax.broadcasted_iota(jnp.int32, (8, LANES), 1)
    low = lax.rem(lane // QUARTER, 2) == 1
    message = total + jnp.where(low, pltpu.roll(error, QUARTER, 1), 0.0)
    for k in range(out_ref.shape[0]):
        out_ref[k] = message


def gather(message):
    over_wide = lax.all_to_all(message, "wide", 0, 0, tiled=True)
    shape = (lax.axis_size("narrow"), 8, LANES)
    relayed = pl.pallas_call(
        relay_kernel,
        out_shape=jax.ShapeDtypeStruct(shape, jnp.float32),
        in_specs=[VMEM],
        out_specs=VMEM,
    )(over_wide)
    return lax.all_to_all(relayed, "narrow", 0, 0, tiled=True)


def state_shapes(b):
    rows, columns, depth = b.shape
    wide, narrow = rows + 2 * STEPS, columns + 2 * STEPS
    shapes = [b.shape] * STEPS + [(wide, 2, narrow + 16, LANES)] * 2 + [(wide, narrow, depth)] * 2
    return [pltpu.VMEM(s, jnp.float32) for s in shapes]


def inner(b, c, r):
    shapes = state_shapes(b) + [jax.ShapeDtypeStruct((2 * STEPS, 8, LANES), jnp.float32)]
    *state, moments = pl.pallas_call(
        inner_kernel,
        cost_estimate=pl.CostEstimate(
            flops=120 * b.size, bytes_accessed=24 * b.size, transcendentals=0
        ),
        out_shape=shapes,
        in_specs=[VMEM] * 3,
        out_specs=[VMEM] * len(shapes),
        compiler_params=pltpu.CompilerParams(vmem_limit_bytes=26 * MIB),
    )(b, c, r)
    return state, moments


def onward(kernel, b, moments, received, state, moments_shape):
    shapes = state_shapes(b) + [jax.ShapeDtypeStruct(moments_shape, jnp.float32)]
    others = 2 + len(received)
    *state, moments = pl.pallas_call(
        kernel,
        out_shape=shapes,
        in_specs=[VMEM] * (others + len(state)),
        out_specs=[VMEM] * len(shapes),
        input_output_aliases={others + k: k for k in range(len(state))},
        compiler_params=pltpu.CompilerParams(vmem_limit_bytes=26 * MIB),
    )(b, moments, *received, *state)
    return state, moments


def coordinates(moment):
    shape = moment[0].shape
    count = shape[0]
    row = lax.broadcasted_iota(jnp.int32, shape, 0)

    def later(v):
        return jnp.where(row == count - 1, 0.0, pltpu.roll(v, count - 1, 0))

    def raised(v):
        return jnp.where(row == 0, 0.0, pltpu.roll(v, 1, 0))

    def spread(v):
        return jnp.broadcast_to(v, shape)

    residual = search = moment
    resid_coord = jnp.where(row == 0, 1.0, 0.0)
    search_coord = resid_coord
    sol_coord = jnp.zeros(shape, jnp.float32)
    for i in range(STEPS):
        mapped = pair_add((later(search[0]), later(search[1])), search)
        old = residual[0][i : i + 1]
        length = old / mapped[0][i : i + 1]
        lengths = spread(length)
        residual = pair_add(residual, pair_scale(mapped, -lengths))
        grown = spread(-length * residual[0][i + 1 : i + 2] / old)
        search = pair_add(residual, pair_scale(search, grown))
        sol_coord = sol_coord + (lengths * (1.0 / SCALE)) * search_coord
        resid_coord = resid_coord - lengths * (raised(search_coord) + search_coord)
        search_coord = resid_coord + grown * search_coord
    return sol_coord, resid_coord


def combine_kernel(m_ref, b_ref, *refs):
    field, (x_ref, r_ref) = refs[:STEPS], refs[STEPS:]
    total, error = summed(m_ref)

    def lane(v, k):
        return jnp.broadcast_to(v[:, k * QUARTER : k * QUARTER + 1], (8, LANES))

    high = jnp.concatenate([lane(total, 0), lane(total, 2)], axis=0)
    low = jnp.concatenate(
        [lane(error, 0) + lane(total, 1), lane(error, 2) + lane(total, 3)], axis=0
    )
    sol_coord, resid_coord = coordinates(fast_two_sum(high, low))
    sol = [jnp.broadcast_to(sol_coord[k : k + 1], (8, LANES)) for k in range(STEPS)]
    res = [jnp.broadcast_to(resid_coord[k : k + 1], (8, LANES)) for k in range(STEPS + 1)]

    def plane(i, _):
        for t in range(b_ref.shape[1] // 8):
            for half in range(b_ref.shape[2] // LANES):
                at = (i, pl.ds(8 * t, 8), pl.ds(half * LANES, LANES))
                fields = [b_ref[at]] + [f[at] for f in field]
                x, r = sol[0] * fields[0], res[0] * fields[0]
                for k in range(1, STEPS + 1):
                    if k < STEPS:
                        x = x + sol[k] * fields[k]
                    r = r + res[k] * fields[k]
                x_ref[at] = x
                r_ref[at] = r
        return 0

    lax.fori_loop(0, b_ref.shape[0], plane, 0)


def combine(gathered, b, fields):
    return pl.pallas_call(
        combine_kernel,
        out_shape=[jax.ShapeDtypeStruct(b.shape, jnp.float32)] * 2,
        in_specs=[VMEM] * (STEPS + 2),
        out_specs=[VMEM] * 2,
        compiler_params=pltpu.CompilerParams(vmem_limit_bytes=20 * MIB),
    )(gathered, b, *fields)


def on_device(right_side, conduct_half, reaction_half):
    *sent, b, c, r = messages(right_side, conduct_half, reaction_half)
    far, near = swapped(sent[1], 1, None), swapped(sent[0], 0, None)
    narrow_halos = [swapped(sent[2 + k], None, k) for k in range(2)]
    state, moments = inner(b, c, r)
    diagonal = corners(narrow_halos, moments)
    diagonal = [swapped(block, k, None) for k, block in enumerate(diagonal)]
    state, moments = onward(border_kernel, b, moments, narrow_halos, state, moments.shape)
    for pairing, received in enumerate(([near, diagonal[0]], [far, diagonal[1]])):
        shape = (lax.axis_size("wide"), 8, LANES) if pairing else moments.shape
        kernel = functools.partial(outer_kernel, pairing)
        state, moments = onward(kernel, b, moments, received, state, shape)
    gathered, fields = gather(moments), state[:STEPS]
    solution, residual = combine(gathered, b, fields)
    return (solution, residual)


def solution(mesh):
    placed = P(("group", "wide"), "narrow", None)
    return jax.shard_map(
        on_device,
        mesh=mesh,
        in_specs=(placed, placed, placed),
        out_specs=(placed, placed),
        check_vma=False,
    )
```

```python
import functools

import jax
import jax.numpy as jnp
from jax import lax
from jax.experimental import pallas as pl
from jax.experimental.pallas import tpu as pltpu
from jax.sharding import PartitionSpec as P

S = 4
OUTER = 2
STEPS = S * OUTER

SCALE = 13.0
CENTER = SCALE
ROOT = SCALE**-0.5

LANES = 128
QUARTER = LANES // 4
CHUNKS = 4
AXES = ("wide", "narrow")
VMEM = pl.BlockSpec(memory_space=pltpu.VMEM)
HBM = pl.BlockSpec(memory_space=pltpu.HBM)
MIB = 1024 * 1024


def two_sum(a, b):
    total = a + b
    part = total - a
    return total, (a - (total - part)) + (b - part)


def fast_two_sum(a, b):
    total = a + b
    return total, b - (total - a)


def split(a):
    big = a * 4097.0
    high = big - (big - a)
    return high, a - high


def two_product(a, b):
    product = a * b
    a_high, a_low = split(a)
    b_high, b_low = split(b)
    error = ((a_high * b_high - product) + a_high * b_low + a_low * b_high) + a_low * b_low
    return product, error


def pair_add(a, b):
    total, error = two_sum(a[0], b[0])
    return fast_two_sum(total, error + (a[1] + b[1]))


def loose_scale(a, factor):
    product, error = two_product(a[0], factor)
    return product, error + a[1] * factor


def sides():
    out = []
    for axis in AXES:
        even = lax.rem(lax.axis_index(axis), 2) == 0
        out.append((even, jnp.logical_not(even)))
    return out


def edge_layer(up, count, d):
    return jnp.where(up, count - d, d - 1)


def send_kernel(*refs):
    args, (w_out, n_out), refs = refs[:3], (refs[3:5], refs[5:7]), refs[7:]
    (b_ref, c_ref, r_ref), (pack, done) = refs[:3], refs[3:]
    rows, columns = b_ref.shape[:2]
    h = STEPS
    copies = [pltpu.make_async_copy(args[k], refs[k], done.at[k]) for k in (1, 2, 0)]
    for copy in copies:
        copy.start()
    wide, narrow = sides()
    left = [pl.multiple_of(jnp.where(up, columns - h, 0), 8) for up in narrow]

    def code(i, _):
        pack[i] = r_ref[i].astype(jnp.float32) + c_ref[i].astype(jnp.float32) * (1.0 / 256.0)
        return 0

    def edges(i, _):
        for k, source in enumerate((b_ref, pack)):
            for side in range(2):
                n_out[side][k, i] = source[i, pl.ds(left[side], h), :]
        return 0

    def layers(d, _):
        for a in range(2):
            at = edge_layer(wide[a], rows, d)
            w_out[a][d - 1] = b_ref[at]
            w_out[a][h + d - 1] = pack[at]
        return 0

    copies[0].wait()
    copies[1].wait()
    lax.fori_loop(0, rows, code, 0, unroll=2)
    copies[2].wait()
    lax.fori_loop(0, rows, edges, 0, unroll=4)
    lax.fori_loop(1, h, layers, 0)
    for a in range(2):
        at = edge_layer(wide[a], rows, h)
        w_out[a][h - 1] = c_ref[at].astype(jnp.float32) * ROOT * b_ref[at]


def messages(b, c, r):
    rows, columns, depth = b.shape
    h = STEPS
    shapes = [(2 * h - 1, columns, depth)] * 2 + [(2, rows, h, depth)] * 2
    return pl.pallas_call(
        send_kernel,
        out_shape=[jax.ShapeDtypeStruct(s, jnp.float32) for s in shapes]
        + [pltpu.VMEM(a.shape, a.dtype) for a in (b, c, r)],
        in_specs=[HBM] * 3,
        out_specs=[VMEM] * 7,
        scratch_shapes=[pltpu.VMEM(b.shape, jnp.float32), pltpu.SemaphoreType.DMA((3,))],
        compiler_params=pltpu.CompilerParams(vmem_limit_bytes=16 * MIB),
    )(*[pltpu.with_memory_space_constraint(a, pltpu.HBM) for a in (b, c, r)])


PAIRS = [(d, STEPS - d) for d in range(1, STEPS // 2 + 1)]


def corner_kernel(*refs):
    n_in, c_out = refs[:2], refs[3:]
    rows = n_in[0].shape[1]
    wide, narrow = sides()
    sub = lax.broadcasted_iota(jnp.int32, n_in[0].shape[2:], 0)
    for a in range(2):
        for side in range(2):
            up = narrow[side]
            for p, (d, other) in enumerate(PAIRS):
                shift = jnp.where(up, STEPS - d, d)
                mine = jnp.where(up, sub, STEPS - 1 - sub) < STEPS - d
                for k in range(2):
                    near = n_in[side][k, edge_layer(wide[a], rows, d)]
                    far = n_in[side][k, edge_layer(wide[a], rows, other)]
                    c_out[a][k, p, side] = jnp.where(mine, near, pltpu.roll(far, shift, 0))


def corners(narrow_halos, after):
    depth = narrow_halos[0].shape[-1]
    shape = jax.ShapeDtypeStruct((2, len(PAIRS), 2, STEPS, depth), jnp.float32)
    return pl.pallas_call(
        corner_kernel,
        out_shape=[shape] * 2,
        in_specs=[VMEM] * 3,
        out_specs=[VMEM] * 2,
        compiler_params=pltpu.CompilerParams(vmem_limit_bytes=8 * MIB),
    )(*narrow_halos, after)


def swapped(array, across, along):
    wides, narrows = lax.axis_size("wide"), lax.axis_size("narrow")

    def partner(index, pairing):
        return index if pairing is None else index + (1 if index % 2 == pairing else -1)

    pairs = []
    for w in range(wides):
        for n in range(narrows):
            to_w, to_n = partner(w, across), partner(n, along)
            if 0 <= to_w < wides and 0 <= to_n < narrows:
                pairs.append((w * narrows + n, to_w * narrows + to_n))
    return lax.ppermute(array, AXES, pairs)


def tree(parts):
    while len(parts) > 1:
        parts = [
            parts[k] + parts[k + 1] if k + 1 < len(parts) else parts[k]
            for k in range(0, len(parts), 2)
        ]
    return parts[0]


def place_u(buffer, i, y, value):
    count = value.shape[0]
    for half in range(2):
        buffer[i, half, pl.ds(y + 8, count), :] = value[:, half * LANES : (half + 1) * LANES]


def diagonal_of(conduct, reaction):
    return ((reaction - CENTER) + 6.0 * (conduct * conduct)) * (1.0 / SCALE)


def outside(u_even, diag, coef, i, y, value, packed):
    count = value.shape[0]
    reaction = jnp.floor(packed * 128.0) * (1.0 / 128.0)
    conduct = (packed - reaction) * 256.0
    root = conduct * ROOT
    place_u(u_even, i, y, root * value)
    coef[i, pl.ds(y, count), :] = root * root
    diag[i, pl.ds(y, count), :] = diagonal_of(conduct, reaction)


def advance(step, runs, refs, carry, chosen=None, silent=()):
    b_ref, field, u_even, u_odd, diag, coef = refs
    h = STEPS
    tiles = diag.shape[1] // 8
    lane = lax.broadcasted_iota(jnp.int32, (8, LANES), 1)
    first, last = lane == 0, lane == LANES - 1
    source, target = (u_even, u_odd) if step % 2 else (u_odd, u_even)
    before = b_ref if step == 1 else field[step - 2]
    now = field[step - 1]
    cross, own = [], []
    for t in range(tiles) if chosen is None else chosen:
        edge = t in (0, tiles - 1)
        if edge and step == STEPS:
            continue
        rows = pl.ds(8 * t + 8, 8)
        for start, count, inside in runs:
            layers = [
                [source[start + d, half, rows, :] for half in range(2)]
                for d in range(-1, count + 1)
            ]
            for d in range(count):
                i = start + d
                left, right = layers[d + 1]
                left_up, left_down = pltpu.roll(left, 1, 1), pltpu.roll(left, LANES - 1, 1)
                right_up, right_down = pltpu.roll(right, 1, 1), pltpu.roll(right, LANES - 1, 1)
                along = (
                    jnp.where(first, 0.0, left_up) + jnp.where(last, right_down, left_down),
                    jnp.where(first, left_up, right_up) + jnp.where(last, 0.0, right_down),
                )
                for half in range(2):
                    beside = (
                        source[i, half, pl.ds(8 * t + 7, 8), :]
                        + source[i, half, pl.ds(8 * t + 9, 8), :]
                    )
                    across = layers[d][half] + layers[d + 2][half]
                    around = (beside + across) + along[half]
                    lanes = pl.ds(half * LANES, LANES)
                    at = (i, pl.ds(8 * t, 8), lanes)
                    if inside and not edge:
                        here = (i - h, pl.ds(8 * t - h, 8), lanes)
                        old = before[here]
                        root = coef[at]
                        value = diag[at] * old - root * around
                        now[here] = value
                        if step < STEPS:
                            target[i, half, rows, :] = root * value
                        if t in silent:
                            continue
                        cross.append(value * old)
                        if step < STEPS:
                            own.append(value * value)
                    else:
                        target[i, half, rows, :] = (
                            diag[at] * layers[d + 1][half] - coef[at] * around
                        )
    if not cross:
        return carry
    return carry[0] + tree(cross), (carry[1] + tree(own) if own else carry[1])


def inner_kernel(b_ref, c_ref, r_ref, *refs):
    field, (u_even, u_odd, diag, coef, m_ref) = refs[:STEPS], refs[STEPS:]
    rows, columns, depth = b_ref.shape
    h = STEPS
    everything = (b_ref, field, u_even, u_odd, diag, coef)
    tiles = range(1, columns // 8 + 1)

    def fill(i, total):
        at = i + h
        value = b_ref[i]
        conduct = c_ref[i].astype(jnp.float32)
        root = conduct * ROOT
        place_u(u_even, at, h, root * value)
        coef[at, pl.ds(h, columns), :] = root
        diag[at, pl.ds(h, columns), :] = diagonal_of(conduct, r_ref[i].astype(jnp.float32))
        square = value * value
        return total + tree(
            [
                square[t * 8 : t * 8 + 8, half * LANES : (half + 1) * LANES]
                for t in range(columns // 8)
                for half in range(2)
            ]
        )

    zero = jnp.zeros((8, LANES), jnp.float32)
    m_ref[0] = lax.fori_loop(0, rows, fill, zero)
    for step in range(1, STEPS + 1):
        quads, rest = divmod(max(rows - 2 * step, 0), 4)

        def work(start, count, carry, step=step):
            runs = [(start, count, True)]
            return advance(step, runs, everything, carry, tiles, (tiles[0], tiles[-1]))

        def body(m, carry, step=step, work=work):
            return work(4 * m + h + step, 4, carry)

        carry = lax.fori_loop(0, quads, body, (zero, zero))
        if rest:
            carry = work(h + rows - step - rest, rest, carry)
        m_ref[2 * step - 1] = carry[0]
        if step < STEPS:
            m_ref[2 * step] = carry[1]


def border_kernel(b_ref, m_in, *refs):
    n_in, refs = refs[:2], refs[2 + STEPS + 4 :]
    field, (u_even, u_odd, diag, coef, m_out) = refs[:STEPS], refs[STEPS:]
    rows, columns, depth = b_ref.shape
    h = STEPS
    tiles = columns // 8 + 2
    left = [pl.multiple_of(jnp.where(up, columns + h, 0), 8) for up in sides()[1]]
    everything = (b_ref, field, u_even, u_odd, diag, coef)

    def fill(i, _):
        at = i + h
        for side in range(2):
            outside(u_even, diag, coef, at, left[side], n_in[side][0, i], n_in[side][1, i])
        for y in (0, columns - 8):
            place_u(u_even, at, y + h, coef[at, pl.ds(y + h, 8), :] * b_ref[i, pl.ds(y, 8), :])
        return 0

    lax.fori_loop(0, rows, fill, 0)
    m_out[0] = m_in[0]
    for step in range(1, STEPS + 1):
        source = u_even if step % 2 else u_odd
        before = b_ref if step == 1 else field[step - 2]
        for i in range(step - 1, rows - step + 1):
            for y in (8, columns - 9):
                row = coef[i + h, y + h : y + h + 1, :] * before[i, y : y + 1, :]
                for half in range(2):
                    source[i + h, half, y + h + 8 : y + h + 9, :] = row[
                        :, half * LANES : (half + 1) * LANES
                    ]
        count = max(rows - 2 * step, 0)
        carry = (m_in[2 * step - 1], m_in[2 * step] if step < STEPS else m_in[0])
        for start, part in ((step, count // 2), (step + count // 2, count - count // 2)):
            if part:
                runs = [(start + h, part, True)]
                carry = advance(step, runs, everything, carry, (0, 1, tiles - 2, tiles - 1))
        m_out[2 * step - 1] = carry[0]
        if step < STEPS:
            m_out[2 * step] = carry[1]


def outer_kernel(pairing, b_ref, m_in, *refs):
    (w_in, c_in), refs = refs[:2], refs[2 + STEPS + 4 :]
    field, (u_even, u_odd, diag, coef, m_out) = refs[:STEPS], refs[STEPS:]
    rows, columns, depth = b_ref.shape
    h = STEPS
    wide, narrow = sides()
    up = wide[pairing]
    left = [pl.multiple_of(jnp.where(side, columns + h, 0), 8) for side in narrow]
    everything = (b_ref, field, u_even, u_odd, diag, coef)

    def halo_layer(d):
        return jnp.where(up, rows + h - 1 + d, h - d)

    def fill(d, _):
        outside(u_even, diag, coef, halo_layer(d), h, w_in[d - 1], w_in[h + d - 1])
        return 0

    lax.fori_loop(1, h, fill, 0)
    place_u(u_even, halo_layer(h), h, w_in[h - 1])
    for side in range(2):
        for p, (d, other) in enumerate(PAIRS):
            near = [c_in[k, p, side] for k in range(2)]
            outside(u_even, diag, coef, halo_layer(d), left[side], *near)
            if other != d:
                shift = jnp.where(narrow[side], d, h - d)
                far = [pltpu.roll(block, shift, 0) for block in near]
                outside(u_even, diag, coef, halo_layer(other), left[side], *far)

    zero = jnp.zeros((8, LANES), jnp.float32)
    moments = [m_in[0]]
    for step in range(1, STEPS + 1):
        carry = (m_in[2 * step - 1], m_in[2 * step] if step < STEPS else zero)
        runs = [(jnp.where(up, rows + h - step, h), step, True)]
        if step < STEPS:
            runs.append((jnp.where(up, rows + h, step), h - step, False))
        carry = advance(step, runs, everything, carry)
        moments += carry if step < STEPS else carry[:1]
    if pairing == 0:
        for k, moment in enumerate(moments):
            m_out[k] = moment
        return

    def folded(high, low, shift, axis):
        total, error = two_sum(high, pltpu.roll(high, shift, axis))
        return total, (low + pltpu.roll(low, shift, axis)) + error

    sublane = lax.broadcasted_iota(jnp.int32, (8, LANES), 0)
    lane = lax.broadcasted_iota(jnp.int32, (8, LANES), 1)
    packed = []
    for group in range(2):
        highs, lows = zero, zero
        for k in range(8):
            high, low = moments[group * 8 + k], zero
            for shift in (4, 2, 1):
                high, low = folded(high, low, shift, 0)
            highs = jnp.where(sublane == k, high, highs)
            lows = jnp.where(sublane == k, low, lows)
        for shift in (64, 32, 16, 8, 4, 2, 1):
            highs, lows = folded(highs, lows, shift, 1)
        packed += [highs, lows]
    message = jnp.where(
        lane < QUARTER,
        packed[0],
        jnp.where(lane < 2 * QUARTER, packed[1], jnp.where(lane < 3 * QUARTER, packed[2], packed[3])),
    )
    for k in range(m_out.shape[0]):
        m_out[k] = message


def summed(m_ref):
    total, error = m_ref[0], jnp.zeros((8, LANES), jnp.float32)
    for k in range(1, m_ref.shape[0]):
        total, lost = two_sum(total, m_ref[k])
        error = error + lost
    return total, error


def state_shapes(b):
    rows, columns, depth = b.shape
    wide, narrow = rows + 2 * STEPS, columns + 2 * STEPS
    shapes = [b.shape] * STEPS + [(wide, 2, narrow + 16, LANES)] * 2 + [(wide, narrow, depth)] * 2
    return [pltpu.VMEM(s, jnp.float32) for s in shapes]


def inner(b, c, r):
    shapes = state_shapes(b) + [jax.ShapeDtypeStruct((2 * STEPS, 8, LANES), jnp.float32)]
    *state, moments = pl.pallas_call(
        inner_kernel,
        cost_estimate=pl.CostEstimate(
            flops=120 * b.size, bytes_accessed=24 * b.size, transcendentals=0
        ),
        out_shape=shapes,
        in_specs=[VMEM] * 3,
        out_specs=[VMEM] * len(shapes),
        compiler_params=pltpu.CompilerParams(vmem_limit_bytes=26 * MIB),
    )(b, c, r)
    return state, moments


def onward(kernel, b, moments, received, state, moments_shape):
    shapes = state_shapes(b) + [jax.ShapeDtypeStruct(moments_shape, jnp.float32)]
    others = 2 + len(received)
    *state, moments = pl.pallas_call(
        kernel,
        out_shape=shapes,
        in_specs=[VMEM] * (others + len(state)),
        out_specs=[VMEM] * len(shapes),
        input_output_aliases={others + k: k for k in range(len(state))},
        compiler_params=pltpu.CompilerParams(vmem_limit_bytes=26 * MIB),
    )(b, moments, *received, *state)
    return state, moments


def coordinates(moment):
    shape = moment[0].shape
    count = shape[0]
    row = lax.broadcasted_iota(jnp.int32, shape, 0)

    def later(v):
        return jnp.where(row == count - 1, 0.0, pltpu.roll(v, count - 1, 0))

    def raised(v):
        return jnp.where(row == 0, 0.0, pltpu.roll(v, 1, 0))

    def spread(v):
        return jnp.broadcast_to(v, shape)

    residual = search = moment
    resid_coord = jnp.where(row == 0, 1.0, 0.0)
    search_coord = resid_coord
    sol_coord = jnp.zeros(shape, jnp.float32)
    for i in range(STEPS):
        mapped, lost = two_sum(later(search[0]), search[0])
        lost = lost + (later(search[1]) + search[1])
        old = residual[0][i : i + 1]
        inverse = 1.0 / old
        length = old / mapped[i : i + 1]
        lengths = spread(length)
        residual = pair_add(residual, loose_scale((mapped, lost), -lengths))
        grown = spread(-length * inverse * residual[0][i + 1 : i + 2])
        search = pair_add(residual, loose_scale(search, grown))
        sol_coord = sol_coord + (lengths * (1.0 / SCALE)) * search_coord
        resid_coord = resid_coord - lengths * (raised(search_coord) + search_coord)
        search_coord = resid_coord + grown * search_coord
    return sol_coord, resid_coord


def combine_kernel(m_ref, b_ref, *refs):
    field, outs, (x_ref, r_ref, done) = refs[:STEPS], refs[STEPS : STEPS + 2], refs[STEPS + 2 :]
    rows = b_ref.shape[0]
    total, error = summed(m_ref)

    def lane(v, k):
        return jnp.broadcast_to(v[:, k * QUARTER : k * QUARTER + 1], (8, LANES))

    high = jnp.concatenate([lane(total, 0), lane(total, 2)], axis=0)
    low = jnp.concatenate(
        [lane(error, 0) + lane(total, 1), lane(error, 2) + lane(total, 3)], axis=0
    )
    sol_coord, resid_coord = coordinates(fast_two_sum(high, low))
    sol = [jnp.broadcast_to(sol_coord[k : k + 1], (8, LANES)) for k in range(STEPS)]
    res = [jnp.broadcast_to(resid_coord[k : k + 1], (8, LANES)) for k in range(STEPS + 1)]

    def plane(i, _):
        for t in range(b_ref.shape[1] // 8):
            for half in range(b_ref.shape[2] // LANES):
                at = (i, pl.ds(8 * t, 8), pl.ds(half * LANES, LANES))
                fields = [b_ref[at]] + [f[at] for f in field]
                x, r = sol[0] * fields[0], res[0] * fields[0]
                for k in range(1, STEPS + 1):
                    if k < STEPS:
                        x = x + sol[k] * fields[k]
                    r = r + res[k] * fields[k]
                x_ref[at] = x
                r_ref[at] = r
        return 0

    copies = []
    for chunk in range(CHUNKS):
        part = pl.ds(chunk * rows // CHUNKS, rows // CHUNKS)
        lax.fori_loop(part.start, part.start + part.size, plane, 0)
        for k, source in enumerate((x_ref, r_ref)):
            copies.append(
                pltpu.make_async_copy(source.at[part], outs[k].at[part], done.at[k, chunk])
            )
            copies[-1].start()
    for copy in copies:
        copy.wait()


def combine(gathered, b, fields):
    return pl.pallas_call(
        combine_kernel,
        out_shape=[jax.ShapeDtypeStruct(b.shape, jnp.float32)] * 2,
        in_specs=[VMEM] * (STEPS + 2),
        out_specs=[HBM] * 2,
        scratch_shapes=[pltpu.VMEM(b.shape, jnp.float32)] * 2
        + [pltpu.SemaphoreType.DMA((2, CHUNKS))],
        compiler_params=pltpu.CompilerParams(vmem_limit_bytes=20 * MIB),
    )(gathered, b, *fields)


def on_device(right_side, conduct_half, reaction_half):
    peers = lax.axis_size("wide") * lax.axis_size("narrow")
    *sent, b, c, r = messages(right_side, conduct_half, reaction_half)
    far, near = swapped(sent[1], 1, None), swapped(sent[0], 0, None)
    narrow_halos = [swapped(sent[2 + k], None, k) for k in range(2)]
    state, moments = inner(b, c, r)
    diagonal = corners(narrow_halos, moments)
    diagonal = [swapped(block, k, None) for k, block in enumerate(diagonal)]
    state, moments = onward(border_kernel, b, moments, narrow_halos, state, moments.shape)
    for pairing, received in enumerate(([near, diagonal[0]], [far, diagonal[1]])):
        shape = (peers, 8, LANES) if pairing else moments.shape
        kernel = functools.partial(outer_kernel, pairing)
        state, moments = onward(kernel, b, moments, received, state, shape)
    gathered, fields = lax.all_to_all(moments, AXES, 0, 0, tiled=True), state[:STEPS]
    solution, residual = combine(gathered, b, fields)
    return (solution, residual)


def solution(mesh):
    placed = P(("group", "wide"), "narrow", None)
    return jax.shard_map(
        on_device,
        mesh=mesh,
        in_specs=(placed, placed, placed),
        out_specs=(placed, placed),
        check_vma=False,
    )
```

```python
import functools

import jax
import jax.numpy as jnp
from jax import lax
from jax.experimental import pallas as pl
from jax.experimental.pallas import tpu as pltpu
from jax.sharding import PartitionSpec as P

S = 4
OUTER = 2
STEPS = S * OUTER

SCALE = 13.0
CENTER = SCALE
ROOT = SCALE**-0.5

LANES = 128
QUARTER = LANES // 4
CHUNKS = 4
AXES = ("wide", "narrow")
VMEM = pl.BlockSpec(memory_space=pltpu.VMEM)
HBM = pl.BlockSpec(memory_space=pltpu.HBM)
MIB = 1024 * 1024


def two_sum(a, b):
    total = a + b
    part = total - a
    return total, (a - (total - part)) + (b - part)


def fast_two_sum(a, b):
    total = a + b
    return total, b - (total - a)


def split(a):
    big = a * 4097.0
    high = big - (big - a)
    return high, a - high


def two_product(a, b):
    product = a * b
    a_high, a_low = split(a)
    b_high, b_low = split(b)
    error = ((a_high * b_high - product) + a_high * b_low + a_low * b_high) + a_low * b_low
    return product, error


def pair_add(a, b):
    total, error = two_sum(a[0], b[0])
    return fast_two_sum(total, error + (a[1] + b[1]))


def loose_scale(a, factor):
    product, error = two_product(a[0], factor)
    return product, error + a[1] * factor


def sides():
    out = []
    for axis in AXES:
        even = lax.rem(lax.axis_index(axis), 2) == 0
        out.append((even, jnp.logical_not(even)))
    return out


def edge_layer(up, count, d):
    return jnp.where(up, count - d, d - 1)


def send_kernel(*refs):
    args, (w_out, n_out), refs = refs[:3], (refs[3:5], refs[5:7]), refs[7:]
    (b_ref, c_ref, r_ref), (pack, done) = refs[:3], refs[3:]
    rows, columns = b_ref.shape[:2]
    h = STEPS
    copies = [pltpu.make_async_copy(args[k], refs[k], done.at[k]) for k in (1, 2, 0)]
    for copy in copies:
        copy.start()
    wide, narrow = sides()
    left = [pl.multiple_of(jnp.where(up, columns - h, 0), 8) for up in narrow]

    def code(i, _):
        pack[i] = r_ref[i].astype(jnp.float32) + c_ref[i].astype(jnp.float32) * (1.0 / 256.0)
        return 0

    def edges(i, _):
        for k, source in enumerate((b_ref, pack)):
            for side in range(2):
                n_out[side][k, i] = source[i, pl.ds(left[side], h), :]
        return 0

    def layers(d, _):
        for a in range(2):
            at = edge_layer(wide[a], rows, d)
            w_out[a][d - 1] = b_ref[at]
            w_out[a][h + d - 1] = pack[at]
        return 0

    copies[0].wait()
    copies[1].wait()
    lax.fori_loop(0, rows, code, 0, unroll=2)
    copies[2].wait()
    lax.fori_loop(0, rows, edges, 0, unroll=4)
    lax.fori_loop(1, h, layers, 0)
    for a in range(2):
        at = edge_layer(wide[a], rows, h)
        w_out[a][h - 1] = c_ref[at].astype(jnp.float32) * ROOT * b_ref[at]


def messages(b, c, r):
    rows, columns, depth = b.shape
    h = STEPS
    shapes = [(2 * h - 1, columns, depth)] * 2 + [(2, rows, h, depth)] * 2
    return pl.pallas_call(
        send_kernel,
        out_shape=[jax.ShapeDtypeStruct(s, jnp.float32) for s in shapes]
        + [pltpu.VMEM(a.shape, a.dtype) for a in (b, c, r)],
        in_specs=[HBM] * 3,
        out_specs=[VMEM] * 7,
        scratch_shapes=[pltpu.VMEM(b.shape, jnp.float32), pltpu.SemaphoreType.DMA((3,))],
        compiler_params=pltpu.CompilerParams(vmem_limit_bytes=16 * MIB),
    )(*[pltpu.with_memory_space_constraint(a, pltpu.HBM) for a in (b, c, r)])


PAIRS = [(d, STEPS - d) for d in range(1, STEPS // 2 + 1)]


def corner_kernel(*refs):
    n_in, c_out = refs[:2], refs[3:]
    rows = n_in[0].shape[1]
    wide, narrow = sides()
    sub = lax.broadcasted_iota(jnp.int32, n_in[0].shape[2:], 0)
    for a in range(2):
        for side in range(2):
            up = narrow[side]
            for p, (d, other) in enumerate(PAIRS):
                shift = jnp.where(up, STEPS - d, d)
                mine = jnp.where(up, sub, STEPS - 1 - sub) < STEPS - d
                for k in range(2):
                    near = n_in[side][k, edge_layer(wide[a], rows, d)]
                    far = n_in[side][k, edge_layer(wide[a], rows, other)]
                    c_out[a][k, p, side] = jnp.where(mine, near, pltpu.roll(far, shift, 0))


def corners(narrow_halos, after):
    depth = narrow_halos[0].shape[-1]
    shape = jax.ShapeDtypeStruct((2, len(PAIRS), 2, STEPS, depth), jnp.float32)
    return pl.pallas_call(
        corner_kernel,
        out_shape=[shape] * 2,
        in_specs=[VMEM] * 3,
        out_specs=[VMEM] * 2,
        compiler_params=pltpu.CompilerParams(vmem_limit_bytes=8 * MIB),
    )(*narrow_halos, after)


def swapped(array, across, along):
    wides, narrows = lax.axis_size("wide"), lax.axis_size("narrow")

    def partner(index, pairing):
        return index if pairing is None else index + (1 if index % 2 == pairing else -1)

    pairs = []
    for w in range(wides):
        for n in range(narrows):
            to_w, to_n = partner(w, across), partner(n, along)
            if 0 <= to_w < wides and 0 <= to_n < narrows:
                pairs.append((w * narrows + n, to_w * narrows + to_n))
    return lax.ppermute(array, AXES, pairs)


def tree(parts):
    while len(parts) > 1:
        parts = [
            parts[k] + parts[k + 1] if k + 1 < len(parts) else parts[k]
            for k in range(0, len(parts), 2)
        ]
    return parts[0]


def place_u(buffer, i, y, value):
    count = value.shape[0]
    for half in range(2):
        buffer[i, half, pl.ds(y + 8, count), :] = value[:, half * LANES : (half + 1) * LANES]


def diagonal_of(conduct, reaction):
    return ((reaction - CENTER) + 6.0 * (conduct * conduct)) * (1.0 / SCALE)


def outside(u_even, diag, coef, i, y, value, packed):
    count = value.shape[0]
    reaction = jnp.floor(packed * 128.0) * (1.0 / 128.0)
    conduct = (packed - reaction) * 256.0
    root = conduct * ROOT
    place_u(u_even, i, y, root * value)
    coef[i, pl.ds(y, count), :] = root * root
    diag[i, pl.ds(y, count), :] = diagonal_of(conduct, reaction)


def advance(step, runs, refs, carry, chosen=None, silent=()):
    b_ref, field, u_even, u_odd, diag, coef = refs
    h = STEPS
    tiles = diag.shape[1] // 8
    lane = lax.broadcasted_iota(jnp.int32, (8, LANES), 1)
    first, last = lane == 0, lane == LANES - 1
    source, target = (u_even, u_odd) if step % 2 else (u_odd, u_even)
    before = b_ref if step == 1 else field[step - 2]
    now = field[step - 1]
    cross, own = [], []
    for t in range(tiles) if chosen is None else chosen:
        edge = t in (0, tiles - 1)
        if edge and step == STEPS:
            continue
        rows = pl.ds(8 * t + 8, 8)
        for start, count, inside in runs:
            layers = [
                [source[start + d, half, rows, :] for half in range(2)]
                for d in range(-1, count + 1)
            ]
            for d in range(count):
                i = start + d
                left, right = layers[d + 1]
                left_up, left_down = pltpu.roll(left, 1, 1), pltpu.roll(left, LANES - 1, 1)
                right_up, right_down = pltpu.roll(right, 1, 1), pltpu.roll(right, LANES - 1, 1)
                along = (
                    jnp.where(first, 0.0, left_up) + jnp.where(last, right_down, left_down),
                    jnp.where(first, left_up, right_up) + jnp.where(last, 0.0, right_down),
                )
                for half in range(2):
                    beside = (
                        source[i, half, pl.ds(8 * t + 7, 8), :]
                        + source[i, half, pl.ds(8 * t + 9, 8), :]
                    )
                    across = layers[d][half] + layers[d + 2][half]
                    around = (beside + across) + along[half]
                    lanes = pl.ds(half * LANES, LANES)
                    at = (i, pl.ds(8 * t, 8), lanes)
                    if inside and not edge:
                        here = (i - h, pl.ds(8 * t - h, 8), lanes)
                        old = before[here]
                        root = coef[at]
                        value = diag[at] * old - root * around
                        now[here] = value
                        if step < STEPS:
                            target[i, half, rows, :] = root * value
                        if t in silent:
                            continue
                        cross.append(value * old)
                        if step < STEPS:
                            own.append(value * value)
                    else:
                        target[i, half, rows, :] = (
                            diag[at] * layers[d + 1][half] - coef[at] * around
                        )
    if not cross:
        return carry
    return carry[0] + tree(cross), (carry[1] + tree(own) if own else carry[1])


def inner_kernel(b_ref, c_ref, r_ref, *refs):
    field, (u_even, u_odd, diag, coef, m_ref) = refs[:STEPS], refs[STEPS:]
    rows, columns, depth = b_ref.shape
    h = STEPS
    everything = (b_ref, field, u_even, u_odd, diag, coef)
    tiles = range(1, columns // 8 + 1)

    def fill(i, total):
        at = i + h
        value = b_ref[i]
        conduct = c_ref[i].astype(jnp.float32)
        root = conduct * ROOT
        place_u(u_even, at, h, root * value)
        coef[at, pl.ds(h, columns), :] = root
        diag[at, pl.ds(h, columns), :] = diagonal_of(conduct, r_ref[i].astype(jnp.float32))
        square = value * value
        return total + tree(
            [
                square[t * 8 : t * 8 + 8, half * LANES : (half + 1) * LANES]
                for t in range(columns // 8)
                for half in range(2)
            ]
        )

    zero = jnp.zeros((8, LANES), jnp.float32)
    m_ref[0] = lax.fori_loop(0, rows, fill, zero)
    for step in range(1, STEPS + 1):
        quads, rest = divmod(max(rows - 2 * step, 0), 4)

        def work(start, count, carry, step=step):
            runs = [(start, count, True)]
            return advance(step, runs, everything, carry, tiles, (tiles[0], tiles[-1]))

        def body(m, carry, step=step, work=work):
            return work(4 * m + h + step, 4, carry)

        carry = lax.fori_loop(0, quads, body, (zero, zero))
        if rest:
            carry = work(h + rows - step - rest, rest, carry)
        m_ref[2 * step - 1] = carry[0]
        if step < STEPS:
            m_ref[2 * step] = carry[1]


def border_kernel(b_ref, m_in, *refs):
    n_in, refs = refs[:2], refs[2 + STEPS + 4 :]
    field, (u_even, u_odd, diag, coef, m_out) = refs[:STEPS], refs[STEPS:]
    rows, columns, depth = b_ref.shape
    h = STEPS
    tiles = columns // 8 + 2
    left = [pl.multiple_of(jnp.where(up, columns + h, 0), 8) for up in sides()[1]]
    everything = (b_ref, field, u_even, u_odd, diag, coef)

    def fill(i, _):
        at = i + h
        for side in range(2):
            outside(u_even, diag, coef, at, left[side], n_in[side][0, i], n_in[side][1, i])
        for y in (0, columns - 8):
            place_u(u_even, at, y + h, coef[at, pl.ds(y + h, 8), :] * b_ref[i, pl.ds(y, 8), :])
        return 0

    lax.fori_loop(0, rows, fill, 0)
    m_out[0] = m_in[0]
    for step in range(1, STEPS + 1):
        source = u_even if step % 2 else u_odd
        before = b_ref if step == 1 else field[step - 2]
        for i in range(step - 1, rows - step + 1):
            for y in (8, columns - 9):
                row = coef[i + h, y + h : y + h + 1, :] * before[i, y : y + 1, :]
                for half in range(2):
                    source[i + h, half, y + h + 8 : y + h + 9, :] = row[
                        :, half * LANES : (half + 1) * LANES
                    ]
        count = max(rows - 2 * step, 0)
        carry = (m_in[2 * step - 1], m_in[2 * step] if step < STEPS else m_in[0])
        for start, part in ((step, count // 2), (step + count // 2, count - count // 2)):
            if part:
                runs = [(start + h, part, True)]
                carry = advance(step, runs, everything, carry, (0, 1, tiles - 2, tiles - 1))
        m_out[2 * step - 1] = carry[0]
        if step < STEPS:
            m_out[2 * step] = carry[1]


def outer_kernel(pairing, b_ref, m_in, *refs):
    (w_in, c_in), refs = refs[:2], refs[2 + STEPS + 4 :]
    field, (u_even, u_odd, diag, coef, m_out) = refs[:STEPS], refs[STEPS:]
    rows, columns, depth = b_ref.shape
    h = STEPS
    wide, narrow = sides()
    up = wide[pairing]
    left = [pl.multiple_of(jnp.where(side, columns + h, 0), 8) for side in narrow]
    everything = (b_ref, field, u_even, u_odd, diag, coef)

    def halo_layer(d):
        return jnp.where(up, rows + h - 1 + d, h - d)

    def fill(d, _):
        outside(u_even, diag, coef, halo_layer(d), h, w_in[d - 1], w_in[h + d - 1])
        return 0

    lax.fori_loop(1, h, fill, 0)
    place_u(u_even, halo_layer(h), h, w_in[h - 1])
    for side in range(2):
        for p, (d, other) in enumerate(PAIRS):
            near = [c_in[k, p, side] for k in range(2)]
            outside(u_even, diag, coef, halo_layer(d), left[side], *near)
            if other != d:
                shift = jnp.where(narrow[side], d, h - d)
                far = [pltpu.roll(block, shift, 0) for block in near]
                outside(u_even, diag, coef, halo_layer(other), left[side], *far)

    zero = jnp.zeros((8, LANES), jnp.float32)
    moments = [m_in[0]]
    for step in range(1, STEPS + 1):
        carry = (m_in[2 * step - 1], m_in[2 * step] if step < STEPS else zero)
        runs = [(jnp.where(up, rows + h - step, h), step, True)]
        if step < STEPS:
            runs.append((jnp.where(up, rows + h, step), h - step, False))
        carry = advance(step, runs, everything, carry)
        moments += carry if step < STEPS else carry[:1]
    if pairing == 0:
        for k, moment in enumerate(moments):
            m_out[k] = moment
        return

    def folded(high, low, shift, axis):
        total, error = two_sum(high, pltpu.roll(high, shift, axis))
        return total, (low + pltpu.roll(low, shift, axis)) + error

    sublane = lax.broadcasted_iota(jnp.int32, (8, LANES), 0)
    lane = lax.broadcasted_iota(jnp.int32, (8, LANES), 1)
    packed = []
    for group in range(2):
        highs, lows = zero, zero
        for k in range(8):
            high, low = moments[group * 8 + k], zero
            for shift in (4, 2, 1):
                high, low = folded(high, low, shift, 0)
            highs = jnp.where(sublane == k, high, highs)
            lows = jnp.where(sublane == k, low, lows)
        for shift in (64, 32, 16, 8, 4, 2, 1):
            highs, lows = folded(highs, lows, shift, 1)
        packed += [highs, lows]
    message = jnp.where(
        lane < QUARTER,
        packed[0],
        jnp.where(lane < 2 * QUARTER, packed[1], jnp.where(lane < 3 * QUARTER, packed[2], packed[3])),
    )
    for k in range(m_out.shape[0]):
        m_out[k] = message


def summed(m_ref):
    total, error = m_ref[0], jnp.zeros((8, LANES), jnp.float32)
    for k in range(1, m_ref.shape[0]):
        total, lost = two_sum(total, m_ref[k])
        error = error + lost
    return total, error


def state_shapes(b):
    rows, columns, depth = b.shape
    wide, narrow = rows + 2 * STEPS, columns + 2 * STEPS
    shapes = [b.shape] * STEPS + [(wide, 2, narrow + 16, LANES)] * 2 + [(wide, narrow, depth)] * 2
    return [pltpu.VMEM(s, jnp.float32) for s in shapes]


def inner(b, c, r):
    shapes = state_shapes(b) + [jax.ShapeDtypeStruct((2 * STEPS, 8, LANES), jnp.float32)]
    *state, moments = pl.pallas_call(
        inner_kernel,
        cost_estimate=pl.CostEstimate(
            flops=120 * b.size, bytes_accessed=24 * b.size, transcendentals=0
        ),
        out_shape=shapes,
        in_specs=[VMEM] * 3,
        out_specs=[VMEM] * len(shapes),
        compiler_params=pltpu.CompilerParams(vmem_limit_bytes=26 * MIB),
    )(b, c, r)
    return state, moments


def onward(kernel, b, moments, received, state, moments_shape):
    shapes = state_shapes(b) + [jax.ShapeDtypeStruct(moments_shape, jnp.float32)]
    others = 2 + len(received)
    *state, moments = pl.pallas_call(
        kernel,
        out_shape=shapes,
        in_specs=[VMEM] * (others + len(state)),
        out_specs=[VMEM] * len(shapes),
        input_output_aliases={others + k: k for k in range(len(state))},
        compiler_params=pltpu.CompilerParams(vmem_limit_bytes=26 * MIB),
    )(b, moments, *received, *state)
    return state, moments


def coordinates(moment):
    shape = moment[0].shape
    count = shape[0]
    row = lax.broadcasted_iota(jnp.int32, shape, 0)

    def later(v):
        return jnp.where(row == count - 1, 0.0, pltpu.roll(v, count - 1, 0))

    def raised(v):
        return jnp.where(row == 0, 0.0, pltpu.roll(v, 1, 0))

    def spread(v):
        return jnp.broadcast_to(v, shape)

    residual = search = moment
    resid_coord = jnp.where(row == 0, 1.0, 0.0)
    search_coord = resid_coord
    sol_coord = jnp.zeros(shape, jnp.float32)
    for i in range(STEPS):
        mapped, lost = two_sum(later(search[0]), search[0])
        lost = lost + (later(search[1]) + search[1])
        old = residual[0][i : i + 1]
        inverse = 1.0 / old
        length = old / mapped[i : i + 1]
        lengths = spread(length)
        residual = pair_add(residual, loose_scale((mapped, lost), -lengths))
        grown = spread(-length * inverse * residual[0][i + 1 : i + 2])
        search = pair_add(residual, loose_scale(search, grown))
        sol_coord = sol_coord + (lengths * (1.0 / SCALE)) * search_coord
        resid_coord = resid_coord - lengths * (raised(search_coord) + search_coord)
        search_coord = resid_coord + grown * search_coord
    return sol_coord, resid_coord


def combine_kernel(m_ref, b_ref, *refs):
    field, outs, (x_ref, r_ref, done) = refs[:STEPS], refs[STEPS : STEPS + 2], refs[STEPS + 2 :]
    rows = b_ref.shape[0]
    total, error = summed(m_ref)

    def lane(v, k):
        return jnp.broadcast_to(v[:, k * QUARTER : k * QUARTER + 1], (8, LANES))

    high = jnp.concatenate([lane(total, 0), lane(total, 2)], axis=0)
    low = jnp.concatenate(
        [lane(error, 0) + lane(total, 1), lane(error, 2) + lane(total, 3)], axis=0
    )
    sol_coord, resid_coord = coordinates(fast_two_sum(high, low))
    sol = [jnp.broadcast_to(sol_coord[k : k + 1], (8, LANES)) for k in range(STEPS)]
    res = [jnp.broadcast_to(resid_coord[k : k + 1], (8, LANES)) for k in range(STEPS + 1)]

    def plane(i, _):
        for t in range(b_ref.shape[1] // 8):
            for half in range(b_ref.shape[2] // LANES):
                at = (i, pl.ds(8 * t, 8), pl.ds(half * LANES, LANES))
                fields = [b_ref[at]] + [f[at] for f in field]
                x, r = sol[0] * fields[0], res[0] * fields[0]
                for k in range(1, STEPS + 1):
                    if k < STEPS:
                        x = x + sol[k] * fields[k]
                    r = r + res[k] * fields[k]
                x_ref[at] = x
                r_ref[at] = r
        return 0

    copies = []
    for chunk in range(CHUNKS):
        part = pl.ds(chunk * rows // CHUNKS, rows // CHUNKS)
        lax.fori_loop(part.start, part.start + part.size, plane, 0)
        for k, source in enumerate((x_ref, r_ref)):
            copies.append(
                pltpu.make_async_copy(source.at[part], outs[k].at[part], done.at[k, chunk])
            )
            copies[-1].start()
    for copy in copies:
        copy.wait()


def combine(gathered, b, fields):
    return pl.pallas_call(
        combine_kernel,
        out_shape=[jax.ShapeDtypeStruct(b.shape, jnp.float32)] * 2,
        in_specs=[VMEM] * (STEPS + 2),
        out_specs=[HBM] * 2,
        scratch_shapes=[pltpu.VMEM(b.shape, jnp.float32)] * 2
        + [pltpu.SemaphoreType.DMA((2, CHUNKS))],
        compiler_params=pltpu.CompilerParams(vmem_limit_bytes=20 * MIB),
    )(gathered, b, *fields)


def on_device(right_side, conduct_half, reaction_half):
    *sent, b, c, r = messages(right_side, conduct_half, reaction_half)
    far, near = swapped(sent[1], 1, None), swapped(sent[0], 0, None)
    narrow_halos = [swapped(sent[2 + k], None, k) for k in range(2)]
    state, moments = inner(b, c, r)
    diagonal = corners(narrow_halos, moments)
    diagonal = [swapped(block, k, None) for k, block in enumerate(diagonal)]
    state, moments = onward(border_kernel, b, moments, narrow_halos, state, moments.shape)
    for pairing, received in enumerate(([near, diagonal[0]], [far, diagonal[1]])):
        shape = (1, 8, LANES) if pairing else moments.shape
        kernel = functools.partial(outer_kernel, pairing)
        state, moments = onward(kernel, b, moments, received, state, shape)
    gathered, fields = lax.all_gather(moments, AXES, axis=0, tiled=True), state[:STEPS]
    solution, residual = combine(gathered, b, fields)
    return (solution, residual)


def solution(mesh):
    placed = P(("group", "wide"), "narrow", None)
    return jax.shard_map(
        on_device,
        mesh=mesh,
        in_specs=(placed, placed, placed),
        out_specs=(placed, placed),
        check_vma=False,
    )
```

```python
import functools

import jax
import jax.numpy as jnp
from jax import lax
from jax.experimental import pallas as pl
from jax.experimental.pallas import tpu as pltpu
from jax.sharding import PartitionSpec as P

S = 4
OUTER = 2
STEPS = S * OUTER

SCALE = 13.0
CENTER = SCALE
ROOT = SCALE**-0.5

LANES = 128
QUARTER = LANES // 4
CHUNKS = 4
AXES = ("wide", "narrow")
VMEM = pl.BlockSpec(memory_space=pltpu.VMEM)
HBM = pl.BlockSpec(memory_space=pltpu.HBM)
MIB = 1024 * 1024


def two_sum(a, b):
    total = a + b
    part = total - a
    return total, (a - (total - part)) + (b - part)


def fast_two_sum(a, b):
    total = a + b
    return total, b - (total - a)


def split(a):
    big = a * 4097.0
    high = big - (big - a)
    return high, a - high


def two_product(a, b):
    product = a * b
    a_high, a_low = split(a)
    b_high, b_low = split(b)
    error = ((a_high * b_high - product) + a_high * b_low + a_low * b_high) + a_low * b_low
    return product, error


def pair_add(a, b):
    total, error = two_sum(a[0], b[0])
    return fast_two_sum(total, error + (a[1] + b[1]))


def loose_scale(a, factor):
    product, error = two_product(a[0], factor)
    return product, error + a[1] * factor


def sides():
    out = []
    for axis in AXES:
        even = lax.rem(lax.axis_index(axis), 2) == 0
        out.append((even, jnp.logical_not(even)))
    return out


def edge_layer(up, count, d):
    return jnp.where(up, count - d, d - 1)


def send_kernel(*refs):
    args, (w_out, n_out), refs = refs[:3], (refs[3:5], refs[5:7]), refs[7:]
    (b_ref, c_ref, r_ref), (pack, done) = refs[:3], refs[3:]
    rows, columns = b_ref.shape[:2]
    h = STEPS
    copies = [pltpu.make_async_copy(args[k], refs[k], done.at[k]) for k in (1, 2, 0)]
    for copy in copies:
        copy.start()
    wide, narrow = sides()
    left = [pl.multiple_of(jnp.where(up, columns - h, 0), 8) for up in narrow]

    def code(i, _):
        pack[i] = r_ref[i].astype(jnp.float32) + c_ref[i].astype(jnp.float32) * (1.0 / 256.0)
        return 0

    def edges(i, _):
        for k, source in enumerate((b_ref, pack)):
            for side in range(2):
                n_out[side][k, i] = source[i, pl.ds(left[side], h), :]
        return 0

    def layers(d, _):
        for a in range(2):
            at = edge_layer(wide[a], rows, d)
            w_out[a][d - 1] = b_ref[at]
            w_out[a][h + d - 1] = pack[at]
        return 0

    copies[0].wait()
    copies[1].wait()
    lax.fori_loop(0, rows, code, 0, unroll=8)
    copies[2].wait()
    lax.fori_loop(0, rows, edges, 0, unroll=16)
    for d in range(1, h):
        layers(d, 0)
    for a in range(2):
        at = edge_layer(wide[a], rows, h)
        w_out[a][h - 1] = c_ref[at].astype(jnp.float32) * ROOT * b_ref[at]


def messages(b, c, r):
    rows, columns, depth = b.shape
    h = STEPS
    shapes = [(2 * h - 1, columns, depth)] * 2 + [(2, rows, h, depth)] * 2
    return pl.pallas_call(
        send_kernel,
        out_shape=[jax.ShapeDtypeStruct(s, jnp.float32) for s in shapes]
        + [pltpu.VMEM(a.shape, a.dtype) for a in (b, c, r)],
        in_specs=[HBM] * 3,
        out_specs=[VMEM] * 7,
        scratch_shapes=[pltpu.VMEM(b.shape, jnp.float32), pltpu.SemaphoreType.DMA((3,))],
        compiler_params=pltpu.CompilerParams(vmem_limit_bytes=16 * MIB),
    )(*[pltpu.with_memory_space_constraint(a, pltpu.HBM) for a in (b, c, r)])


PAIRS = [(d, STEPS - d) for d in range(1, STEPS // 2 + 1)]


def corner_kernel(*refs):
    n_in, c_out = refs[:2], refs[3:]
    rows = n_in[0].shape[1]
    wide, narrow = sides()
    sub = lax.broadcasted_iota(jnp.int32, n_in[0].shape[2:], 0)
    for a in range(2):
        for side in range(2):
            up = narrow[side]
            for p, (d, other) in enumerate(PAIRS):
                shift = jnp.where(up, STEPS - d, d)
                mine = jnp.where(up, sub, STEPS - 1 - sub) < STEPS - d
                for k in range(2):
                    near = n_in[side][k, edge_layer(wide[a], rows, d)]
                    far = n_in[side][k, edge_layer(wide[a], rows, other)]
                    c_out[a][k, p, side] = jnp.where(mine, near, pltpu.roll(far, shift, 0))


def corners(narrow_halos, after):
    depth = narrow_halos[0].shape[-1]
    shape = jax.ShapeDtypeStruct((2, len(PAIRS), 2, STEPS, depth), jnp.float32)
    return pl.pallas_call(
        corner_kernel,
        out_shape=[shape] * 2,
        in_specs=[VMEM] * 3,
        out_specs=[VMEM] * 2,
        compiler_params=pltpu.CompilerParams(vmem_limit_bytes=8 * MIB),
    )(*narrow_halos, after)


def swapped(array, across, along):
    wides, narrows = lax.axis_size("wide"), lax.axis_size("narrow")

    def partner(index, pairing):
        return index if pairing is None else index + (1 if index % 2 == pairing else -1)

    pairs = []
    for w in range(wides):
        for n in range(narrows):
            to_w, to_n = partner(w, across), partner(n, along)
            if 0 <= to_w < wides and 0 <= to_n < narrows:
                pairs.append((w * narrows + n, to_w * narrows + to_n))
    return lax.ppermute(array, AXES, pairs)


def tree(parts):
    while len(parts) > 1:
        parts = [
            parts[k] + parts[k + 1] if k + 1 < len(parts) else parts[k]
            for k in range(0, len(parts), 2)
        ]
    return parts[0]


def place_u(buffer, i, y, value):
    count = value.shape[0]
    for half in range(2):
        buffer[i, half, pl.ds(y + 8, count), :] = value[:, half * LANES : (half + 1) * LANES]


def diagonal_of(conduct, reaction):
    return ((reaction - CENTER) + 6.0 * (conduct * conduct)) * (1.0 / SCALE)


def outside(u_even, diag, coef, i, y, value, packed):
    count = value.shape[0]
    reaction = jnp.floor(packed * 128.0) * (1.0 / 128.0)
    conduct = (packed - reaction) * 256.0
    root = conduct * ROOT
    place_u(u_even, i, y, root * value)
    coef[i, pl.ds(y, count), :] = root * root
    diag[i, pl.ds(y, count), :] = diagonal_of(conduct, reaction)


def advance(step, runs, refs, carry, chosen=None, silent=()):
    b_ref, field, u_even, u_odd, diag, coef = refs
    h = STEPS
    tiles = diag.shape[1] // 8
    lane = lax.broadcasted_iota(jnp.int32, (8, LANES), 1)
    first, last = lane == 0, lane == LANES - 1
    source, target = (u_even, u_odd) if step % 2 else (u_odd, u_even)
    before = b_ref if step == 1 else field[step - 2]
    now = field[step - 1]
    cross, own = [], []
    for t in range(tiles) if chosen is None else chosen:
        edge = t in (0, tiles - 1)
        if edge and step == STEPS:
            continue
        rows = pl.ds(8 * t + 8, 8)
        for start, count, inside in runs:
            layers = [
                [source[start + d, half, rows, :] for half in range(2)]
                for d in range(-1, count + 1)
            ]
            for d in range(count):
                i = start + d
                left, right = layers[d + 1]
                left_up, left_down = pltpu.roll(left, 1, 1), pltpu.roll(left, LANES - 1, 1)
                right_up, right_down = pltpu.roll(right, 1, 1), pltpu.roll(right, LANES - 1, 1)
                along = (
                    jnp.where(first, 0.0, left_up) + jnp.where(last, right_down, left_down),
                    jnp.where(first, left_up, right_up) + jnp.where(last, 0.0, right_down),
                )
                for half in range(2):
                    beside = (
                        source[i, half, pl.ds(8 * t + 7, 8), :]
                        + source[i, half, pl.ds(8 * t + 9, 8), :]
                    )
                    across = layers[d][half] + layers[d + 2][half]
                    around = (beside + across) + along[half]
                    lanes = pl.ds(half * LANES, LANES)
                    at = (i, pl.ds(8 * t, 8), lanes)
                    if inside and not edge:
                        here = (i - h, pl.ds(8 * t - h, 8), lanes)
                        old = before[here]
                        root = coef[at]
                        value = diag[at] * old - root * around
                        now[here] = value
                        if step < STEPS:
                            target[i, half, rows, :] = root * value
                        if t in silent:
                            continue
                        cross.append(value * old)
                        if step < STEPS:
                            own.append(value * value)
                    else:
                        target[i, half, rows, :] = (
                            diag[at] * layers[d + 1][half] - coef[at] * around
                        )
    if not cross:
        return carry
    return carry[0] + tree(cross), (carry[1] + tree(own) if own else carry[1])


def inner_kernel(b_ref, c_ref, r_ref, *refs):
    field, (u_even, u_odd, diag, coef, m_ref) = refs[:STEPS], refs[STEPS:]
    rows, columns, depth = b_ref.shape
    h = STEPS
    everything = (b_ref, field, u_even, u_odd, diag, coef)
    tiles = range(1, columns // 8 + 1)

    def fill(i, total):
        at = i + h
        value = b_ref[i]
        conduct = c_ref[i].astype(jnp.float32)
        root = conduct * ROOT
        place_u(u_even, at, h, root * value)
        coef[at, pl.ds(h, columns), :] = root
        diag[at, pl.ds(h, columns), :] = diagonal_of(conduct, r_ref[i].astype(jnp.float32))
        square = value * value
        return total + tree(
            [
                square[t * 8 : t * 8 + 8, half * LANES : (half + 1) * LANES]
                for t in range(columns // 8)
                for half in range(2)
            ]
        )

    zero = jnp.zeros((8, LANES), jnp.float32)
    m_ref[0] = lax.fori_loop(0, rows, fill, zero, unroll=4)
    for step in range(1, STEPS + 1):
        quads, rest = divmod(max(rows - 2 * step, 0), 4)

        def work(start, count, carry, step=step):
            runs = [(start, count, True)]
            return advance(step, runs, everything, carry, tiles, (tiles[0], tiles[-1]))

        def body(m, carry, step=step, work=work):
            return work(4 * m + h + step, 4, carry)

        carry = lax.fori_loop(0, quads, body, (zero, zero))
        if rest:
            carry = work(h + rows - step - rest, rest, carry)
        m_ref[2 * step - 1] = carry[0]
        if step < STEPS:
            m_ref[2 * step] = carry[1]


def border_kernel(b_ref, m_in, *refs):
    n_in, refs = refs[:2], refs[2 + STEPS + 4 :]
    field, (u_even, u_odd, diag, coef, m_out) = refs[:STEPS], refs[STEPS:]
    rows, columns, depth = b_ref.shape
    h = STEPS
    tiles = columns // 8 + 2
    left = [pl.multiple_of(jnp.where(up, columns + h, 0), 8) for up in sides()[1]]
    everything = (b_ref, field, u_even, u_odd, diag, coef)

    def fill(i, _):
        at = i + h
        for side in range(2):
            outside(u_even, diag, coef, at, left[side], n_in[side][0, i], n_in[side][1, i])
        for y in (0, columns - 8):
            place_u(u_even, at, y + h, coef[at, pl.ds(y + h, 8), :] * b_ref[i, pl.ds(y, 8), :])
        return 0

    for i in range(rows):
        fill(i, 0)
    m_out[0] = m_in[0]
    for step in range(1, STEPS + 1):
        source = u_even if step % 2 else u_odd
        before = b_ref if step == 1 else field[step - 2]
        for i in range(step - 1, rows - step + 1):
            for y in (8, columns - 9):
                row = coef[i + h, y + h : y + h + 1, :] * before[i, y : y + 1, :]
                for half in range(2):
                    source[i + h, half, y + h + 8 : y + h + 9, :] = row[
                        :, half * LANES : (half + 1) * LANES
                    ]
        count = max(rows - 2 * step, 0)
        carry = (m_in[2 * step - 1], m_in[2 * step] if step < STEPS else m_in[0])
        for start, part in ((step, count // 2), (step + count // 2, count - count // 2)):
            if part:
                runs = [(start + h, part, True)]
                carry = advance(step, runs, everything, carry, (0, 1, tiles - 2, tiles - 1))
        m_out[2 * step - 1] = carry[0]
        if step < STEPS:
            m_out[2 * step] = carry[1]


def outer_kernel(pairing, b_ref, m_in, *refs):
    (w_in, c_in), refs = refs[:2], refs[2 + STEPS + 4 :]
    field, (u_even, u_odd, diag, coef, m_out) = refs[:STEPS], refs[STEPS:]
    rows, columns, depth = b_ref.shape
    h = STEPS
    wide, narrow = sides()
    up = wide[pairing]
    left = [pl.multiple_of(jnp.where(side, columns + h, 0), 8) for side in narrow]
    everything = (b_ref, field, u_even, u_odd, diag, coef)

    def halo_layer(d):
        return jnp.where(up, rows + h - 1 + d, h - d)

    def fill(d, _):
        outside(u_even, diag, coef, halo_layer(d), h, w_in[d - 1], w_in[h + d - 1])
        return 0

    for d in range(1, h):
        fill(d, 0)
    place_u(u_even, halo_layer(h), h, w_in[h - 1])
    for side in range(2):
        for p, (d, other) in enumerate(PAIRS):
            near = [c_in[k, p, side] for k in range(2)]
            outside(u_even, diag, coef, halo_layer(d), left[side], *near)
            if other != d:
                shift = jnp.where(narrow[side], d, h - d)
                far = [pltpu.roll(block, shift, 0) for block in near]
                outside(u_even, diag, coef, halo_layer(other), left[side], *far)

    zero = jnp.zeros((8, LANES), jnp.float32)
    moments = [m_in[0]]
    for step in range(1, STEPS + 1):
        carry = (m_in[2 * step - 1], m_in[2 * step] if step < STEPS else zero)
        runs = [(jnp.where(up, rows + h - step, h), step, True)]
        if step < STEPS:
            runs.append((jnp.where(up, rows + h, step), h - step, False))
        carry = advance(step, runs, everything, carry)
        moments += carry if step < STEPS else carry[:1]
    if pairing == 0:
        for k, moment in enumerate(moments):
            m_out[k] = moment
        return

    def folded(high, low, shift, axis):
        total, error = two_sum(high, pltpu.roll(high, shift, axis))
        return total, (low + pltpu.roll(low, shift, axis)) + error

    sublane = lax.broadcasted_iota(jnp.int32, (8, LANES), 0)
    lane = lax.broadcasted_iota(jnp.int32, (8, LANES), 1)
    packed = []
    for group in range(2):
        highs, lows = zero, zero
        for k in range(8):
            high, low = moments[group * 8 + k], zero
            for shift in (4, 2, 1):
                high, low = folded(high, low, shift, 0)
            highs = jnp.where(sublane == k, high, highs)
            lows = jnp.where(sublane == k, low, lows)
        for shift in (64, 32, 16, 8, 4, 2, 1):
            highs, lows = folded(highs, lows, shift, 1)
        packed += [highs, lows]
    message = jnp.where(
        lane < QUARTER,
        packed[0],
        jnp.where(lane < 2 * QUARTER, packed[1], jnp.where(lane < 3 * QUARTER, packed[2], packed[3])),
    )
    for k in range(m_out.shape[0]):
        m_out[k] = message


def summed(m_ref):
    total, error = m_ref[0], jnp.zeros((8, LANES), jnp.float32)
    for k in range(1, m_ref.shape[0]):
        total, lost = two_sum(total, m_ref[k])
        error = error + lost
    return total, error


def state_shapes(b):
    rows, columns, depth = b.shape
    wide, narrow = rows + 2 * STEPS, columns + 2 * STEPS
    shapes = [b.shape] * STEPS + [(wide, 2, narrow + 16, LANES)] * 2 + [(wide, narrow, depth)] * 2
    return [pltpu.VMEM(s, jnp.float32) for s in shapes]


def inner(b, c, r):
    shapes = state_shapes(b) + [jax.ShapeDtypeStruct((2 * STEPS, 8, LANES), jnp.float32)]
    *state, moments = pl.pallas_call(
        inner_kernel,
        cost_estimate=pl.CostEstimate(
            flops=120 * b.size, bytes_accessed=24 * b.size, transcendentals=0
        ),
        out_shape=shapes,
        in_specs=[VMEM] * 3,
        out_specs=[VMEM] * len(shapes),
        compiler_params=pltpu.CompilerParams(vmem_limit_bytes=26 * MIB),
    )(b, c, r)
    return state, moments


def onward(kernel, b, moments, received, state, moments_shape):
    shapes = state_shapes(b) + [jax.ShapeDtypeStruct(moments_shape, jnp.float32)]
    others = 2 + len(received)
    *state, moments = pl.pallas_call(
        kernel,
        out_shape=shapes,
        in_specs=[VMEM] * (others + len(state)),
        out_specs=[VMEM] * len(shapes),
        input_output_aliases={others + k: k for k in range(len(state))},
        compiler_params=pltpu.CompilerParams(vmem_limit_bytes=26 * MIB),
    )(b, moments, *received, *state)
    return state, moments


def coordinates(moment):
    shape = moment[0].shape
    count = shape[0]
    row = lax.broadcasted_iota(jnp.int32, shape, 0)

    def later(v):
        return jnp.where(row == count - 1, 0.0, pltpu.roll(v, count - 1, 0))

    def raised(v):
        return jnp.where(row == 0, 0.0, pltpu.roll(v, 1, 0))

    def spread(v):
        return jnp.broadcast_to(v, shape)

    residual = search = moment
    resid_coord = jnp.where(row == 0, 1.0, 0.0)
    search_coord = resid_coord
    sol_coord = jnp.zeros(shape, jnp.float32)
    for i in range(STEPS):
        mapped, lost = two_sum(later(search[0]), search[0])
        lost = lost + (later(search[1]) + search[1])
        old = residual[0][i : i + 1]
        inverse = 1.0 / old
        length = old / mapped[i : i + 1]
        lengths = spread(length)
        residual = pair_add(residual, loose_scale((mapped, lost), -lengths))
        grown = spread(-length * inverse * residual[0][i + 1 : i + 2])
        search = pair_add(residual, loose_scale(search, grown))
        sol_coord = sol_coord + (lengths * (1.0 / SCALE)) * search_coord
        resid_coord = resid_coord - lengths * (raised(search_coord) + search_coord)
        search_coord = resid_coord + grown * search_coord
    return sol_coord, resid_coord


def combine_kernel(m_ref, b_ref, *refs):
    field, outs, (x_ref, r_ref, done) = refs[:STEPS], refs[STEPS : STEPS + 2], refs[STEPS + 2 :]
    rows = b_ref.shape[0]
    total, error = summed(m_ref)

    def lane(v, k):
        return jnp.broadcast_to(v[:, k * QUARTER : k * QUARTER + 1], (8, LANES))

    high = jnp.concatenate([lane(total, 0), lane(total, 2)], axis=0)
    low = jnp.concatenate(
        [lane(error, 0) + lane(total, 1), lane(error, 2) + lane(total, 3)], axis=0
    )
    sol_coord, resid_coord = coordinates(fast_two_sum(high, low))
    sol = [jnp.broadcast_to(sol_coord[k : k + 1], (8, LANES)) for k in range(STEPS)]
    res = [jnp.broadcast_to(resid_coord[k : k + 1], (8, LANES)) for k in range(STEPS + 1)]

    def plane(i, _):
        for t in range(b_ref.shape[1] // 8):
            for half in range(b_ref.shape[2] // LANES):
                at = (i, pl.ds(8 * t, 8), pl.ds(half * LANES, LANES))
                fields = [b_ref[at]] + [f[at] for f in field]
                x, r = sol[0] * fields[0], res[0] * fields[0]
                for k in range(1, STEPS + 1):
                    if k < STEPS:
                        x = x + sol[k] * fields[k]
                    r = r + res[k] * fields[k]
                x_ref[at] = x
                r_ref[at] = r
        return 0

    copies = []
    for chunk in range(CHUNKS):
        part = pl.ds(chunk * rows // CHUNKS, rows // CHUNKS)
        lax.fori_loop(part.start, part.start + part.size, plane, 0, unroll=2)
        for k, source in enumerate((x_ref, r_ref)):
            copies.append(
                pltpu.make_async_copy(source.at[part], outs[k].at[part], done.at[k, chunk])
            )
            copies[-1].start()
    for copy in copies:
        copy.wait()


def combine(gathered, b, fields):
    return pl.pallas_call(
        combine_kernel,
        out_shape=[jax.ShapeDtypeStruct(b.shape, jnp.float32)] * 2,
        in_specs=[VMEM] * (STEPS + 2),
        out_specs=[HBM] * 2,
        scratch_shapes=[pltpu.VMEM(b.shape, jnp.float32)] * 2
        + [pltpu.SemaphoreType.DMA((2, CHUNKS))],
        compiler_params=pltpu.CompilerParams(vmem_limit_bytes=20 * MIB),
    )(gathered, b, *fields)


def on_device(right_side, conduct_half, reaction_half):
    peers = lax.axis_size("wide") * lax.axis_size("narrow")
    *sent, b, c, r = messages(right_side, conduct_half, reaction_half)
    far, near = swapped(sent[1], 1, None), swapped(sent[0], 0, None)
    narrow_halos = [swapped(sent[2 + k], None, k) for k in range(2)]
    state, moments = inner(b, c, r)
    diagonal = corners(narrow_halos, moments)
    diagonal = [swapped(block, k, None) for k, block in enumerate(diagonal)]
    state, moments = onward(border_kernel, b, moments, narrow_halos, state, moments.shape)
    for pairing, received in enumerate(([near, diagonal[0]], [far, diagonal[1]])):
        shape = (peers, 8, LANES) if pairing else moments.shape
        kernel = functools.partial(outer_kernel, pairing)
        state, moments = onward(kernel, b, moments, received, state, shape)
    gathered, fields = lax.all_to_all(moments, AXES, 0, 0, tiled=True), state[:STEPS]
    solution, residual = combine(gathered, b, fields)
    return (solution, residual)


def solution(mesh):
    placed = P(("group", "wide"), "narrow", None)
    return jax.shard_map(
        on_device,
        mesh=mesh,
        in_specs=(placed, placed, placed),
        out_specs=(placed, placed),
        check_vma=False,
    )
```

```python
import functools

import jax
import jax.numpy as jnp
from jax import lax
from jax.experimental import pallas as pl
from jax.experimental.pallas import tpu as pltpu
from jax.sharding import PartitionSpec as P

S = 4
OUTER = 2
STEPS = S * OUTER

SCALE = 13.0
CENTER = SCALE
ROOT = SCALE**-0.5

LANES = 128
QUARTER = LANES // 4
CHUNKS = 4
NEAR = 2
AXES = ("wide", "narrow")
VMEM = pl.BlockSpec(memory_space=pltpu.VMEM)
HBM = pl.BlockSpec(memory_space=pltpu.HBM)
MIB = 1024 * 1024


def two_sum(a, b):
    total = a + b
    part = total - a
    return total, (a - (total - part)) + (b - part)


def fast_two_sum(a, b):
    total = a + b
    return total, b - (total - a)


def split(a):
    big = a * 4097.0
    high = big - (big - a)
    return high, a - high


def two_product(a, b):
    product = a * b
    a_high, a_low = split(a)
    b_high, b_low = split(b)
    error = ((a_high * b_high - product) + a_high * b_low + a_low * b_high) + a_low * b_low
    return product, error


def pair_add(a, b):
    total, error = two_sum(a[0], b[0])
    return fast_two_sum(total, error + (a[1] + b[1]))


def loose_scale(a, factor):
    product, error = two_product(a[0], factor)
    return product, error + a[1] * factor


def sides():
    wide, narrow = (lax.rem(lax.axis_index(axis), 2) == 0 for axis in AXES)
    return (wide, jnp.logical_not(wide)), (jnp.logical_not(narrow), narrow)


def wide_plane(d, near):
    return 4 * (d - 1) if near else 3 * (d - 1) + NEAR


WIDE_PLANES = wide_plane(STEPS, False) + 1


def edge_layer(up, count, d):
    return jnp.where(up, count - d, d - 1)


def send_kernel(*refs):
    args, (w_out, n_out), refs = refs[:3], (refs[3:5], refs[5:7]), refs[7:]
    (b_ref, c_ref, r_ref), (pack, done) = refs[:3], refs[3:]
    rows, columns = b_ref.shape[:2]
    h = STEPS
    copies = [pltpu.make_async_copy(args[k], refs[k], done.at[k]) for k in (1, 2, 0)]
    for copy in copies:
        copy.start()
    wide, narrow = sides()
    left = [pl.multiple_of(jnp.where(up, columns - h, 0), 8) for up in narrow]

    def code(i, _):
        for y in (0, columns - 2 * h):
            at = (i, pl.ds(y, 2 * h))
            reaction, conduct = r_ref[at].astype(jnp.float32), c_ref[at].astype(jnp.float32)
            pack[at] = reaction + conduct * (1.0 / 256.0)
        return 0

    def edges(i, _):
        for k, source in enumerate((b_ref, pack)):
            for side in range(2):
                n_out[side][k, i] = source[i, pl.ds(left[side], h), :]
        return 0

    copies[0].wait()
    copies[1].wait()
    lax.fori_loop(0, rows, code, 0, unroll=8)
    copies[2].wait()
    lax.fori_loop(0, rows, edges, 0, unroll=16)
    for a in range(2):
        for d in range(1, h):
            at, k = edge_layer(wide[a], rows, d), wide_plane(d, d <= NEAR)
            high = b_ref[at].astype(jnp.bfloat16)
            w_out[a][k] = high
            if d <= NEAR:
                k += 1
                w_out[a][k] = (b_ref[at] - high.astype(jnp.float32)).astype(jnp.bfloat16)
            w_out[a][k + 1] = c_ref[at]
            w_out[a][k + 2] = r_ref[at]
        at = edge_layer(wide[a], rows, h)
        root = c_ref[at].astype(jnp.float32) * ROOT
        w_out[a][WIDE_PLANES - 1] = (root * b_ref[at]).astype(jnp.bfloat16)


def messages(b, c, r):
    rows, columns, depth = b.shape
    h = STEPS
    outs = [jax.ShapeDtypeStruct((WIDE_PLANES, columns, depth), jnp.bfloat16)] * 2
    outs += [jax.ShapeDtypeStruct((2, rows, h, depth), jnp.float32)] * 2
    return pl.pallas_call(
        send_kernel,
        out_shape=outs
        + [pltpu.VMEM(a.shape, a.dtype) for a in (b, c, r)],
        in_specs=[HBM] * 3,
        out_specs=[VMEM] * 7,
        scratch_shapes=[pltpu.VMEM(b.shape, jnp.float32), pltpu.SemaphoreType.DMA((3,))],
        compiler_params=pltpu.CompilerParams(vmem_limit_bytes=16 * MIB),
    )(*[pltpu.with_memory_space_constraint(a, pltpu.HBM) for a in (b, c, r)])


PAIRS = [(d, STEPS - d) for d in range(1, STEPS // 2 + 1)]


def corner_kernel(*refs):
    n_in, c_out = refs[:2], refs[3:]
    rows = n_in[0].shape[1]
    wide, narrow = sides()
    sub = lax.broadcasted_iota(jnp.int32, n_in[0].shape[2:], 0)
    for a in range(2):
        for side in range(2):
            up = narrow[side]
            for p, (d, other) in enumerate(PAIRS):
                shift = jnp.where(up, STEPS - d, d)
                mine = jnp.where(up, sub, STEPS - 1 - sub) < STEPS - d
                for k in range(2):
                    near = n_in[side][k, edge_layer(wide[a], rows, d)]
                    far = n_in[side][k, edge_layer(wide[a], rows, other)]
                    c_out[a][k, p, side] = jnp.where(mine, near, pltpu.roll(far, shift, 0))


def corners(narrow_halos, after):
    depth = narrow_halos[0].shape[-1]
    shape = jax.ShapeDtypeStruct((2, len(PAIRS), 2, STEPS, depth), jnp.float32)
    return pl.pallas_call(
        corner_kernel,
        out_shape=[shape] * 2,
        in_specs=[VMEM] * 3,
        out_specs=[VMEM] * 2,
        compiler_params=pltpu.CompilerParams(vmem_limit_bytes=8 * MIB),
    )(*narrow_halos, after)


def swapped(array, across, along):
    wides, narrows = lax.axis_size("wide"), lax.axis_size("narrow")

    def partner(index, pairing):
        return index if pairing is None else index + (1 if index % 2 == pairing else -1)

    pairs = []
    for w in range(wides):
        for n in range(narrows):
            to_w, to_n = partner(w, across), partner(n, along)
            if 0 <= to_w < wides and 0 <= to_n < narrows:
                pairs.append((w * narrows + n, to_w * narrows + to_n))
    return lax.ppermute(array, AXES, pairs)


def tree(parts):
    while len(parts) > 1:
        parts = [
            parts[k] + parts[k + 1] if k + 1 < len(parts) else parts[k]
            for k in range(0, len(parts), 2)
        ]
    return parts[0]


def place_u(buffer, i, y, value):
    count = value.shape[0]
    for half in range(2):
        buffer[i, half, pl.ds(y + 8, count), :] = value[:, half * LANES : (half + 1) * LANES]


def diagonal_of(conduct, reaction):
    return ((reaction - CENTER) + 6.0 * (conduct * conduct)) * (1.0 / SCALE)


def settle(u_even, diag, coef, i, y, value, conduct, reaction):
    count = value.shape[0]
    root = conduct * ROOT
    place_u(u_even, i, y, root * value)
    coef[i, pl.ds(y, count), :] = root * root
    diag[i, pl.ds(y, count), :] = diagonal_of(conduct, reaction)


def outside(u_even, diag, coef, i, y, value, packed):
    reaction = jnp.floor(packed * 128.0) * (1.0 / 128.0)
    conduct = (packed - reaction) * 256.0
    settle(u_even, diag, coef, i, y, value, conduct, reaction)


def advance(step, runs, refs, carry, chosen=None, silent=()):
    b_ref, field, u_even, u_odd, diag, coef = refs
    h = STEPS
    tiles = diag.shape[1] // 8
    lane = lax.broadcasted_iota(jnp.int32, (8, LANES), 1)
    first, last = lane == 0, lane == LANES - 1
    source, target = (u_even, u_odd) if step % 2 else (u_odd, u_even)
    before = b_ref if step == 1 else field[step - 2]
    now = field[step - 1]
    cross, own = [], []
    for t in range(tiles) if chosen is None else chosen:
        edge = t in (0, tiles - 1)
        if edge and step == STEPS:
            continue
        rows = pl.ds(8 * t + 8, 8)
        for start, count, inside in runs:
            layers = [
                [source[start + d, half, rows, :] for half in range(2)]
                for d in range(-1, count + 1)
            ]
            for d in range(count):
                i = start + d
                left, right = layers[d + 1]
                left_up, left_down = pltpu.roll(left, 1, 1), pltpu.roll(left, LANES - 1, 1)
                right_up, right_down = pltpu.roll(right, 1, 1), pltpu.roll(right, LANES - 1, 1)
                along = (
                    jnp.where(first, 0.0, left_up) + jnp.where(last, right_down, left_down),
                    jnp.where(first, left_up, right_up) + jnp.where(last, 0.0, right_down),
                )
                for half in range(2):
                    beside = (
                        source[i, half, pl.ds(8 * t + 7, 8), :]
                        + source[i, half, pl.ds(8 * t + 9, 8), :]
                    )
                    across = layers[d][half] + layers[d + 2][half]
                    around = (beside + across) + along[half]
                    lanes = pl.ds(half * LANES, LANES)
                    at = (i, pl.ds(8 * t, 8), lanes)
                    if inside and not edge:
                        here = (i - h, pl.ds(8 * t - h, 8), lanes)
                        old = before[here]
                        root = coef[at]
                        value = diag[at] * old - root * around
                        now[here] = value
                        if step < STEPS:
                            target[i, half, rows, :] = root * value
                        if t in silent:
                            continue
                        cross.append(value * old)
                        if step < STEPS:
                            own.append(value * value)
                    else:
                        target[i, half, rows, :] = (
                            diag[at] * layers[d + 1][half] - coef[at] * around
                        )
    if not cross:
        return carry
    return carry[0] + tree(cross), (carry[1] + tree(own) if own else carry[1])


def inner_kernel(b_ref, c_ref, r_ref, *refs):
    field, (u_even, u_odd, diag, coef, m_ref) = refs[:STEPS], refs[STEPS:]
    rows, columns, depth = b_ref.shape
    h = STEPS
    everything = (b_ref, field, u_even, u_odd, diag, coef)
    tiles = range(1, columns // 8 + 1)

    def fill(i, total):
        at = i + h
        value = b_ref[i]
        conduct = c_ref[i].astype(jnp.float32)
        root = conduct * ROOT
        place_u(u_even, at, h, root * value)
        coef[at, pl.ds(h, columns), :] = root
        diag[at, pl.ds(h, columns), :] = diagonal_of(conduct, r_ref[i].astype(jnp.float32))
        square = value * value
        return total + tree(
            [
                square[t * 8 : t * 8 + 8, half * LANES : (half + 1) * LANES]
                for t in range(columns // 8)
                for half in range(2)
            ]
        )

    zero = jnp.zeros((8, LANES), jnp.float32)
    m_ref[0] = lax.fori_loop(0, rows, fill, zero, unroll=4)
    for step in range(1, STEPS + 1):
        quads, rest = divmod(max(rows - 2 * step, 0), 4)

        def work(start, count, carry, step=step):
            runs = [(start, count, True)]
            return advance(step, runs, everything, carry, tiles, (tiles[0], tiles[-1]))

        def body(m, carry, step=step, work=work):
            return work(4 * m + h + step, 4, carry)

        carry = lax.fori_loop(0, quads, body, (zero, zero))
        if rest:
            carry = work(h + rows - step - rest, rest, carry)
        m_ref[2 * step - 1] = carry[0]
        if step < STEPS:
            m_ref[2 * step] = carry[1]


def border_kernel(b_ref, m_in, *refs):
    n_in, refs = refs[:2], refs[2 + STEPS + 4 :]
    field, (u_even, u_odd, diag, coef, m_out) = refs[:STEPS], refs[STEPS:]
    rows, columns, depth = b_ref.shape
    h = STEPS
    tiles = columns // 8 + 2
    left = [pl.multiple_of(jnp.where(up, columns + h, 0), 8) for up in sides()[1]]
    everything = (b_ref, field, u_even, u_odd, diag, coef)

    def fill(i, _):
        at = i + h
        for side in range(2):
            outside(u_even, diag, coef, at, left[side], n_in[side][0, i], n_in[side][1, i])
        for y in (0, columns - 8):
            place_u(u_even, at, y + h, coef[at, pl.ds(y + h, 8), :] * b_ref[i, pl.ds(y, 8), :])
        return 0

    for i in range(rows):
        fill(i, 0)
    m_out[0] = m_in[0]
    for step in range(1, STEPS + 1):
        source = u_even if step % 2 else u_odd
        before = b_ref if step == 1 else field[step - 2]
        for i in range(step - 1, rows - step + 1):
            for y in (8, columns - 9):
                row = coef[i + h, y + h : y + h + 1, :] * before[i, y : y + 1, :]
                for half in range(2):
                    source[i + h, half, y + h + 8 : y + h + 9, :] = row[
                        :, half * LANES : (half + 1) * LANES
                    ]
        count = max(rows - 2 * step, 0)
        carry = (m_in[2 * step - 1], m_in[2 * step] if step < STEPS else m_in[0])
        for start, part in ((step, count // 2), (step + count // 2, count - count // 2)):
            if part:
                runs = [(start + h, part, True)]
                carry = advance(step, runs, everything, carry, (0, 1, tiles - 2, tiles - 1))
        m_out[2 * step - 1] = carry[0]
        if step < STEPS:
            m_out[2 * step] = carry[1]


def outer_kernel(pairing, b_ref, m_in, *refs):
    (w_in, c_in), refs = refs[:2], refs[2 + STEPS + 4 :]
    field, (u_even, u_odd, diag, coef, m_out) = refs[:STEPS], refs[STEPS:]
    rows, columns, depth = b_ref.shape
    h = STEPS
    wide, narrow = sides()
    up = wide[pairing]
    left = [pl.multiple_of(jnp.where(side, columns + h, 0), 8) for side in narrow]
    everything = (b_ref, field, u_even, u_odd, diag, coef)

    def halo_layer(d):
        return jnp.where(up, rows + h - 1 + d, h - d)

    def plane(k):
        return w_in[k].astype(jnp.float32)

    def fill(near, d, _):
        k = wide_plane(d, near)
        value = plane(k)
        if near:
            k += 1
            value = value + plane(k)
        settle(u_even, diag, coef, halo_layer(d), h, value, plane(k + 1), plane(k + 2))
        return 0

    lax.fori_loop(1, NEAR + 1, functools.partial(fill, True), 0)
    lax.fori_loop(NEAR + 1, h, functools.partial(fill, False), 0)
    place_u(u_even, halo_layer(h), h, plane(WIDE_PLANES - 1))
    for side in range(2):
        for p, (d, other) in enumerate(PAIRS):
            near = [c_in[k, p, side] for k in range(2)]
            outside(u_even, diag, coef, halo_layer(d), left[side], *near)
            if other != d:
                shift = jnp.where(narrow[side], d, h - d)
                far = [pltpu.roll(block, shift, 0) for block in near]
                outside(u_even, diag, coef, halo_layer(other), left[side], *far)

    zero = jnp.zeros((8, LANES), jnp.float32)
    moments = [m_in[0]]
    for step in range(1, STEPS + 1):
        carry = (m_in[2 * step - 1], m_in[2 * step] if step < STEPS else zero)
        runs = [(jnp.where(up, rows + h - step, h), step, True)]
        if step < STEPS:
            runs.append((jnp.where(up, rows + h, step), h - step, False))
        carry = advance(step, runs, everything, carry)
        moments += carry if step < STEPS else carry[:1]
    if pairing == 0:
        for k, moment in enumerate(moments):
            m_out[k] = moment
        return

    def folded(high, low, shift, axis):
        total, error = two_sum(high, pltpu.roll(high, shift, axis))
        return total, (low + pltpu.roll(low, shift, axis)) + error

    sublane = lax.broadcasted_iota(jnp.int32, (8, LANES), 0)
    lane = lax.broadcasted_iota(jnp.int32, (8, LANES), 1)
    packed = []
    for group in range(2):
        highs, lows = zero, zero
        for k in range(8):
            high, low = moments[group * 8 + k], zero
            for shift in (4, 2, 1):
                high, low = folded(high, low, shift, 0)
            highs = jnp.where(sublane == k, high, highs)
            lows = jnp.where(sublane == k, low, lows)
        for shift in (64, 32, 16, 8, 4, 2, 1):
            highs, lows = folded(highs, lows, shift, 1)
        packed += [highs, lows]
    message = jnp.where(
        lane < QUARTER,
        packed[0],
        jnp.where(lane < 2 * QUARTER, packed[1], jnp.where(lane < 3 * QUARTER, packed[2], packed[3])),
    )
    for k in range(m_out.shape[0]):
        m_out[k] = message


def summed(m_ref):
    total, error = m_ref[0], jnp.zeros((8, LANES), jnp.float32)
    for k in range(1, m_ref.shape[0]):
        total, lost = two_sum(total, m_ref[k])
        error = error + lost
    return total, error


def state_shapes(b):
    rows, columns, depth = b.shape
    wide, narrow = rows + 2 * STEPS, columns + 2 * STEPS
    shapes = [b.shape] * STEPS + [(wide, 2, narrow + 16, LANES)] * 2 + [(wide, narrow, depth)] * 2
    return [pltpu.VMEM(s, jnp.float32) for s in shapes]


def inner(b, c, r):
    shapes = state_shapes(b) + [jax.ShapeDtypeStruct((2 * STEPS, 8, LANES), jnp.float32)]
    *state, moments = pl.pallas_call(
        inner_kernel,
        cost_estimate=pl.CostEstimate(
            flops=120 * b.size, bytes_accessed=24 * b.size, transcendentals=0
        ),
        out_shape=shapes,
        in_specs=[VMEM] * 3,
        out_specs=[VMEM] * len(shapes),
        compiler_params=pltpu.CompilerParams(vmem_limit_bytes=26 * MIB),
    )(b, c, r)
    return state, moments


def onward(kernel, b, moments, received, state, moments_shape):
    shapes = state_shapes(b) + [jax.ShapeDtypeStruct(moments_shape, jnp.float32)]
    others = 2 + len(received)
    *state, moments = pl.pallas_call(
        kernel,
        out_shape=shapes,
        in_specs=[VMEM] * (others + len(state)),
        out_specs=[VMEM] * len(shapes),
        input_output_aliases={others + k: k for k in range(len(state))},
        compiler_params=pltpu.CompilerParams(vmem_limit_bytes=26 * MIB),
    )(b, moments, *received, *state)
    return state, moments


def coordinates(moment):
    shape = moment[0].shape
    count = shape[0]
    row = lax.broadcasted_iota(jnp.int32, shape, 0)

    def later(v):
        return jnp.where(row == count - 1, 0.0, pltpu.roll(v, count - 1, 0))

    def raised(v):
        return jnp.where(row == 0, 0.0, pltpu.roll(v, 1, 0))

    def spread(v):
        return jnp.broadcast_to(v, shape)

    residual = search = moment
    resid_coord = jnp.where(row == 0, 1.0, 0.0)
    search_coord = resid_coord
    sol_coord = jnp.zeros(shape, jnp.float32)
    for i in range(STEPS):
        mapped, lost = two_sum(later(search[0]), search[0])
        lost = lost + (later(search[1]) + search[1])
        old = residual[0][i : i + 1]
        inverse = 1.0 / old
        length = old / mapped[i : i + 1]
        lengths = spread(length)
        residual = pair_add(residual, loose_scale((mapped, lost), -lengths))
        grown = spread(-length * inverse * residual[0][i + 1 : i + 2])
        search = pair_add(residual, loose_scale(search, grown))
        sol_coord = sol_coord + (lengths * (1.0 / SCALE)) * search_coord
        resid_coord = resid_coord - lengths * (raised(search_coord) + search_coord)
        search_coord = resid_coord + grown * search_coord
    return sol_coord, resid_coord


def combine_kernel(m_ref, b_ref, *refs):
    field, outs, (x_ref, r_ref, done) = refs[:STEPS], refs[STEPS : STEPS + 2], refs[STEPS + 2 :]
    rows = b_ref.shape[0]
    total, error = summed(m_ref)

    def lane(v, k):
        return jnp.broadcast_to(v[:, k * QUARTER : k * QUARTER + 1], (8, LANES))

    high = jnp.concatenate([lane(total, 0), lane(total, 2)], axis=0)
    low = jnp.concatenate(
        [lane(error, 0) + lane(total, 1), lane(error, 2) + lane(total, 3)], axis=0
    )
    sol_coord, resid_coord = coordinates(fast_two_sum(high, low))
    sol = [jnp.broadcast_to(sol_coord[k : k + 1], (8, LANES)) for k in range(STEPS)]
    res = [jnp.broadcast_to(resid_coord[k : k + 1], (8, LANES)) for k in range(STEPS + 1)]

    def plane(i, _):
        for t in range(b_ref.shape[1] // 8):
            for half in range(b_ref.shape[2] // LANES):
                at = (i, pl.ds(8 * t, 8), pl.ds(half * LANES, LANES))
                fields = [b_ref[at]] + [f[at] for f in field]
                x, r = sol[0] * fields[0], res[0] * fields[0]
                for k in range(1, STEPS + 1):
                    if k < STEPS:
                        x = x + sol[k] * fields[k]
                    r = r + res[k] * fields[k]
                x_ref[at] = x
                r_ref[at] = r
        return 0

    copies = []
    for chunk in range(CHUNKS):
        part = pl.ds(chunk * rows // CHUNKS, rows // CHUNKS)
        lax.fori_loop(part.start, part.start + part.size, plane, 0, unroll=2)
        for k, source in enumerate((x_ref, r_ref)):
            copies.append(
                pltpu.make_async_copy(source.at[part], outs[k].at[part], done.at[k, chunk])
            )
            copies[-1].start()
    for copy in copies:
        copy.wait()


def combine(gathered, b, fields):
    return pl.pallas_call(
        combine_kernel,
        out_shape=[jax.ShapeDtypeStruct(b.shape, jnp.float32)] * 2,
        in_specs=[VMEM] * (STEPS + 2),
        out_specs=[HBM] * 2,
        scratch_shapes=[pltpu.VMEM(b.shape, jnp.float32)] * 2
        + [pltpu.SemaphoreType.DMA((2, CHUNKS))],
        compiler_params=pltpu.CompilerParams(vmem_limit_bytes=20 * MIB),
    )(gathered, b, *fields)


def on_device(right_side, conduct_half, reaction_half):
    peers = lax.axis_size("wide") * lax.axis_size("narrow")
    *sent, b, c, r = messages(right_side, conduct_half, reaction_half)
    far, near = swapped(sent[1], 1, None), swapped(sent[0], 0, None)
    narrow_halos = [swapped(sent[2 + k], None, 1 - k) for k in range(2)]
    state, moments = inner(b, c, r)
    diagonal = corners(narrow_halos, moments)
    diagonal = [swapped(block, k, None) for k, block in enumerate(diagonal)]
    state, moments = onward(border_kernel, b, moments, narrow_halos, state, moments.shape)
    for pairing, received in enumerate(([near, diagonal[0]], [far, diagonal[1]])):
        shape = (peers, 8, LANES) if pairing else moments.shape
        kernel = functools.partial(outer_kernel, pairing)
        state, moments = onward(kernel, b, moments, received, state, shape)
    gathered, fields = lax.all_to_all(moments, AXES, 0, 0, tiled=True), state[:STEPS]
    solution, residual = combine(gathered, b, fields)
    return (solution, residual)


def solution(mesh):
    placed = P(("group", "wide"), "narrow", None)
    return jax.shard_map(
        on_device,
        mesh=mesh,
        in_specs=(placed, placed, placed),
        out_specs=(placed, placed),
        check_vma=False,
    )
```

```python
import functools

import jax
import jax.numpy as jnp
from jax import lax
from jax.experimental import pallas as pl
from jax.experimental.pallas import tpu as pltpu
from jax.sharding import PartitionSpec as P

S = 4
OUTER = 2
STEPS = S * OUTER

SCALE = 13.0
CENTER = SCALE
ROOT = SCALE**-0.5

LANES = 128
QUARTER = LANES // 4
CHUNKS = 4
NEAR = 2
AXES = ("wide", "narrow")
VMEM = pl.BlockSpec(memory_space=pltpu.VMEM)
HBM = pl.BlockSpec(memory_space=pltpu.HBM)
MIB = 1024 * 1024


def two_sum(a, b):
    total = a + b
    part = total - a
    return total, (a - (total - part)) + (b - part)


def fast_two_sum(a, b):
    total = a + b
    return total, b - (total - a)


def split(a):
    big = a * 4097.0
    high = big - (big - a)
    return high, a - high


def two_product(a, b):
    product = a * b
    a_high, a_low = split(a)
    b_high, b_low = split(b)
    error = ((a_high * b_high - product) + a_high * b_low + a_low * b_high) + a_low * b_low
    return product, error


def pair_add(a, b):
    total, error = two_sum(a[0], b[0])
    return fast_two_sum(total, error + (a[1] + b[1]))


def loose_scale(a, factor):
    product, error = two_product(a[0], factor)
    return product, error + a[1] * factor


def sides():
    wide, narrow = (lax.rem(lax.axis_index(axis), 2) == 0 for axis in AXES)
    return (wide, jnp.logical_not(wide)), (jnp.logical_not(narrow), narrow)


def wide_plane(d, near):
    return 4 * (d - 1) if near else 3 * (d - 1) + NEAR


WIDE_PLANES = wide_plane(STEPS, False) + 1


def edge_layer(up, count, d):
    return jnp.where(up, count - d, d - 1)


def send_kernel(*refs):
    args, (w_out, n_out), refs = refs[:3], (refs[3:5], refs[5:7]), refs[7:]
    (b_ref, c_ref, r_ref), (pack, done) = refs[:3], refs[3:]
    rows, columns = b_ref.shape[:2]
    h = STEPS
    copies = [pltpu.make_async_copy(args[k], refs[k], done.at[k]) for k in (1, 2, 0)]
    for copy in copies:
        copy.start()
    wide, narrow = sides()
    left = [pl.multiple_of(jnp.where(up, columns - h, 0), 8) for up in narrow]

    def code(i, _):
        for y in (0, columns - 2 * h):
            at = (i, pl.ds(y, 2 * h))
            reaction, conduct = r_ref[at].astype(jnp.float32), c_ref[at].astype(jnp.float32)
            pack[at] = reaction + conduct * (1.0 / 256.0)
        return 0

    def edges(i, _):
        for k, source in enumerate((b_ref, pack)):
            for side in range(2):
                n_out[side][k, i] = source[i, pl.ds(left[side], h), :]
        return 0

    copies[0].wait()
    copies[1].wait()
    lax.fori_loop(0, rows, code, 0, unroll=8)
    copies[2].wait()
    lax.fori_loop(0, rows, edges, 0, unroll=16)
    for a in range(2):
        for d in range(1, h):
            at, k = edge_layer(wide[a], rows, d), wide_plane(d, d <= NEAR)
            high = b_ref[at].astype(jnp.bfloat16)
            w_out[a][k] = high
            if d <= NEAR:
                k += 1
                w_out[a][k] = (b_ref[at] - high.astype(jnp.float32)).astype(jnp.bfloat16)
            w_out[a][k + 1] = c_ref[at]
            w_out[a][k + 2] = r_ref[at]
        at = edge_layer(wide[a], rows, h)
        root = c_ref[at].astype(jnp.float32) * ROOT
        w_out[a][WIDE_PLANES - 1] = (root * b_ref[at]).astype(jnp.bfloat16)


def messages(b, c, r):
    rows, columns, depth = b.shape
    h = STEPS
    outs = [jax.ShapeDtypeStruct((WIDE_PLANES, columns, depth), jnp.bfloat16)] * 2
    outs += [jax.ShapeDtypeStruct((2, rows, h, depth), jnp.float32)] * 2
    return pl.pallas_call(
        send_kernel,
        out_shape=outs
        + [pltpu.VMEM(a.shape, a.dtype) for a in (b, c, r)],
        in_specs=[HBM] * 3,
        out_specs=[VMEM] * 7,
        scratch_shapes=[pltpu.VMEM(b.shape, jnp.float32), pltpu.SemaphoreType.DMA((3,))],
        compiler_params=pltpu.CompilerParams(vmem_limit_bytes=16 * MIB),
    )(*[pltpu.with_memory_space_constraint(a, pltpu.HBM) for a in (b, c, r)])


PAIRS = [(d, STEPS - d) for d in range(1, STEPS // 2 + 1)]


def corner_kernel(*refs):
    n_in, c_out = refs[:2], refs[3:]
    rows = n_in[0].shape[1]
    wide, narrow = sides()
    sub = lax.broadcasted_iota(jnp.int32, n_in[0].shape[2:], 0)
    for a in range(2):
        for side in range(2):
            up = narrow[side]
            for p, (d, other) in enumerate(PAIRS):
                shift = jnp.where(up, STEPS - d, d)
                mine = jnp.where(up, sub, STEPS - 1 - sub) < STEPS - d
                for k in range(2):
                    near = n_in[side][k, edge_layer(wide[a], rows, d)]
                    far = n_in[side][k, edge_layer(wide[a], rows, other)]
                    c_out[a][k, p, side] = jnp.where(mine, near, pltpu.roll(far, shift, 0))


def corners(narrow_halos, after):
    depth = narrow_halos[0].shape[-1]
    shape = jax.ShapeDtypeStruct((2, len(PAIRS), 2, STEPS, depth), jnp.float32)
    return pl.pallas_call(
        corner_kernel,
        out_shape=[shape] * 2,
        in_specs=[VMEM] * 3,
        out_specs=[VMEM] * 2,
        compiler_params=pltpu.CompilerParams(vmem_limit_bytes=8 * MIB),
    )(*narrow_halos, after)


def swapped(array, across, along):
    wides, narrows = lax.axis_size("wide"), lax.axis_size("narrow")

    def partner(index, pairing):
        return index if pairing is None else index + (1 if index % 2 == pairing else -1)

    pairs = []
    for w in range(wides):
        for n in range(narrows):
            to_w, to_n = partner(w, across), partner(n, along)
            if 0 <= to_w < wides and 0 <= to_n < narrows:
                pairs.append((w * narrows + n, to_w * narrows + to_n))
    return lax.ppermute(array, AXES, pairs)


def tree(parts):
    while len(parts) > 1:
        parts = [
            parts[k] + parts[k + 1] if k + 1 < len(parts) else parts[k]
            for k in range(0, len(parts), 2)
        ]
    return parts[0]


def place_u(buffer, i, y, value):
    count = value.shape[0]
    for half in range(2):
        buffer[i, half, pl.ds(y + 8, count), :] = value[:, half * LANES : (half + 1) * LANES]


def diagonal_of(conduct, reaction):
    return ((reaction - CENTER) + 6.0 * (conduct * conduct)) * (1.0 / SCALE)


def settle(u_even, diag, coef, i, y, value, conduct, reaction):
    count = value.shape[0]
    root = conduct * ROOT
    place_u(u_even, i, y, root * value)
    coef[i, pl.ds(y, count), :] = root * root
    diag[i, pl.ds(y, count), :] = diagonal_of(conduct, reaction)


def outside(u_even, diag, coef, i, y, value, packed):
    reaction = jnp.floor(packed * 128.0) * (1.0 / 128.0)
    conduct = (packed - reaction) * 256.0
    settle(u_even, diag, coef, i, y, value, conduct, reaction)


def advance(step, runs, refs, carry, chosen=None, silent=()):
    b_ref, field, u_even, u_odd, diag, coef = refs
    h = STEPS
    tiles = diag.shape[1] // 8
    lane = lax.broadcasted_iota(jnp.int32, (8, LANES), 1)
    first, last = lane == 0, lane == LANES - 1
    source, target = (u_even, u_odd) if step % 2 else (u_odd, u_even)
    before = b_ref if step == 1 else field[step - 2]
    now = field[step - 1]
    cross, own = [], []
    for t in range(tiles) if chosen is None else chosen:
        edge = t in (0, tiles - 1)
        if edge and step == STEPS:
            continue
        rows = pl.ds(8 * t + 8, 8)
        for start, count, inside in runs:
            layers = [
                [source[start + d, half, rows, :] for half in range(2)]
                for d in range(-1, count + 1)
            ]
            for d in range(count):
                i = start + d
                left, right = layers[d + 1]
                left_up, left_down = pltpu.roll(left, 1, 1), pltpu.roll(left, LANES - 1, 1)
                right_up, right_down = pltpu.roll(right, 1, 1), pltpu.roll(right, LANES - 1, 1)
                along = (
                    jnp.where(first, 0.0, left_up) + jnp.where(last, right_down, left_down),
                    jnp.where(first, left_up, right_up) + jnp.where(last, 0.0, right_down),
                )
                for half in range(2):
                    beside = (
                        source[i, half, pl.ds(8 * t + 7, 8), :]
                        + source[i, half, pl.ds(8 * t + 9, 8), :]
                    )
                    across = layers[d][half] + layers[d + 2][half]
                    around = (beside + across) + along[half]
                    lanes = pl.ds(half * LANES, LANES)
                    at = (i, pl.ds(8 * t, 8), lanes)
                    if inside and not edge:
                        here = (i - h, pl.ds(8 * t - h, 8), lanes)
                        old = before[here]
                        root = coef[at]
                        value = diag[at] * old - root * around
                        now[here] = value
                        if step < STEPS:
                            target[i, half, rows, :] = root * value
                        if t in silent:
                            continue
                        cross.append(value * old)
                        if step < STEPS:
                            own.append(value * value)
                    else:
                        target[i, half, rows, :] = (
                            diag[at] * layers[d + 1][half] - coef[at] * around
                        )
    if not cross:
        return carry
    return carry[0] + tree(cross), (carry[1] + tree(own) if own else carry[1])


def inner_kernel(b_ref, c_ref, r_ref, *refs):
    field, (u_even, u_odd, diag, coef, m_ref) = refs[:STEPS], refs[STEPS:]
    rows, columns, depth = b_ref.shape
    h = STEPS
    everything = (b_ref, field, u_even, u_odd, diag, coef)
    tiles = range(1, columns // 8 + 1)

    def fill(i, total):
        at = i + h
        value = b_ref[i]
        conduct = c_ref[i].astype(jnp.float32)
        root = conduct * ROOT
        place_u(u_even, at, h, root * value)
        coef[at, pl.ds(h, columns), :] = root
        diag[at, pl.ds(h, columns), :] = diagonal_of(conduct, r_ref[i].astype(jnp.float32))
        square = value * value
        return total + tree(
            [
                square[t * 8 : t * 8 + 8, half * LANES : (half + 1) * LANES]
                for t in range(columns // 8)
                for half in range(2)
            ]
        )

    zero = jnp.zeros((8, LANES), jnp.float32)
    m_ref[0] = lax.fori_loop(0, rows, fill, zero, unroll=4)
    for step in range(1, STEPS + 1):
        quads, rest = divmod(max(rows - 2 * step, 0), 4)

        def work(start, count, carry, step=step):
            runs = [(start, count, True)]
            return advance(step, runs, everything, carry, tiles, (tiles[0], tiles[-1]))

        def body(m, carry, step=step, work=work):
            return work(4 * m + h + step, 4, carry)

        carry = lax.fori_loop(0, quads, body, (zero, zero))
        if rest:
            carry = work(h + rows - step - rest, rest, carry)
        m_ref[2 * step - 1] = carry[0]
        if step < STEPS:
            m_ref[2 * step] = carry[1]


def end_runs(up, rows, step):
    h = STEPS
    runs = [(jnp.where(up, rows + h - step, h), step, True)]
    if step < h:
        runs.append((jnp.where(up, rows + h, step), h - step, False))
    return runs


def wide_fill(up, w_in, rows, u_even, diag, coef):
    h = STEPS

    def layer(d):
        return jnp.where(up, rows + h - 1 + d, h - d)

    def plane(k):
        return w_in[k].astype(jnp.float32)

    def fill(near, d, _):
        k = wide_plane(d, near)
        value = plane(k)
        if near:
            k += 1
            value = value + plane(k)
        settle(u_even, diag, coef, layer(d), h, value, plane(k + 1), plane(k + 2))
        return 0

    lax.fori_loop(1, NEAR + 1, functools.partial(fill, True), 0)
    lax.fori_loop(NEAR + 1, h, functools.partial(fill, False), 0)
    place_u(u_even, layer(h), h, plane(WIDE_PLANES - 1))


def corner_fill(up, c_in, rows, columns, u_even, diag, coef):
    h = STEPS

    def layer(d):
        return jnp.where(up, rows + h - 1 + d, h - d)

    for side, above in enumerate(sides()[1]):
        left = pl.multiple_of(jnp.where(above, columns + h, 0), 8)
        for p, (d, other) in enumerate(PAIRS):
            near = [c_in[k, p, side] for k in range(2)]
            outside(u_even, diag, coef, layer(d), left, *near)
            if other != d:
                shift = jnp.where(above, d, h - d)
                far = [pltpu.roll(block, shift, 0) for block in near]
                outside(u_even, diag, coef, layer(other), left, *far)


def halo_layers(up, rows, step):
    base, first = jnp.where(up, rows + STEPS, 0), jnp.where(up, 0, step)
    return [(first + k, base + first + k) for k in range(STEPS - step)]


def early_kernel(b_ref, m_in, w_in, *refs):
    refs = refs[STEPS + 4 :]
    field, (u_even, u_odd, diag, coef, m_out, rim, keep) = refs[:STEPS], refs[STEPS:]
    rows, columns, depth = b_ref.shape
    up = sides()[0][0]
    everything = (b_ref, field, u_even, u_odd, diag, coef)
    tiles = range(1, columns // 8 + 1)

    def save(step, buffer):
        for k, i in halo_layers(up, rows, step):
            for which, t in enumerate((tiles[1], tiles[-2])):
                for half in range(2):
                    rim[step, k, which, half] = buffer[i, half, pl.ds(8 * t + 8, 8), :]

    wide_fill(up, w_in, rows, u_even, diag, coef)
    for k, i in halo_layers(up, rows, 0):
        for which, t in enumerate((tiles[0], tiles[-1])):
            for half in range(2):
                keep[k, which, half] = u_even[i, half, pl.ds(8 * t + 8, 8), :]
    save(0, u_even)
    m_out[0] = m_in[0]
    for step in range(1, STEPS + 1):
        carry = (m_in[2 * step - 1], m_in[2 * step] if step < STEPS else m_in[0])
        runs = end_runs(up, rows, step)
        carry = advance(step, runs, everything, carry, tiles, (tiles[0], tiles[-1]))
        m_out[2 * step - 1] = carry[0]
        if step < STEPS:
            m_out[2 * step] = carry[1]
            save(step, u_odd if step % 2 else u_even)


def border_kernel(b_ref, m_in, *refs):
    n_in, (c_in, rim, keep), refs = refs[:2], refs[2:5], refs[5 + STEPS + 4 :]
    field, (u_even, u_odd, diag, coef, m_out) = refs[:STEPS], refs[STEPS:]
    rows, columns, depth = b_ref.shape
    h = STEPS
    tiles = columns // 8 + 2
    outermost = (0, 1, tiles - 2, tiles - 1)
    wide, narrow = sides()
    left = [pl.multiple_of(jnp.where(up, columns + h, 0), 8) for up in narrow]
    up = wide[0]
    everything = (b_ref, field, u_even, u_odd, diag, coef)

    def fill(i, _):
        at = i + h
        for side in range(2):
            outside(u_even, diag, coef, at, left[side], n_in[side][0, i], n_in[side][1, i])
        for y in (0, columns - 8):
            place_u(u_even, at, y + h, coef[at, pl.ds(y + h, 8), :] * b_ref[i, pl.ds(y, 8), :])
        return 0

    def renew(step, layers):
        source = u_even if step % 2 else u_odd
        before = b_ref if step == 1 else field[step - 2]
        for i in layers:
            for y in (8, columns - 9):
                row = coef[i + h, y + h : y + h + 1, :] * before[i, y : y + 1, :]
                for half in range(2):
                    source[i + h, half, y + h + 8 : y + h + 9, :] = row[
                        :, half * LANES : (half + 1) * LANES
                    ]

    for i in range(rows):
        fill(i, 0)
    moments = [(m_in[2 * k - 1], m_in[2 * k] if k < h else m_in[0]) for k in range(1, h + 1)]
    for step in range(1, h + 1):
        renew(step, range(step - 1, rows - step + 1))
        count = max(rows - 2 * step, 0)
        for start, part in ((step, count // 2), (step + count // 2, count - count // 2)):
            if part:
                runs = [(start + h, part, True)]
                moments[step - 1] = advance(step, runs, everything, moments[step - 1], outermost)

    corner_fill(up, c_in, rows, columns, u_even, diag, coef)
    for k, i in halo_layers(up, rows, 0):
        for which, t in enumerate((1, tiles - 2)):
            for half in range(2):
                u_even[i, half, pl.ds(8 * t + 8, 8), :] = keep[k, which, half]
    m_out[0] = m_in[0]
    for step in range(1, h + 1):
        source = u_even if step % 2 else u_odd
        first = jnp.where(up, rows - step, 0)
        renew(step, [first + k for k in range(step)])
        for k, i in halo_layers(up, rows, step):
            for half in range(2):
                source[i, half, 24:25, :] = rim[step - 1, k, 0, half][:1]
                source[i, half, columns + 7 : columns + 8, :] = rim[step - 1, k, 1, half][7:]
        runs = end_runs(up, rows, step)
        carry = advance(step, runs, everything, moments[step - 1], outermost)
        m_out[2 * step - 1] = carry[0]
        if step < h:
            m_out[2 * step] = carry[1]


def late_kernel(b_ref, m_in, *refs):
    (w_in, c_in), refs = refs[:2], refs[2 + STEPS + 4 :]
    field, (u_even, u_odd, diag, coef, m_out) = refs[:STEPS], refs[STEPS:]
    rows, columns, depth = b_ref.shape
    up = sides()[0][1]
    everything = (b_ref, field, u_even, u_odd, diag, coef)
    wide_fill(up, w_in, rows, u_even, diag, coef)
    corner_fill(up, c_in, rows, columns, u_even, diag, coef)
    zero = jnp.zeros((8, LANES), jnp.float32)
    moments = [m_in[0]]
    for step in range(1, STEPS + 1):
        carry = (m_in[2 * step - 1], m_in[2 * step] if step < STEPS else zero)
        carry = advance(step, end_runs(up, rows, step), everything, carry)
        moments += carry if step < STEPS else carry[:1]

    def folded(high, low, shift, axis):
        total, error = two_sum(high, pltpu.roll(high, shift, axis))
        return total, (low + pltpu.roll(low, shift, axis)) + error

    sublane = lax.broadcasted_iota(jnp.int32, (8, LANES), 0)
    lane = lax.broadcasted_iota(jnp.int32, (8, LANES), 1)
    packed = []
    for group in range(2):
        highs, lows = zero, zero
        for k in range(8):
            high, low = moments[group * 8 + k], zero
            for shift in (4, 2, 1):
                high, low = folded(high, low, shift, 0)
            highs = jnp.where(sublane == k, high, highs)
            lows = jnp.where(sublane == k, low, lows)
        for shift in (64, 32, 16, 8, 4, 2, 1):
            highs, lows = folded(highs, lows, shift, 1)
        packed += [highs, lows]
    message = jnp.where(
        lane < QUARTER,
        packed[0],
        jnp.where(lane < 2 * QUARTER, packed[1], jnp.where(lane < 3 * QUARTER, packed[2], packed[3])),
    )
    for k in range(m_out.shape[0]):
        m_out[k] = message


def summed(m_ref):
    total, error = m_ref[0], jnp.zeros((8, LANES), jnp.float32)
    for k in range(1, m_ref.shape[0]):
        total, lost = two_sum(total, m_ref[k])
        error = error + lost
    return total, error


def state_shapes(b):
    rows, columns, depth = b.shape
    wide, narrow = rows + 2 * STEPS, columns + 2 * STEPS
    shapes = [b.shape] * STEPS + [(wide, 2, narrow + 16, LANES)] * 2 + [(wide, narrow, depth)] * 2
    return [pltpu.VMEM(s, jnp.float32) for s in shapes]


def inner(b, c, r):
    shapes = state_shapes(b) + [jax.ShapeDtypeStruct((2 * STEPS, 8, LANES), jnp.float32)]
    *state, moments = pl.pallas_call(
        inner_kernel,
        cost_estimate=pl.CostEstimate(
            flops=120 * b.size, bytes_accessed=24 * b.size, transcendentals=0
        ),
        out_shape=shapes,
        in_specs=[VMEM] * 3,
        out_specs=[VMEM] * len(shapes),
        compiler_params=pltpu.CompilerParams(vmem_limit_bytes=26 * MIB),
    )(b, c, r)
    return state, moments


def onward(kernel, b, moments, received, state, moments_shape, extra=()):
    shapes = state_shapes(b) + [jax.ShapeDtypeStruct(moments_shape, jnp.float32)]
    shapes += [pltpu.VMEM(shape, jnp.float32) for shape in extra]
    others, count = 2 + len(received), len(state)
    outs = pl.pallas_call(
        kernel,
        out_shape=shapes,
        in_specs=[VMEM] * (others + count),
        out_specs=[VMEM] * len(shapes),
        input_output_aliases={others + k: k for k in range(count)},
        compiler_params=pltpu.CompilerParams(vmem_limit_bytes=24 * MIB),
        cost_estimate=pl.CostEstimate(
            flops=120 * b.size, bytes_accessed=24 * b.size, transcendentals=0
        ),
    )(b, moments, *received, *state)
    return outs[:count], *outs[count:]


def coordinates(moment):
    shape = moment[0].shape
    count = shape[0]
    row = lax.broadcasted_iota(jnp.int32, shape, 0)

    def later(v):
        return jnp.where(row == count - 1, 0.0, pltpu.roll(v, count - 1, 0))

    def raised(v):
        return jnp.where(row == 0, 0.0, pltpu.roll(v, 1, 0))

    def spread(v):
        return jnp.broadcast_to(v, shape)

    residual = search = moment
    resid_coord = jnp.where(row == 0, 1.0, 0.0)
    search_coord = resid_coord
    sol_coord = jnp.zeros(shape, jnp.float32)
    for i in range(STEPS):
        mapped, lost = two_sum(later(search[0]), search[0])
        lost = lost + (later(search[1]) + search[1])
        old = residual[0][i : i + 1]
        inverse = 1.0 / old
        length = old / mapped[i : i + 1]
        lengths = spread(length)
        residual = pair_add(residual, loose_scale((mapped, lost), -lengths))
        grown = spread(-length * inverse * residual[0][i + 1 : i + 2])
        search = pair_add(residual, loose_scale(search, grown))
        sol_coord = sol_coord + (lengths * (1.0 / SCALE)) * search_coord
        resid_coord = resid_coord - lengths * (raised(search_coord) + search_coord)
        search_coord = resid_coord + grown * search_coord
    return sol_coord, resid_coord


def combine_kernel(m_ref, b_ref, *refs):
    field, outs, (x_ref, r_ref, done) = refs[:STEPS], refs[STEPS : STEPS + 2], refs[STEPS + 2 :]
    rows = b_ref.shape[0]
    total, error = summed(m_ref)

    def lane(v, k):
        return jnp.broadcast_to(v[:, k * QUARTER : k * QUARTER + 1], (8, LANES))

    high = jnp.concatenate([lane(total, 0), lane(total, 2)], axis=0)
    low = jnp.concatenate(
        [lane(error, 0) + lane(total, 1), lane(error, 2) + lane(total, 3)], axis=0
    )
    sol_coord, resid_coord = coordinates(fast_two_sum(high, low))
    sol = [jnp.broadcast_to(sol_coord[k : k + 1], (8, LANES)) for k in range(STEPS)]
    res = [jnp.broadcast_to(resid_coord[k : k + 1], (8, LANES)) for k in range(STEPS + 1)]

    def plane(i, _):
        for t in range(b_ref.shape[1] // 8):
            for half in range(b_ref.shape[2] // LANES):
                at = (i, pl.ds(8 * t, 8), pl.ds(half * LANES, LANES))
                fields = [b_ref[at]] + [f[at] for f in field]
                x, r = sol[0] * fields[0], res[0] * fields[0]
                for k in range(1, STEPS + 1):
                    if k < STEPS:
                        x = x + sol[k] * fields[k]
                    r = r + res[k] * fields[k]
                x_ref[at] = x
                r_ref[at] = r
        return 0

    copies = []
    for chunk in range(CHUNKS):
        part = pl.ds(chunk * rows // CHUNKS, rows // CHUNKS)
        lax.fori_loop(part.start, part.start + part.size, plane, 0, unroll=2)
        for k, source in enumerate((x_ref, r_ref)):
            copies.append(
                pltpu.make_async_copy(source.at[part], outs[k].at[part], done.at[k, chunk])
            )
            copies[-1].start()
    for copy in copies:
        copy.wait()


def combine(gathered, b, fields):
    return pl.pallas_call(
        combine_kernel,
        out_shape=[jax.ShapeDtypeStruct(b.shape, jnp.float32)] * 2,
        in_specs=[VMEM] * (STEPS + 2),
        out_specs=[HBM] * 2,
        scratch_shapes=[pltpu.VMEM(b.shape, jnp.float32)] * 2
        + [pltpu.SemaphoreType.DMA((2, CHUNKS))],
        compiler_params=pltpu.CompilerParams(vmem_limit_bytes=20 * MIB),
    )(gathered, b, *fields)


def on_device(right_side, conduct_half, reaction_half):
    peers = lax.axis_size("wide") * lax.axis_size("narrow")
    *sent, b, c, r = messages(right_side, conduct_half, reaction_half)
    far, near = swapped(sent[1], 1, None), swapped(sent[0], 0, None)
    narrow_halos = [swapped(sent[2 + k], None, 1 - k) for k in range(2)]
    state, moments = inner(b, c, r)
    tiles = (2, 2, 8, LANES)
    extra = [(STEPS, STEPS, *tiles), (STEPS, *tiles)]
    state, moments, *saved = onward(early_kernel, b, moments, [near], state, moments.shape, extra)
    diagonal = corners(narrow_halos, moments)
    diagonal = [swapped(block, k, None) for k, block in enumerate(diagonal)]
    received = [*narrow_halos, diagonal[0], *saved]
    state, moments = onward(border_kernel, b, moments, received, state, moments.shape)
    received = [far, diagonal[1]]
    state, moments = onward(late_kernel, b, moments, received, state, (peers, 8, LANES))
    gathered, fields = lax.all_to_all(moments, AXES, 0, 0, tiled=True), state[:STEPS]
    solution, residual = combine(gathered, b, fields)
    return (solution, residual)


def solution(mesh):
    placed = P(("group", "wide"), "narrow", None)
    return jax.shard_map(
        on_device,
        mesh=mesh,
        in_specs=(placed, placed, placed),
        out_specs=(placed, placed),
        check_vma=False,
    )
```

```python
import functools

import jax
import jax.numpy as jnp
from jax import lax
from jax.experimental import pallas as pl
from jax.experimental.pallas import tpu as pltpu
from jax.sharding import PartitionSpec as P

S = 4
OUTER = 2
STEPS = S * OUTER

SCALE = 13.0
CENTER = SCALE
ROOT = SCALE**-0.5

LANES = 128
QUARTER = LANES // 4
CHUNKS = 4
NEAR = 2
AXES = ("wide", "narrow")
VMEM = pl.BlockSpec(memory_space=pltpu.VMEM)
HBM = pl.BlockSpec(memory_space=pltpu.HBM)
MIB = 1024 * 1024


def two_sum(a, b):
    total = a + b
    part = total - a
    return total, (a - (total - part)) + (b - part)


def fast_two_sum(a, b):
    total = a + b
    return total, b - (total - a)


def split(a):
    big = a * 4097.0
    high = big - (big - a)
    return high, a - high


def two_product(a, b):
    product = a * b
    a_high, a_low = split(a)
    b_high, b_low = split(b)
    error = ((a_high * b_high - product) + a_high * b_low + a_low * b_high) + a_low * b_low
    return product, error


def pair_add(a, b):
    total, error = two_sum(a[0], b[0])
    return fast_two_sum(total, error + (a[1] + b[1]))


def loose_scale(a, factor):
    product, error = two_product(a[0], factor)
    return product, error + a[1] * factor


def sides():
    wide, narrow = (lax.rem(lax.axis_index(axis), 2) == 0 for axis in AXES)
    return (wide, jnp.logical_not(wide)), (jnp.logical_not(narrow), narrow)


def wide_plane(d, near):
    return 4 * (d - 1) if near else 3 * (d - 1) + NEAR


WIDE_PLANES = wide_plane(STEPS, False) + 1


def edge_layer(up, count, d):
    return jnp.where(up, count - d, d - 1)


def send_kernel(*refs):
    args, (w_out, n_out), refs = refs[:3], (refs[3:5], refs[5:7]), refs[7:]
    (b_ref, c_ref, r_ref), (pack, done) = refs[:3], refs[3:]
    rows, columns = b_ref.shape[:2]
    h = STEPS
    copies = [pltpu.make_async_copy(args[k], refs[k], done.at[k]) for k in (1, 2, 0)]
    for copy in copies:
        copy.start()
    wide, narrow = sides()
    left = [pl.multiple_of(jnp.where(up, columns - h, 0), 8) for up in narrow]

    def code(i, _):
        for y in (0, columns - 2 * h):
            at = (i, pl.ds(y, 2 * h))
            reaction, conduct = r_ref[at].astype(jnp.float32), c_ref[at].astype(jnp.float32)
            pack[at] = reaction + conduct * (1.0 / 256.0)
        return 0

    def edges(i, _):
        for k, source in enumerate((b_ref, pack)):
            for side in range(2):
                n_out[side][k, i] = source[i, pl.ds(left[side], h), :]
        return 0

    copies[0].wait()
    copies[1].wait()
    lax.fori_loop(0, rows, code, 0, unroll=8)
    copies[2].wait()
    lax.fori_loop(0, rows, edges, 0, unroll=16)
    for a in range(2):
        for d in range(1, h):
            at, k = edge_layer(wide[a], rows, d), wide_plane(d, d <= NEAR)
            high = b_ref[at].astype(jnp.bfloat16)
            w_out[a][k] = high
            if d <= NEAR:
                k += 1
                w_out[a][k] = (b_ref[at] - high.astype(jnp.float32)).astype(jnp.bfloat16)
            w_out[a][k + 1] = c_ref[at]
            w_out[a][k + 2] = r_ref[at]
        at = edge_layer(wide[a], rows, h)
        root = c_ref[at].astype(jnp.float32) * ROOT
        w_out[a][WIDE_PLANES - 1] = (root * b_ref[at]).astype(jnp.bfloat16)


def messages(b, c, r):
    rows, columns, depth = b.shape
    h = STEPS
    outs = [jax.ShapeDtypeStruct((WIDE_PLANES, columns, depth), jnp.bfloat16)] * 2
    outs += [jax.ShapeDtypeStruct((2, rows, h, depth), jnp.float32)] * 2
    return pl.pallas_call(
        send_kernel,
        out_shape=outs
        + [pltpu.VMEM(a.shape, a.dtype) for a in (b, c, r)],
        in_specs=[HBM] * 3,
        out_specs=[VMEM] * 7,
        scratch_shapes=[pltpu.VMEM(b.shape, jnp.float32), pltpu.SemaphoreType.DMA((3,))],
        compiler_params=pltpu.CompilerParams(vmem_limit_bytes=16 * MIB),
    )(*[pltpu.with_memory_space_constraint(a, pltpu.HBM) for a in (b, c, r)])


PAIRS = [(d, STEPS - d) for d in range(1, STEPS // 2 + 1)]


def unpacked(packed):
    reaction = jnp.floor(packed * 128.0) * (1.0 / 128.0)
    return (packed - reaction) * 256.0, reaction


def corner_kernel(*refs):
    n_in, c_out = refs[:2], refs[3:]
    rows = n_in[0].shape[1]
    wide, narrow = sides()
    sub = lax.broadcasted_iota(jnp.int32, n_in[0].shape[2:], 0)
    for a in range(2):
        for p, (d, other) in enumerate(PAIRS):
            blocks = []
            for side in range(2):
                up = narrow[side]
                shift = jnp.where(up, STEPS - d, d)
                mine = jnp.where(up, sub, STEPS - 1 - sub) < STEPS - d
                value, packed = (
                    jnp.where(
                        mine,
                        n_in[side][k, edge_layer(wide[a], rows, d)],
                        pltpu.roll(n_in[side][k, edge_layer(wide[a], rows, other)], shift, 0),
                    )
                    for k in range(2)
                )
                blocks.append((value, *unpacked(packed)))
            for k in range(3):
                both = jnp.concatenate([blocks[0][k], blocks[1][k]], axis=0)
                c_out[a][k, p] = both.astype(jnp.bfloat16)


def corners(narrow_halos, after):
    depth = narrow_halos[0].shape[-1]
    shape = jax.ShapeDtypeStruct((3, len(PAIRS), 2 * STEPS, depth), jnp.bfloat16)
    return pl.pallas_call(
        corner_kernel,
        out_shape=[shape] * 2,
        in_specs=[VMEM] * 3,
        out_specs=[VMEM] * 2,
        compiler_params=pltpu.CompilerParams(vmem_limit_bytes=8 * MIB),
    )(*narrow_halos, after)


def swapped(array, across, along):
    wides, narrows = lax.axis_size("wide"), lax.axis_size("narrow")

    def partner(index, pairing):
        return index if pairing is None else index + (1 if index % 2 == pairing else -1)

    pairs = []
    for w in range(wides):
        for n in range(narrows):
            to_w, to_n = partner(w, across), partner(n, along)
            if 0 <= to_w < wides and 0 <= to_n < narrows:
                pairs.append((w * narrows + n, to_w * narrows + to_n))
    return lax.ppermute(array, AXES, pairs)


def tree(parts):
    while len(parts) > 1:
        parts = [
            parts[k] + parts[k + 1] if k + 1 < len(parts) else parts[k]
            for k in range(0, len(parts), 2)
        ]
    return parts[0]


def place_u(buffer, i, y, value):
    count = value.shape[0]
    for half in range(2):
        buffer[i, half, pl.ds(y + 8, count), :] = value[:, half * LANES : (half + 1) * LANES]


def diagonal_of(conduct, reaction):
    return ((reaction - CENTER) + 6.0 * (conduct * conduct)) * (1.0 / SCALE)


def settle(u_even, diag, coef, i, y, value, conduct, reaction):
    count = value.shape[0]
    root = conduct * ROOT
    place_u(u_even, i, y, root * value)
    coef[i, pl.ds(y, count), :] = root * root
    diag[i, pl.ds(y, count), :] = diagonal_of(conduct, reaction)


def outside(u_even, diag, coef, i, y, value, packed):
    settle(u_even, diag, coef, i, y, value, *unpacked(packed))


def advance(step, runs, refs, carry, chosen=None, silent=()):
    b_ref, field, u_even, u_odd, diag, coef = refs
    h = STEPS
    tiles = diag.shape[1] // 8
    lane = lax.broadcasted_iota(jnp.int32, (8, LANES), 1)
    first, last = lane == 0, lane == LANES - 1
    source, target = (u_even, u_odd) if step % 2 else (u_odd, u_even)
    before = b_ref if step == 1 else field[step - 2]
    now = field[step - 1]
    cross, own = [], []
    for t in range(tiles) if chosen is None else chosen:
        edge = t in (0, tiles - 1)
        if edge and step == STEPS:
            continue
        rows = pl.ds(8 * t + 8, 8)
        for start, count, inside in runs:
            layers = [
                [source[start + d, half, rows, :] for half in range(2)]
                for d in range(-1, count + 1)
            ]
            for d in range(count):
                i = start + d
                left, right = layers[d + 1]
                left_up, left_down = pltpu.roll(left, 1, 1), pltpu.roll(left, LANES - 1, 1)
                right_up, right_down = pltpu.roll(right, 1, 1), pltpu.roll(right, LANES - 1, 1)
                along = (
                    jnp.where(first, 0.0, left_up) + jnp.where(last, right_down, left_down),
                    jnp.where(first, left_up, right_up) + jnp.where(last, 0.0, right_down),
                )
                for half in range(2):
                    beside = (
                        source[i, half, pl.ds(8 * t + 7, 8), :]
                        + source[i, half, pl.ds(8 * t + 9, 8), :]
                    )
                    across = layers[d][half] + layers[d + 2][half]
                    around = (beside + across) + along[half]
                    lanes = pl.ds(half * LANES, LANES)
                    at = (i, pl.ds(8 * t, 8), lanes)
                    if inside and not edge:
                        here = (i - h, pl.ds(8 * t - h, 8), lanes)
                        old = before[here]
                        root = coef[at]
                        value = diag[at] * old - root * around
                        now[here] = value
                        if step < STEPS:
                            target[i, half, rows, :] = root * value
                        if t in silent:
                            continue
                        cross.append(value * old)
                        if step < STEPS:
                            own.append(value * value)
                    else:
                        target[i, half, rows, :] = (
                            diag[at] * layers[d + 1][half] - coef[at] * around
                        )
    if not cross:
        return carry
    return carry[0] + tree(cross), (carry[1] + tree(own) if own else carry[1])


def inner_kernel(b_ref, c_ref, r_ref, *refs):
    field, (u_even, u_odd, diag, coef, m_ref) = refs[:STEPS], refs[STEPS:]
    rows, columns, depth = b_ref.shape
    h = STEPS
    everything = (b_ref, field, u_even, u_odd, diag, coef)
    tiles = range(1, columns // 8 + 1)

    def fill(i, total):
        at = i + h
        value = b_ref[i]
        conduct = c_ref[i].astype(jnp.float32)
        root = conduct * ROOT
        place_u(u_even, at, h, root * value)
        coef[at, pl.ds(h, columns), :] = root
        diag[at, pl.ds(h, columns), :] = diagonal_of(conduct, r_ref[i].astype(jnp.float32))
        square = value * value
        return total + tree(
            [
                square[t * 8 : t * 8 + 8, half * LANES : (half + 1) * LANES]
                for t in range(columns // 8)
                for half in range(2)
            ]
        )

    zero = jnp.zeros((8, LANES), jnp.float32)
    m_ref[0] = lax.fori_loop(0, rows, fill, zero, unroll=4)
    for step in range(1, STEPS + 1):
        count, carry = max(rows - 2 * step, 0), (zero, zero)
        for start, part in ((step, count // 2), (step + count // 2, count - count // 2)):
            if part:
                runs = [(start + h, part, True)]
                carry = advance(step, runs, everything, carry, tiles, (tiles[0], tiles[-1]))
        m_ref[2 * step - 1] = carry[0]
        if step < STEPS:
            m_ref[2 * step] = carry[1]


def end_runs(up, rows, step):
    h = STEPS
    runs = [(jnp.where(up, rows + h - step, h), step, True)]
    if step < h:
        runs.append((jnp.where(up, rows + h, step), h - step, False))
    return runs


def wide_fill(up, w_in, rows, u_even, diag, coef):
    h = STEPS

    def layer(d):
        return jnp.where(up, rows + h - 1 + d, h - d)

    def plane(k):
        return w_in[k].astype(jnp.float32)

    def fill(near, d, _):
        k = wide_plane(d, near)
        value = plane(k)
        if near:
            k += 1
            value = value + plane(k)
        settle(u_even, diag, coef, layer(d), h, value, plane(k + 1), plane(k + 2))
        return 0

    lax.fori_loop(1, NEAR + 1, functools.partial(fill, True), 0)
    lax.fori_loop(NEAR + 1, h, functools.partial(fill, False), 0)
    place_u(u_even, layer(h), h, plane(WIDE_PLANES - 1))


def corner_fill(up, c_in, rows, columns, u_even, diag, coef):
    h = STEPS

    def layer(d):
        return jnp.where(up, rows + h - 1 + d, h - d)

    for side, above in enumerate(sides()[1]):
        left = pl.multiple_of(jnp.where(above, columns + h, 0), 8)
        for p, (d, other) in enumerate(PAIRS):
            near = [c_in[k, p].astype(jnp.float32)[h * side : h * side + h] for k in range(3)]
            settle(u_even, diag, coef, layer(d), left, *near)
            if other != d:
                shift = jnp.where(above, d, h - d)
                far = [pltpu.roll(block, shift, 0) for block in near]
                settle(u_even, diag, coef, layer(other), left, *far)


def halo_layers(up, rows, step):
    base, first = jnp.where(up, rows + STEPS, 0), jnp.where(up, 0, step)
    return [(first + k, base + first + k) for k in range(STEPS - step)]


def early_kernel(b_ref, m_in, w_in, *refs):
    refs = refs[STEPS + 4 :]
    field, (u_even, u_odd, diag, coef, m_out, rim, keep) = refs[:STEPS], refs[STEPS:]
    rows, columns, depth = b_ref.shape
    up = sides()[0][0]
    everything = (b_ref, field, u_even, u_odd, diag, coef)
    tiles = range(1, columns // 8 + 1)

    def save(step, buffer):
        for k, i in halo_layers(up, rows, step):
            for which, t in enumerate((tiles[1], tiles[-2])):
                for half in range(2):
                    rim[step, k, which, half] = buffer[i, half, pl.ds(8 * t + 8, 8), :]

    wide_fill(up, w_in, rows, u_even, diag, coef)
    for k, i in halo_layers(up, rows, 0):
        for which, t in enumerate((tiles[0], tiles[-1])):
            for half in range(2):
                keep[k, which, half] = u_even[i, half, pl.ds(8 * t + 8, 8), :]
    save(0, u_even)
    m_out[0] = m_in[0]
    for step in range(1, STEPS + 1):
        carry = (m_in[2 * step - 1], m_in[2 * step] if step < STEPS else m_in[0])
        runs = end_runs(up, rows, step)
        carry = advance(step, runs, everything, carry, tiles, (tiles[0], tiles[-1]))
        m_out[2 * step - 1] = carry[0]
        if step < STEPS:
            m_out[2 * step] = carry[1]
            save(step, u_odd if step % 2 else u_even)


def border_kernel(b_ref, m_in, *refs):
    n_in, (c_in, rim, keep), refs = refs[:2], refs[2:5], refs[5 + STEPS + 4 :]
    field, (u_even, u_odd, diag, coef, m_out) = refs[:STEPS], refs[STEPS:]
    rows, columns, depth = b_ref.shape
    h = STEPS
    tiles = columns // 8 + 2
    outermost = (0, 1, tiles - 2, tiles - 1)
    wide, narrow = sides()
    left = [pl.multiple_of(jnp.where(up, columns + h, 0), 8) for up in narrow]
    up = wide[0]
    everything = (b_ref, field, u_even, u_odd, diag, coef)

    def fill(i, _):
        at = i + h
        for side in range(2):
            outside(u_even, diag, coef, at, left[side], n_in[side][0, i], n_in[side][1, i])
        for y in (0, columns - 8):
            place_u(u_even, at, y + h, coef[at, pl.ds(y + h, 8), :] * b_ref[i, pl.ds(y, 8), :])
        return 0

    def renew(step, layers):
        source = u_even if step % 2 else u_odd
        before = b_ref if step == 1 else field[step - 2]
        for i in layers:
            for y in (8, columns - 9):
                row = coef[i + h, y + h : y + h + 1, :] * before[i, y : y + 1, :]
                for half in range(2):
                    source[i + h, half, y + h + 8 : y + h + 9, :] = row[
                        :, half * LANES : (half + 1) * LANES
                    ]

    for i in range(rows):
        fill(i, 0)
    moments = [(m_in[2 * k - 1], m_in[2 * k] if k < h else m_in[0]) for k in range(1, h + 1)]
    for step in range(1, h + 1):
        renew(step, range(step - 1, rows - step + 1))
        count = max(rows - 2 * step, 0)
        for start, part in ((step, count // 2), (step + count // 2, count - count // 2)):
            if part:
                runs = [(start + h, part, True)]
                moments[step - 1] = advance(step, runs, everything, moments[step - 1], outermost)

    corner_fill(up, c_in, rows, columns, u_even, diag, coef)
    for k, i in halo_layers(up, rows, 0):
        for which, t in enumerate((1, tiles - 2)):
            for half in range(2):
                u_even[i, half, pl.ds(8 * t + 8, 8), :] = keep[k, which, half]
    m_out[0] = m_in[0]
    for step in range(1, h + 1):
        source = u_even if step % 2 else u_odd
        first = jnp.where(up, rows - step, 0)
        renew(step, [first + k for k in range(step)])
        for k, i in halo_layers(up, rows, step):
            for half in range(2):
                source[i, half, 24:25, :] = rim[step - 1, k, 0, half][:1]
                source[i, half, columns + 7 : columns + 8, :] = rim[step - 1, k, 1, half][7:]
        runs = end_runs(up, rows, step)
        carry = advance(step, runs, everything, moments[step - 1], outermost)
        m_out[2 * step - 1] = carry[0]
        if step < h:
            m_out[2 * step] = carry[1]


def late_kernel(b_ref, m_in, *refs):
    (w_in, c_in), refs = refs[:2], refs[2 + STEPS + 4 :]
    field, (u_even, u_odd, diag, coef, m_out) = refs[:STEPS], refs[STEPS:]
    rows, columns, depth = b_ref.shape
    up = sides()[0][1]
    everything = (b_ref, field, u_even, u_odd, diag, coef)
    wide_fill(up, w_in, rows, u_even, diag, coef)
    corner_fill(up, c_in, rows, columns, u_even, diag, coef)
    zero = jnp.zeros((8, LANES), jnp.float32)
    moments = [m_in[0]]
    for step in range(1, STEPS + 1):
        carry = (m_in[2 * step - 1], m_in[2 * step] if step < STEPS else zero)
        carry = advance(step, end_runs(up, rows, step), everything, carry)
        moments += carry if step < STEPS else carry[:1]

    def folded(high, low, shift, axis):
        total, error = two_sum(high, pltpu.roll(high, shift, axis))
        return total, (low + pltpu.roll(low, shift, axis)) + error

    sublane = lax.broadcasted_iota(jnp.int32, (8, LANES), 0)
    lane = lax.broadcasted_iota(jnp.int32, (8, LANES), 1)
    packed = []
    for group in range(2):
        highs, lows = zero, zero
        for k in range(8):
            high, low = moments[group * 8 + k], zero
            for shift in (4, 2, 1):
                high, low = folded(high, low, shift, 0)
            highs = jnp.where(sublane == k, high, highs)
            lows = jnp.where(sublane == k, low, lows)
        for shift in (64, 32, 16, 8, 4, 2, 1):
            highs, lows = folded(highs, lows, shift, 1)
        packed += [highs, lows]
    message = jnp.where(
        lane < QUARTER,
        packed[0],
        jnp.where(lane < 2 * QUARTER, packed[1], jnp.where(lane < 3 * QUARTER, packed[2], packed[3])),
    )
    for k in range(m_out.shape[0]):
        m_out[k] = message


def summed(m_ref):
    total, error = m_ref[0], jnp.zeros((8, LANES), jnp.float32)
    for k in range(1, m_ref.shape[0]):
        total, lost = two_sum(total, m_ref[k])
        error = error + lost
    return total, error


def merge_kernel(mine, other, out_ref):
    total, error = two_sum(mine[0], other[0])
    lane = lax.broadcasted_iota(jnp.int32, (8, LANES), 1)
    low = lax.rem(lane // QUARTER, 2) == 1
    message = total + jnp.where(low, pltpu.roll(error, QUARTER, 1), 0.0)
    for k in range(out_ref.shape[0]):
        out_ref[k] = message


def gather(message):
    wides, narrows = lax.axis_size("wide"), lax.axis_size("narrow")
    peers = wides // 2 * narrows
    merged = pl.pallas_call(
        merge_kernel,
        out_shape=jax.ShapeDtypeStruct((peers, 8, LANES), jnp.float32),
        in_specs=[VMEM] * 2,
        out_specs=VMEM,
        compiler_params=pltpu.CompilerParams(vmem_limit_bytes=2 * MIB),
    )(message, swapped(message, 0, None))
    groups = [
        [w * narrows + n for w in range(core, wides, 2) for n in range(narrows)] for core in range(2)
    ]
    return lax.all_to_all(merged, AXES, 0, 0, axis_index_groups=groups, tiled=True)


def state_shapes(b):
    rows, columns, depth = b.shape
    wide, narrow = rows + 2 * STEPS, columns + 2 * STEPS
    shapes = [b.shape] * STEPS + [(wide, 2, narrow + 16, LANES)] * 2 + [(wide, narrow, depth)] * 2
    return [pltpu.VMEM(s, jnp.float32) for s in shapes]


def inner(b, c, r):
    shapes = state_shapes(b) + [jax.ShapeDtypeStruct((2 * STEPS, 8, LANES), jnp.float32)]
    *state, moments = pl.pallas_call(
        inner_kernel,
        cost_estimate=pl.CostEstimate(
            flops=120 * b.size, bytes_accessed=24 * b.size, transcendentals=0
        ),
        out_shape=shapes,
        in_specs=[VMEM] * 3,
        out_specs=[VMEM] * len(shapes),
        compiler_params=pltpu.CompilerParams(vmem_limit_bytes=26 * MIB),
    )(b, c, r)
    return state, moments


def onward(kernel, b, moments, received, state, moments_shape, extra=()):
    shapes = state_shapes(b) + [jax.ShapeDtypeStruct(moments_shape, jnp.float32)]
    shapes += [pltpu.VMEM(shape, jnp.float32) for shape in extra]
    others, count = 2 + len(received), len(state)
    outs = pl.pallas_call(
        kernel,
        out_shape=shapes,
        in_specs=[VMEM] * (others + count),
        out_specs=[VMEM] * len(shapes),
        input_output_aliases={others + k: k for k in range(count)},
        compiler_params=pltpu.CompilerParams(vmem_limit_bytes=24 * MIB),
        cost_estimate=pl.CostEstimate(
            flops=120 * b.size, bytes_accessed=24 * b.size, transcendentals=0
        ),
    )(b, moments, *received, *state)
    return outs[:count], *outs[count:]


def coordinates(moment):
    shape = moment[0].shape
    count = shape[0]
    row = lax.broadcasted_iota(jnp.int32, shape, 0)

    def later(v):
        return jnp.where(row == count - 1, 0.0, pltpu.roll(v, count - 1, 0))

    def raised(v):
        return jnp.where(row == 0, 0.0, pltpu.roll(v, 1, 0))

    def spread(v):
        return jnp.broadcast_to(v, shape)

    residual = search = moment
    resid_coord = jnp.where(row == 0, 1.0, 0.0)
    search_coord = resid_coord
    sol_coord = jnp.zeros(shape, jnp.float32)
    for i in range(STEPS):
        mapped, lost = two_sum(later(search[0]), search[0])
        lost = lost + (later(search[1]) + search[1])
        old = residual[0][i : i + 1]
        inverse = 1.0 / old
        length = old / mapped[i : i + 1]
        lengths = spread(length)
        residual = pair_add(residual, loose_scale((mapped, lost), -lengths))
        grown = spread(-length * inverse * residual[0][i + 1 : i + 2])
        search = pair_add(residual, loose_scale(search, grown))
        sol_coord = sol_coord + (lengths * (1.0 / SCALE)) * search_coord
        resid_coord = resid_coord - lengths * (raised(search_coord) + search_coord)
        search_coord = resid_coord + grown * search_coord
    return sol_coord, resid_coord


def combine_kernel(m_ref, b_ref, *refs):
    field, outs, (x_ref, r_ref, done) = refs[:STEPS], refs[STEPS : STEPS + 2], refs[STEPS + 2 :]
    rows = b_ref.shape[0]
    total, error = summed(m_ref)

    def lane(v, k):
        return jnp.broadcast_to(v[:, k * QUARTER : k * QUARTER + 1], (8, LANES))

    high = jnp.concatenate([lane(total, 0), lane(total, 2)], axis=0)
    low = jnp.concatenate(
        [lane(error, 0) + lane(total, 1), lane(error, 2) + lane(total, 3)], axis=0
    )
    sol_coord, resid_coord = coordinates(fast_two_sum(high, low))
    sol = [jnp.broadcast_to(sol_coord[k : k + 1], (8, LANES)) for k in range(STEPS)]
    res = [jnp.broadcast_to(resid_coord[k : k + 1], (8, LANES)) for k in range(STEPS + 1)]

    def plane(i, _):
        for t in range(b_ref.shape[1] // 8):
            for half in range(b_ref.shape[2] // LANES):
                at = (i, pl.ds(8 * t, 8), pl.ds(half * LANES, LANES))
                fields = [b_ref[at]] + [f[at] for f in field]
                x, r = sol[0] * fields[0], res[0] * fields[0]
                for k in range(1, STEPS + 1):
                    if k < STEPS:
                        x = x + sol[k] * fields[k]
                    r = r + res[k] * fields[k]
                x_ref[at] = x
                r_ref[at] = r
        return 0

    copies = []
    for chunk in range(CHUNKS):
        part = pl.ds(chunk * rows // CHUNKS, rows // CHUNKS)
        lax.fori_loop(part.start, part.start + part.size, plane, 0, unroll=2)
        for k, source in enumerate((x_ref, r_ref)):
            copies.append(
                pltpu.make_async_copy(source.at[part], outs[k].at[part], done.at[k, chunk])
            )
            copies[-1].start()
    for copy in copies:
        copy.wait()


def combine(gathered, b, fields):
    return pl.pallas_call(
        combine_kernel,
        out_shape=[jax.ShapeDtypeStruct(b.shape, jnp.float32)] * 2,
        in_specs=[VMEM] * (STEPS + 2),
        out_specs=[HBM] * 2,
        scratch_shapes=[pltpu.VMEM(b.shape, jnp.float32)] * 2
        + [pltpu.SemaphoreType.DMA((2, CHUNKS))],
        compiler_params=pltpu.CompilerParams(vmem_limit_bytes=20 * MIB),
    )(gathered, b, *fields)


def on_device(right_side, conduct_half, reaction_half):
    *sent, b, c, r = messages(right_side, conduct_half, reaction_half)
    far, near = swapped(sent[1], 1, None), swapped(sent[0], 0, None)
    narrow_halos = [swapped(sent[2 + k], None, 1 - k) for k in range(2)]
    state, moments = inner(b, c, r)
    tiles = (2, 2, 8, LANES)
    extra = [(STEPS, STEPS, *tiles), (STEPS, *tiles)]
    state, moments, *saved = onward(early_kernel, b, moments, [near], state, moments.shape, extra)
    diagonal = corners(narrow_halos, moments)
    diagonal = [swapped(block, k, None) for k, block in enumerate(diagonal)]
    received = [*narrow_halos, diagonal[0], *saved]
    state, moments = onward(border_kernel, b, moments, received, state, moments.shape)
    received = [far, diagonal[1]]
    state, moments = onward(late_kernel, b, moments, received, state, (1, 8, LANES))
    gathered, fields = gather(moments), state[:STEPS]
    solution, residual = combine(gathered, b, fields)
    return (solution, residual)


def solution(mesh):
    placed = P(("group", "wide"), "narrow", None)
    return jax.shard_map(
        on_device,
        mesh=mesh,
        in_specs=(placed, placed, placed),
        out_specs=(placed, placed),
        check_vma=False,
    )
```

```python
import functools

import jax
import jax.numpy as jnp
from jax import lax
from jax.experimental import pallas as pl
from jax.experimental.pallas import tpu as pltpu
from jax.sharding import PartitionSpec as P

S = 4
OUTER = 2
STEPS = S * OUTER

SCALE = 13.0
CENTER = SCALE
ROOT = SCALE**-0.5

LANES = 128
QUARTER = LANES // 4
CHUNKS = 4
NEAR = 2
AXES = ("wide", "narrow")
VMEM = pl.BlockSpec(memory_space=pltpu.VMEM)
HBM = pl.BlockSpec(memory_space=pltpu.HBM)
MIB = 1024 * 1024


def two_sum(a, b):
    total = a + b
    part = total - a
    return total, (a - (total - part)) + (b - part)


def fast_two_sum(a, b):
    total = a + b
    return total, b - (total - a)


def split(a):
    big = a * 4097.0
    high = big - (big - a)
    return high, a - high


def two_product(a, b):
    product = a * b
    a_high, a_low = split(a)
    b_high, b_low = split(b)
    error = ((a_high * b_high - product) + a_high * b_low + a_low * b_high) + a_low * b_low
    return product, error


def pair_add(a, b):
    total, error = two_sum(a[0], b[0])
    return fast_two_sum(total, error + (a[1] + b[1]))


def loose_scale(a, factor):
    product, error = two_product(a[0], factor)
    return product, error + a[1] * factor


def sides():
    wide, narrow = (lax.rem(lax.axis_index(axis), 2) == 0 for axis in AXES)
    return (wide, jnp.logical_not(wide)), (jnp.logical_not(narrow), narrow)


def wide_plane(d, near):
    return 4 * (d - 1) if near else 3 * (d - 1) + NEAR


WIDE_PLANES = wide_plane(STEPS, False) + 1


def edge_layer(up, count, d):
    return jnp.where(up, count - d, d - 1)


def send_kernel(*refs):
    args, (w_out, n_out), refs = refs[:3], (refs[3:5], refs[5:7]), refs[7:]
    (b_ref, c_ref, r_ref), (pack, done) = refs[:3], refs[3:]
    rows, columns = b_ref.shape[:2]
    h = STEPS
    copies = [pltpu.make_async_copy(args[k], refs[k], done.at[k]) for k in (1, 2, 0)]
    for copy in copies:
        copy.start()
    wide, narrow = sides()
    left = [pl.multiple_of(jnp.where(up, columns - h, 0), 8) for up in narrow]

    def code(i, _):
        for y in (0, columns - 2 * h):
            at = (i, pl.ds(y, 2 * h))
            reaction, conduct = r_ref[at].astype(jnp.float32), c_ref[at].astype(jnp.float32)
            pack[at] = reaction + conduct * (1.0 / 256.0)
        return 0

    def edges(i, _):
        for k, source in enumerate((b_ref, pack)):
            for side in range(2):
                n_out[side][k, i] = source[i, pl.ds(left[side], h), :]
        return 0

    copies[0].wait()
    copies[1].wait()
    lax.fori_loop(0, rows, code, 0, unroll=8)
    copies[2].wait()
    lax.fori_loop(0, rows, edges, 0, unroll=16)
    for a in range(2):
        for d in range(1, h):
            at, k = edge_layer(wide[a], rows, d), wide_plane(d, d <= NEAR)
            high = b_ref[at].astype(jnp.bfloat16)
            w_out[a][k] = high
            if d <= NEAR:
                k += 1
                w_out[a][k] = (b_ref[at] - high.astype(jnp.float32)).astype(jnp.bfloat16)
            w_out[a][k + 1] = c_ref[at]
            w_out[a][k + 2] = r_ref[at]
        at = edge_layer(wide[a], rows, h)
        root = c_ref[at].astype(jnp.float32) * ROOT
        w_out[a][WIDE_PLANES - 1] = (root * b_ref[at]).astype(jnp.bfloat16)


def messages(b, c, r):
    rows, columns, depth = b.shape
    h = STEPS
    outs = [jax.ShapeDtypeStruct((WIDE_PLANES, columns, depth), jnp.bfloat16)] * 2
    outs += [jax.ShapeDtypeStruct((2, rows, h, depth), jnp.float32)] * 2
    return pl.pallas_call(
        send_kernel,
        out_shape=outs
        + [pltpu.VMEM(a.shape, a.dtype) for a in (b, c, r)],
        in_specs=[HBM] * 3,
        out_specs=[VMEM] * 7,
        scratch_shapes=[pltpu.VMEM(b.shape, jnp.float32), pltpu.SemaphoreType.DMA((3,))],
        compiler_params=pltpu.CompilerParams(vmem_limit_bytes=16 * MIB),
    )(*[pltpu.with_memory_space_constraint(a, pltpu.HBM) for a in (b, c, r)])


PAIRS = [(d, STEPS - d) for d in range(1, STEPS // 2 + 1)]


def unpacked(packed):
    reaction = jnp.floor(packed * 128.0) * (1.0 / 128.0)
    return (packed - reaction) * 256.0, reaction


def corner_kernel(*refs):
    n_in, c_out = refs[:2], refs[3:]
    rows = n_in[0].shape[1]
    wide, narrow = sides()
    sub = lax.broadcasted_iota(jnp.int32, n_in[0].shape[2:], 0)
    for a in range(2):
        for p, (d, other) in enumerate(PAIRS):
            blocks = []
            for side in range(2):
                up = narrow[side]
                shift = jnp.where(up, STEPS - d, d)
                mine = jnp.where(up, sub, STEPS - 1 - sub) < STEPS - d
                value, packed = (
                    jnp.where(
                        mine,
                        n_in[side][k, edge_layer(wide[a], rows, d)],
                        pltpu.roll(n_in[side][k, edge_layer(wide[a], rows, other)], shift, 0),
                    )
                    for k in range(2)
                )
                blocks.append((value, *unpacked(packed)))
            for k in range(3):
                both = jnp.concatenate([blocks[0][k], blocks[1][k]], axis=0)
                c_out[a][k, p] = both.astype(jnp.bfloat16)


def corners(narrow_halos, after):
    depth = narrow_halos[0].shape[-1]
    shape = jax.ShapeDtypeStruct((3, len(PAIRS), 2 * STEPS, depth), jnp.bfloat16)
    return pl.pallas_call(
        corner_kernel,
        out_shape=[shape] * 2,
        in_specs=[VMEM] * 3,
        out_specs=[VMEM] * 2,
        compiler_params=pltpu.CompilerParams(vmem_limit_bytes=8 * MIB),
    )(*narrow_halos, after)


def swapped(array, across, along):
    wides, narrows = lax.axis_size("wide"), lax.axis_size("narrow")

    def partner(index, pairing):
        return index if pairing is None else index + (1 if index % 2 == pairing else -1)

    pairs = []
    for w in range(wides):
        for n in range(narrows):
            to_w, to_n = partner(w, across), partner(n, along)
            if 0 <= to_w < wides and 0 <= to_n < narrows:
                pairs.append((w * narrows + n, to_w * narrows + to_n))
    return lax.ppermute(array, AXES, pairs)


def tree(parts):
    while len(parts) > 1:
        parts = [
            parts[k] + parts[k + 1] if k + 1 < len(parts) else parts[k]
            for k in range(0, len(parts), 2)
        ]
    return parts[0]


def place_u(buffer, i, y, value):
    count = value.shape[0]
    for half in range(2):
        buffer[i, half, pl.ds(y + 8, count), :] = value[:, half * LANES : (half + 1) * LANES]


def diagonal_of(conduct, reaction):
    return ((reaction - CENTER) + 6.0 * (conduct * conduct)) * (1.0 / SCALE)


def settle(u_even, diag, coef, i, y, value, conduct, reaction):
    count = value.shape[0]
    root = conduct * ROOT
    place_u(u_even, i, y, root * value)
    coef[i, pl.ds(y, count), :] = root * root
    diag[i, pl.ds(y, count), :] = diagonal_of(conduct, reaction)


def outside(u_even, diag, coef, i, y, value, packed):
    settle(u_even, diag, coef, i, y, value, *unpacked(packed))


def advance(step, runs, refs, carry, chosen=None, silent=()):
    b_ref, field, u_even, u_odd, diag, coef = refs
    h = STEPS
    tiles = diag.shape[1] // 8
    lane = lax.broadcasted_iota(jnp.int32, (8, LANES), 1)
    first, last = lane == 0, lane == LANES - 1
    source, target = (u_even, u_odd) if step % 2 else (u_odd, u_even)
    before = b_ref if step == 1 else field[step - 2]
    now = field[step - 1]
    cross, own = [], []
    for t in range(tiles) if chosen is None else chosen:
        edge = t in (0, tiles - 1)
        if edge and step == STEPS:
            continue
        rows = pl.ds(8 * t + 8, 8)
        for start, count, inside in runs:
            layers = [
                [source[start + d, half, rows, :] for half in range(2)]
                for d in range(-1, count + 1)
            ]
            for d in range(count):
                i = start + d
                left, right = layers[d + 1]
                left_up, left_down = pltpu.roll(left, 1, 1), pltpu.roll(left, LANES - 1, 1)
                right_up, right_down = pltpu.roll(right, 1, 1), pltpu.roll(right, LANES - 1, 1)
                along = (
                    jnp.where(first, 0.0, left_up) + jnp.where(last, right_down, left_down),
                    jnp.where(first, left_up, right_up) + jnp.where(last, 0.0, right_down),
                )
                for half in range(2):
                    beside = (
                        source[i, half, pl.ds(8 * t + 7, 8), :]
                        + source[i, half, pl.ds(8 * t + 9, 8), :]
                    )
                    across = layers[d][half] + layers[d + 2][half]
                    around = (beside + across) + along[half]
                    lanes = pl.ds(half * LANES, LANES)
                    at = (i, pl.ds(8 * t, 8), lanes)
                    if inside and not edge:
                        here = (i - h, pl.ds(8 * t - h, 8), lanes)
                        old = before[here]
                        root = coef[at]
                        value = diag[at] * old - root * around
                        now[here] = value
                        if step < STEPS:
                            target[i, half, rows, :] = root * value
                        if t in silent:
                            continue
                        cross.append(value * old)
                        if step < STEPS:
                            own.append(value * value)
                    else:
                        target[i, half, rows, :] = (
                            diag[at] * layers[d + 1][half] - coef[at] * around
                        )
    if not cross:
        return carry
    return carry[0] + tree(cross), (carry[1] + tree(own) if own else carry[1])


def inner_kernel(b_ref, c_ref, r_ref, *refs):
    field, (u_even, u_odd, diag, coef, m_ref) = refs[:STEPS], refs[STEPS:]
    rows, columns, depth = b_ref.shape
    h = STEPS
    everything = (b_ref, field, u_even, u_odd, diag, coef)
    tiles = range(1, columns // 8 + 1)

    def fill(i, total):
        at = i + h
        value = b_ref[i]
        conduct = c_ref[i].astype(jnp.float32)
        root = conduct * ROOT
        place_u(u_even, at, h, root * value)
        coef[at, pl.ds(h, columns), :] = root
        diag[at, pl.ds(h, columns), :] = diagonal_of(conduct, r_ref[i].astype(jnp.float32))
        square = value * value
        return total + tree(
            [
                square[t * 8 : t * 8 + 8, half * LANES : (half + 1) * LANES]
                for t in range(columns // 8)
                for half in range(2)
            ]
        )

    zero = jnp.zeros((8, LANES), jnp.float32)
    m_ref[0] = lax.fori_loop(0, rows, fill, zero, unroll=4)
    for step in range(1, STEPS + 1):
        count, carry = max(rows - 2 * step, 0), (zero, zero)
        for start, part in ((step, count // 2), (step + count // 2, count - count // 2)):
            if part:
                runs = [(start + h, part, True)]
                carry = advance(step, runs, everything, carry, tiles, (tiles[0], tiles[-1]))
        m_ref[2 * step - 1] = carry[0]
        if step < STEPS:
            m_ref[2 * step] = carry[1]


def end_runs(up, rows, step):
    h = STEPS
    runs = [(jnp.where(up, rows + h - step, h), step, True)]
    if step < h:
        runs.append((jnp.where(up, rows + h, step), h - step, False))
    return runs


def wide_fill(up, w_in, rows, u_even, diag, coef):
    h = STEPS

    def layer(d):
        return jnp.where(up, rows + h - 1 + d, h - d)

    def plane(k):
        return w_in[k].astype(jnp.float32)

    def fill(near, d, _):
        k = wide_plane(d, near)
        value = plane(k)
        if near:
            k += 1
            value = value + plane(k)
        settle(u_even, diag, coef, layer(d), h, value, plane(k + 1), plane(k + 2))
        return 0

    lax.fori_loop(1, NEAR + 1, functools.partial(fill, True), 0)
    lax.fori_loop(NEAR + 1, h, functools.partial(fill, False), 0)
    place_u(u_even, layer(h), h, plane(WIDE_PLANES - 1))


def corner_fill(up, c_in, rows, columns, u_even, diag, coef):
    h = STEPS

    def layer(d):
        return jnp.where(up, rows + h - 1 + d, h - d)

    for side, above in enumerate(sides()[1]):
        left = pl.multiple_of(jnp.where(above, columns + h, 0), 8)
        for p, (d, other) in enumerate(PAIRS):
            near = [c_in[k, p].astype(jnp.float32)[h * side : h * side + h] for k in range(3)]
            settle(u_even, diag, coef, layer(d), left, *near)
            if other != d:
                shift = jnp.where(above, d, h - d)
                far = [pltpu.roll(block, shift, 0) for block in near]
                settle(u_even, diag, coef, layer(other), left, *far)


def halo_layers(up, rows, step):
    base, first = jnp.where(up, rows + STEPS, 0), jnp.where(up, 0, step)
    return [(first + k, base + first + k) for k in range(STEPS - step)]


def early_kernel(b_ref, m_in, w_in, *refs):
    refs = refs[STEPS + 4 :]
    field, (u_even, u_odd, diag, coef, m_out, rim, keep) = refs[:STEPS], refs[STEPS:]
    rows, columns, depth = b_ref.shape
    up = sides()[0][0]
    everything = (b_ref, field, u_even, u_odd, diag, coef)
    tiles = range(1, columns // 8 + 1)

    def save(step, buffer):
        for k, i in halo_layers(up, rows, step):
            for which, t in enumerate((tiles[1], tiles[-2])):
                for half in range(2):
                    rim[step, k, which, half] = buffer[i, half, pl.ds(8 * t + 8, 8), :]

    wide_fill(up, w_in, rows, u_even, diag, coef)
    for k, i in halo_layers(up, rows, 0):
        for which, t in enumerate((tiles[0], tiles[-1])):
            for half in range(2):
                keep[k, which, half] = u_even[i, half, pl.ds(8 * t + 8, 8), :]
    save(0, u_even)
    m_out[0] = m_in[0]
    for step in range(1, STEPS + 1):
        carry = (m_in[2 * step - 1], m_in[2 * step] if step < STEPS else m_in[0])
        runs = end_runs(up, rows, step)
        carry = advance(step, runs, everything, carry, tiles, (tiles[0], tiles[-1]))
        m_out[2 * step - 1] = carry[0]
        if step < STEPS:
            m_out[2 * step] = carry[1]
            save(step, u_odd if step % 2 else u_even)


def border_kernel(b_ref, m_in, *refs):
    n_in, (c_in, rim, keep), refs = refs[:2], refs[2:5], refs[5 + STEPS + 4 :]
    field, (u_even, u_odd, diag, coef, m_out) = refs[:STEPS], refs[STEPS:]
    rows, columns, depth = b_ref.shape
    h = STEPS
    tiles = columns // 8 + 2
    outermost = (0, 1, tiles - 2, tiles - 1)
    wide, narrow = sides()
    left = [pl.multiple_of(jnp.where(up, columns + h, 0), 8) for up in narrow]
    up = wide[0]
    everything = (b_ref, field, u_even, u_odd, diag, coef)

    def fill(i, _):
        at = i + h
        for side in range(2):
            outside(u_even, diag, coef, at, left[side], n_in[side][0, i], n_in[side][1, i])
        for y in (0, columns - 8):
            place_u(u_even, at, y + h, coef[at, pl.ds(y + h, 8), :] * b_ref[i, pl.ds(y, 8), :])
        return 0

    def renew(step, layers):
        source = u_even if step % 2 else u_odd
        before = b_ref if step == 1 else field[step - 2]
        for i in layers:
            for y in (8, columns - 9):
                row = coef[i + h, y + h : y + h + 1, :] * before[i, y : y + 1, :]
                for half in range(2):
                    source[i + h, half, y + h + 8 : y + h + 9, :] = row[
                        :, half * LANES : (half + 1) * LANES
                    ]

    for i in range(rows):
        fill(i, 0)
    moments = [(m_in[2 * k - 1], m_in[2 * k] if k < h else m_in[0]) for k in range(1, h + 1)]
    for step in range(1, h + 1):
        renew(step, range(step - 1, rows - step + 1))
        count = max(rows - 2 * step, 0)
        for start, part in ((step, count // 2), (step + count // 2, count - count // 2)):
            if part:
                runs = [(start + h, part, True)]
                moments[step - 1] = advance(step, runs, everything, moments[step - 1], outermost)

    corner_fill(up, c_in, rows, columns, u_even, diag, coef)
    for k, i in halo_layers(up, rows, 0):
        for which, t in enumerate((1, tiles - 2)):
            for half in range(2):
                u_even[i, half, pl.ds(8 * t + 8, 8), :] = keep[k, which, half]
    m_out[0] = m_in[0]
    for step in range(1, h + 1):
        source = u_even if step % 2 else u_odd
        first = jnp.where(up, rows - step, 0)
        renew(step, [first + k for k in range(step)])
        for k, i in halo_layers(up, rows, step):
            for half in range(2):
                source[i, half, 24:25, :] = rim[step - 1, k, 0, half][:1]
                source[i, half, columns + 7 : columns + 8, :] = rim[step - 1, k, 1, half][7:]
        runs = end_runs(up, rows, step)
        carry = advance(step, runs, everything, moments[step - 1], outermost)
        m_out[2 * step - 1] = carry[0]
        if step < h:
            m_out[2 * step] = carry[1]


def late_kernel(b_ref, m_in, *refs):
    (w_in, c_in), refs = refs[:2], refs[2 + STEPS + 4 :]
    field, (u_even, u_odd, diag, coef, m_out) = refs[:STEPS], refs[STEPS:]
    rows, columns, depth = b_ref.shape
    up = sides()[0][1]
    everything = (b_ref, field, u_even, u_odd, diag, coef)
    wide_fill(up, w_in, rows, u_even, diag, coef)
    corner_fill(up, c_in, rows, columns, u_even, diag, coef)
    zero = jnp.zeros((8, LANES), jnp.float32)
    moments = [m_in[0]]
    for step in range(1, STEPS + 1):
        carry = (m_in[2 * step - 1], m_in[2 * step] if step < STEPS else zero)
        carry = advance(step, end_runs(up, rows, step), everything, carry)
        moments += carry if step < STEPS else carry[:1]

    def folded(high, low, shift, axis):
        total, error = two_sum(high, pltpu.roll(high, shift, axis))
        return total, (low + pltpu.roll(low, shift, axis)) + error

    sublane = lax.broadcasted_iota(jnp.int32, (8, LANES), 0)
    lane = lax.broadcasted_iota(jnp.int32, (8, LANES), 1)
    packed = []
    for group in range(2):
        highs, lows = zero, zero
        for k in range(8):
            high, low = moments[group * 8 + k], zero
            for shift in (4, 2, 1):
                high, low = folded(high, low, shift, 0)
            highs = jnp.where(sublane == k, high, highs)
            lows = jnp.where(sublane == k, low, lows)
        for shift in (64, 32, 16, 8, 4, 2, 1):
            highs, lows = folded(highs, lows, shift, 1)
        packed += [highs, lows]
    message = jnp.where(
        lane < QUARTER,
        packed[0],
        jnp.where(lane < 2 * QUARTER, packed[1], jnp.where(lane < 3 * QUARTER, packed[2], packed[3])),
    )
    for k in range(m_out.shape[0]):
        m_out[k] = message


def summed(m_ref):
    total, error = m_ref[0], jnp.zeros((8, LANES), jnp.float32)
    for k in range(1, m_ref.shape[0]):
        total, lost = two_sum(total, m_ref[k])
        error = error + lost
    return total, error


def state_shapes(b):
    rows, columns, depth = b.shape
    wide, narrow = rows + 2 * STEPS, columns + 2 * STEPS
    shapes = [b.shape] * STEPS + [(wide, 2, narrow + 16, LANES)] * 2 + [(wide, narrow, depth)] * 2
    return [pltpu.VMEM(s, jnp.float32) for s in shapes]


def inner(b, c, r):
    shapes = state_shapes(b) + [jax.ShapeDtypeStruct((2 * STEPS, 8, LANES), jnp.float32)]
    *state, moments = pl.pallas_call(
        inner_kernel,
        cost_estimate=pl.CostEstimate(
            flops=120 * b.size, bytes_accessed=24 * b.size, transcendentals=0
        ),
        out_shape=shapes,
        in_specs=[VMEM] * 3,
        out_specs=[VMEM] * len(shapes),
        compiler_params=pltpu.CompilerParams(vmem_limit_bytes=26 * MIB),
    )(b, c, r)
    return state, moments


def onward(kernel, b, moments, received, state, moments_shape, extra=()):
    shapes = state_shapes(b) + [jax.ShapeDtypeStruct(moments_shape, jnp.float32)]
    shapes += [pltpu.VMEM(shape, jnp.float32) for shape in extra]
    others, count = 2 + len(received), len(state)
    outs = pl.pallas_call(
        kernel,
        out_shape=shapes,
        in_specs=[VMEM] * (others + count),
        out_specs=[VMEM] * len(shapes),
        input_output_aliases={others + k: k for k in range(count)},
        compiler_params=pltpu.CompilerParams(vmem_limit_bytes=24 * MIB),
        cost_estimate=pl.CostEstimate(
            flops=120 * b.size, bytes_accessed=24 * b.size, transcendentals=0
        ),
    )(b, moments, *received, *state)
    return outs[:count], *outs[count:]


def coordinates(moment):
    shape = moment[0].shape
    count = shape[0]
    row = lax.broadcasted_iota(jnp.int32, shape, 0)

    def later(v):
        return jnp.where(row == count - 1, 0.0, pltpu.roll(v, count - 1, 0))

    def raised(v):
        return jnp.where(row == 0, 0.0, pltpu.roll(v, 1, 0))

    def spread(v):
        return jnp.broadcast_to(v, shape)

    residual = search = moment
    resid_coord = jnp.where(row == 0, 1.0, 0.0)
    search_coord = resid_coord
    sol_coord = jnp.zeros(shape, jnp.float32)
    for i in range(STEPS):
        mapped, lost = two_sum(later(search[0]), search[0])
        lost = lost + (later(search[1]) + search[1])
        old = residual[0][i : i + 1]
        inverse = 1.0 / old
        length = old / mapped[i : i + 1]
        lengths = spread(length)
        residual = pair_add(residual, loose_scale((mapped, lost), -lengths))
        grown = spread(-length * inverse * residual[0][i + 1 : i + 2])
        search = pair_add(residual, loose_scale(search, grown))
        sol_coord = sol_coord + (lengths * (1.0 / SCALE)) * search_coord
        resid_coord = resid_coord - lengths * (raised(search_coord) + search_coord)
        search_coord = resid_coord + grown * search_coord
    return sol_coord, resid_coord


def combine_kernel(m_ref, b_ref, *refs):
    field, outs, (x_ref, r_ref, done) = refs[:STEPS], refs[STEPS : STEPS + 2], refs[STEPS + 2 :]
    rows = b_ref.shape[0]
    total, error = summed(m_ref)

    def lane(v, k):
        return jnp.broadcast_to(v[:, k * QUARTER : k * QUARTER + 1], (8, LANES))

    high = jnp.concatenate([lane(total, 0), lane(total, 2)], axis=0)
    low = jnp.concatenate(
        [lane(error, 0) + lane(total, 1), lane(error, 2) + lane(total, 3)], axis=0
    )
    sol_coord, resid_coord = coordinates(fast_two_sum(high, low))
    sol = [jnp.broadcast_to(sol_coord[k : k + 1], (8, LANES)) for k in range(STEPS)]
    res = [jnp.broadcast_to(resid_coord[k : k + 1], (8, LANES)) for k in range(STEPS + 1)]

    def plane(i, _):
        for t in range(b_ref.shape[1] // 8):
            for half in range(b_ref.shape[2] // LANES):
                at = (i, pl.ds(8 * t, 8), pl.ds(half * LANES, LANES))
                fields = [b_ref[at]] + [f[at] for f in field]
                x, r = sol[0] * fields[0], res[0] * fields[0]
                for k in range(1, STEPS + 1):
                    if k < STEPS:
                        x = x + sol[k] * fields[k]
                    r = r + res[k] * fields[k]
                x_ref[at] = x
                r_ref[at] = r
        return 0

    copies = []
    for chunk in range(CHUNKS):
        part = pl.ds(chunk * rows // CHUNKS, rows // CHUNKS)
        lax.fori_loop(part.start, part.start + part.size, plane, 0, unroll=2)
        for k, source in enumerate((x_ref, r_ref)):
            copies.append(
                pltpu.make_async_copy(source.at[part], outs[k].at[part], done.at[k, chunk])
            )
            copies[-1].start()
    for copy in copies:
        copy.wait()


def combine(gathered, b, fields):
    return pl.pallas_call(
        combine_kernel,
        out_shape=[jax.ShapeDtypeStruct(b.shape, jnp.float32)] * 2,
        in_specs=[VMEM] * (STEPS + 2),
        out_specs=[HBM] * 2,
        scratch_shapes=[pltpu.VMEM(b.shape, jnp.float32)] * 2
        + [pltpu.SemaphoreType.DMA((2, CHUNKS))],
        compiler_params=pltpu.CompilerParams(vmem_limit_bytes=20 * MIB),
    )(gathered, b, *fields)


def on_device(right_side, conduct_half, reaction_half):
    peers = lax.axis_size("wide") * lax.axis_size("narrow")
    *sent, b, c, r = messages(right_side, conduct_half, reaction_half)
    far, near = swapped(sent[1], 1, None), swapped(sent[0], 0, None)
    narrow_halos = [swapped(sent[2 + k], None, 1 - k) for k in range(2)]
    state, moments = inner(b, c, r)
    tiles = (2, 2, 8, LANES)
    extra = [(STEPS, STEPS, *tiles), (STEPS, *tiles)]
    state, moments, *saved = onward(early_kernel, b, moments, [near], state, moments.shape, extra)
    diagonal = corners(narrow_halos, moments)
    diagonal = [swapped(block, k, None) for k, block in enumerate(diagonal)]
    received = [*narrow_halos, diagonal[0], *saved]
    state, moments = onward(border_kernel, b, moments, received, state, moments.shape)
    received = [far, diagonal[1]]
    state, moments = onward(late_kernel, b, moments, received, state, (peers, 8, LANES))
    gathered, fields = lax.all_to_all(moments, AXES, 0, 0, tiled=True), state[:STEPS]
    solution, residual = combine(gathered, b, fields)
    return (solution, residual)


def solution(mesh):
    placed = P(("group", "wide"), "narrow", None)
    return jax.shard_map(
        on_device,
        mesh=mesh,
        in_specs=(placed, placed, placed),
        out_specs=(placed, placed),
        check_vma=False,
    )
```
